128 devices in a mesh: outer: 8 (over y_lo, x), inner: 16 (over z, y_hi, core).
Axes of the slice: x: 4, y: 4 (y_hi: 2, y_lo: 2; y = y_hi * 2 + y_lo), z: 4, core: 2. Of those that a mesh axis runs over, the one named last changes fastest.
Arguments:
- stream_in: bfloat16 [16, 1024, 2560], P('inner', 'outer'), may hold values from -6 to 6
- queries: bfloat16 [16, 1024, 2560], P('inner', 'outer'), may hold values from -6 to 6
- key_rows: bfloat16 [16, 1024, 2560], P('inner', 'outer'), may hold values from -6 to 6
- value_rows: bfloat16 [16, 1024, 2560], P('inner', 'outer'), may hold values from -6 to 6
- segment_ids: int32 [16, 1024], P('inner'), may hold values from 0 to 1, never falling along the last dimension, each value on 1 to 768 neighbouring positions
- norm_gain: float32 [2560], replicated, may hold values from 0.1 to 1.9
- router_w: bfloat16 [2560, 64], replicated, may hold values from -0.125 to 0.125
- expert_ids: int32 [16, 1024, 2], P('inner', 'outer'), may hold values from 0 to 63, all different within a row; in each aligned block of 128 rows (0 to 127, 128 to 255, ..., all dimensions but the last counted through in order) at most 6 rows name the same one
- gate_w: bfloat16 [128, 2560, 512], P(('outer', 'inner')), may hold values from -0.125 to 0.125
- up_w: bfloat16 [128, 2560, 512], P(('outer', 'inner')), may hold values from -0.125 to 0.125
- down_w: bfloat16 [128, 512, 2560], P(('outer', 'inner')), may hold values from -0.1875 to 0.1875
- out_grad: bfloat16 [16, 1024, 2560], P('inner', 'outer'), may hold values from -6 to 6
Outputs:
- stream_grad: bfloat16 [16, 1024, 2560], P('inner', 'outer')
- query_grad: bfloat16 [16, 1024, 2560], P('inner', 'outer')
- key_grad: bfloat16 [16, 1024, 2560], P('inner', 'outer')
- value_grad: bfloat16 [16, 1024, 2560], P('inner', 'outer')
- gain_grad: float32 [2560], replicated
- router_grad: float32 [2560, 64], replicated
- gate_grad: bfloat16 [128, 2560, 512], P(('outer', 'inner'))
- up_grad: bfloat16 [128, 2560, 512], P(('outer', 'inner'))
- down_grad: bfloat16 [128, 512, 2560], P(('outer', 'inner'))
The draws below stay inside these ranges and needn't reach their ends.
Inputs may be any that keep to these rules, and one draw needn't show every extreme that they name: `expert_ids`: the two ids of a frame differ. Within the 128 frames of one device no expert is chosen more than 6 times, a bound that some block reaches. `segment_ids`: Non-decreasing along each sequence; each sequence holds 2 utterances of 256 to 768 frames each, 1024 frames together.
All inputs are finite; a program needn't handle non-finite values.
Results may differ from the reference program's by a relative error of at most 0.029.
Values may be sent and summed in bfloat16 or wider, within the bound.
No kernel may reach another device: no remote copies, remote signals or barrier semaphores. Data moves between devices by JAX's collectives and lax.ppermute only.
A program may use at most 192 MiB of HBM per device.

```python
import math
import jax
import jax.numpy as jnp
import numpy as np
from jax import lax

D = 2560
HEADS = 20
HD = 128
FFE = 1024
TOK_DEV = 128
UTTS = 2
SEQS = 16
LEN = 1024
LONGEST = 768
EXPERTS = 64
CAP = 6
PIECES = 128
HALF = 512
N_OUTER = 8


def draw_queries(key, part):
    key = jax.random.fold_in(key, 11)
    return jnp.clip(jax.random.normal(key, (SEQS, LEN, D), jnp.float32), -6.0, 6.0).astype(jnp.bfloat16)


def draw_key_rows(key, part):
    key = jax.random.fold_in(key, 23)
    return jnp.clip(jax.random.normal(key, (SEQS, LEN, D), jnp.float32), -6.0, 6.0).astype(jnp.bfloat16)


def levels(stream_key, dims, cuts, smallest, top_value):
    def one(axis_at, blocks):
        steps = jax.random.uniform(jax.random.fold_in(jax.random.fold_in(stream_key, 6), axis_at), (blocks,), jnp.float32, smallest / len(cuts), top_value / len(cuts))
        return jnp.repeat(jnp.exp(steps), dims[axis_at] // blocks).reshape((-1,) + (1,) * (len(dims) - axis_at - 1))

    loudness = one(*cuts[0])
    for cut in cuts[1:]:
        loudness = loudness * one(*cut)
    return loudness


def profile(count, total, bound, slope):
    weights = [(1 << 20) // math.isqrt(grade ** slope) + 1 for grade in range(2, count + 1)]
    spare, counts = total - bound - (count - 1), [1] * (count - 1)
    while spare > 0:
        movable = [i for i in range(count - 1) if counts[i] < bound]
        whole, budget = sum([weights[i] for i in movable]), spare
        for i in movable:
            extra = min(bound - counts[i], max(1, budget * weights[i] // whole), spare)
            counts[i] = counts[i] + extra
            spare = spare - extra
    return np.array([bound] + counts)


def uneven(own_key, number_of, total, most, lean):
    if number_of == 2:
        one = jax.random.randint(own_key, (), max(1, total - most), min(most, total - 1) + 1)
        return jnp.stack([one, total - one])
    sizes = jnp.asarray(profile(number_of, total, most, lean), jnp.int32)
    pairs = (number_of - 1) // 2
    source_of, sink = sizes[1:1 + 2 * pairs:2], sizes[2:2 + 2 * pairs:2]
    slack = jnp.minimum(source_of - 1, most - sink)
    shifted = jax.random.randint(jax.random.fold_in(own_key, 1), (pairs,), 0, 1 << 20) % (slack + 1)
    sizes = sizes.at[1:1 + 2 * pairs:2].set(source_of - shifted).at[2:2 + 2 * pairs:2].set(sink + shifted)
    return sizes[jax.random.permutation(jax.random.fold_in(own_key, 2), number_of)]


def deal_out(stream_key, own, number, rows, count, top, bound, skew):
    order = jax.random.permutation(stream_key, count)
    heavy_load, common = load_shares(count, rows * top, bound, skew, True), load_shares(count, rows * top, bound, skew, False)
    places = jnp.arange(count)

    def named(lengths, offset_by):
        used = int((lengths > 0).sum())
        fixed = max(1, used // 4)
        passed = fixed + (places - fixed + offset_by * (used - fixed)) % max(1, count - fixed)
        return jnp.zeros((count,), jnp.int32).at[order[jnp.where(places < fixed, places, passed)]].set(jnp.asarray(lengths, jnp.int32))

    lengths = jnp.where(number % 4 == 0, named(heavy_load, number // 4), named(common, number - number // 4 - 1))
    mixed = jax.random.permutation(jax.random.fold_in(own, 3), count)
    donor, taker = mixed[0:count // 2 * 2:2], mixed[1:count // 2 * 2:2]
    slack = jnp.minimum(lengths[donor] - 1, bound - lengths[taker]) // 2
    slack = jnp.where((donor == order[0]) | (taker == order[0]) | (lengths[taker] == 0), 0, jnp.maximum(slack, 0))
    passed = jax.random.randint(jax.random.fold_in(own, 4), (count // 2,), 0, 1 << 20) % (slack + 1)
    lengths = lengths.at[donor].add(-passed).at[taker].add(passed)
    members = jnp.searchsorted(jnp.cumsum(lengths), jnp.arange(rows * top), side="right").astype(jnp.int32)
    grid = members.reshape(top, rows).T
    grid = grid[jax.random.permutation(jax.random.fold_in(own, 1), rows)]
    offset_by = jax.random.randint(jax.random.fold_in(own, 2), (rows, 1), 0, top)
    return jnp.take_along_axis(grid, (jnp.arange(top)[None, :] + offset_by) % top, axis=1)


def load_shares(number_of, total, bound, skew, full):
    loads = [(1 << 20) // math.isqrt(grade ** skew) + 1 for grade in range(1, number_of + 1)]
    largest = bound if full else min(bound, max(-(-total // number_of), total * loads[0] // sum(loads)))
    least = 1 if total - largest >= number_of - 1 else 0
    given, spare = [largest] + [least] * (number_of - 1), total - largest - least * (number_of - 1)
    while spare > 0:
        candidates = [i for i in range(1, number_of) if given[i] < largest] or [i for i in range(1, number_of) if given[i] < bound]
        whole, left = sum([loads[i] for i in candidates]), spare
        for i in candidates:
            extra = min(bound - given[i], max(1, left * loads[i] // whole), spare)
            given[i] = given[i] + extra
            spare = spare - extra
    return np.array(given)


def noise(stream_key, dims, deviation, reach, split=(), kind=jnp.bfloat16):
    loudness = levels(stream_key, dims, split, -0.22, 0.18) if split else 1.0
    array = jax.random.normal(stream_key, dims, jnp.float32) * deviation * loudness
    return jnp.minimum(jnp.maximum(array, -reach), reach).astype(kind)


def setup_inputs(seed: int = 0) -> dict:
    seeds = jax.random.split(jax.random.key(seed), 13)
    stream_in = noise(seeds[0], (SEQS, LEN, D), 1.0, 6.0, ((0, 16), (1, 8)))
    queries = draw_queries(jax.random.fold_in(seeds[12], 71), 0)
    key_rows = draw_key_rows(jax.random.fold_in(seeds[12], 71), 0)
    value_rows = noise(seeds[3], (SEQS, LEN, D), 1.0, 6.0, ((0, 16), (1, 8)))
    segment_ids = jax.vmap(lambda own: jnp.searchsorted(jnp.cumsum(uneven(own, UTTS, LEN, LONGEST, 0)), jnp.arange(LEN), side="right"))(jax.random.split(seeds[4], SEQS)).reshape((SEQS, LEN)).astype(jnp.int32)
    norm_gain = jnp.clip(1.0 + 0.18 * jax.random.normal(seeds[5], (D,), jnp.float32), 0.1, 1.9)
    router_w = noise(seeds[6], (D, EXPERTS), D ** -0.5, 0.125)
    expert_ids_keys = jax.random.split(jax.random.fold_in(seeds[7], 1), SEQS * LEN // TOK_DEV)
    expert_ids_turns = jax.random.permutation(jax.random.fold_in(seeds[7], 3), SEQS * LEN // TOK_DEV)
    expert_ids = jax.vmap(lambda own, number: deal_out(jax.random.fold_in(seeds[7], 2), own, number, TOK_DEV, EXPERTS, 2, CAP, 2))(expert_ids_keys, expert_ids_turns).reshape((SEQS, LEN, 2))
    gate_w = noise(seeds[8], (PIECES, D, HALF), D ** -0.5, 0.125, ((0, 128),))
    up_w = noise(seeds[9], (PIECES, D, HALF), D ** -0.5, 0.125, ((0, 128),))
    down_w = noise(seeds[10], (PIECES, HALF, D), FFE ** -0.5, 0.1875, ((0, 128),))
    out_grad = noise(seeds[11], (SEQS, LEN, D), 1.0, 6.0, ((0, 16), (1, 8)))
    return {"stream_in": stream_in, "queries": queries, "key_rows": key_rows, "value_rows": value_rows, "segment_ids": segment_ids, "norm_gain": norm_gain, "router_w": router_w, "expert_ids": expert_ids, "gate_w": gate_w, "up_w": up_w, "down_w": down_w, "out_grad": out_grad}


def reference(stream_in, queries, key_rows, value_rows, segment_ids, norm_gain, router_w, expert_ids, gate_w, up_w, down_w, out_grad):
    scale = HD ** (-0.5)
    f32 = jnp.float32
    bf16 = jnp.bfloat16

    def split_heads(x):
        return x.astype(f32).reshape(LEN, HEADS, HD)

    def probabilities(query, keys, seg):
        scores = jnp.einsum('qhd,khd->hqk', split_heads(query), split_heads(keys)) * scale
        scores = jnp.where((seg[:, None] == seg[None, :])[None], scores, -1e+30)
        top = lax.optimization_barrier(jnp.max(scores, -1, keepdims=True))
        lse = top + jnp.log(lax.optimization_barrier(jnp.sum(jnp.exp(scores - top), -1, keepdims=True)))
        return jnp.exp(scores - lse)

    def forward_seq(items):
        query, keys, values, seg = items
        probs_b = probabilities(query, keys, seg).astype(bf16)
        attended = jnp.einsum('hqk,khd->qhd', probs_b.astype(f32), split_heads(values))
        return attended.reshape(LEN, D)
    attended = lax.map(forward_seq, (queries, key_rows, value_rows, segment_ids))
    mixed = (stream_in.astype(f32) + attended).astype(bf16).reshape(-1, D).astype(f32)
    rstd = lax.rsqrt(lax.optimization_barrier(jnp.mean(mixed * mixed, -1, keepdims=True)) + 1e-06)
    normed = mixed * rstd
    routed_in = (normed * norm_gain).astype(bf16)
    frames = routed_in.shape[0]
    logits = jnp.dot(routed_in, router_w, preferred_element_type=f32)
    ids = expert_ids.reshape(frames, 2)
    onehot = (ids[:, :, None] == jnp.arange(EXPERTS, dtype=jnp.int32)[None, None, :]).astype(f32)
    sig = jax.nn.sigmoid(lax.optimization_barrier(jnp.sum(onehot * logits[:, None, :], -1)))
    gate = sig.astype(bf16)
    total = frames * 2
    grads_flat = out_grad.reshape(frames, D)
    rows_pad = jnp.concatenate([jnp.repeat(routed_in, 2, axis=0), jnp.zeros((1, D), bf16)], 0)
    grad_pad = jnp.concatenate([jnp.repeat(grads_flat, 2, axis=0), jnp.zeros((1, D), bf16)], 0)
    gate_pad = jnp.concatenate([gate.reshape(-1), jnp.zeros((1,), bf16)], 0)
    flat_ids = ids.reshape(-1)
    slots = SEQS * N_OUTER * CAP

    def expert(index):
        picked = jnp.nonzero(flat_ids == index, size=slots, fill_value=total)[0].astype(jnp.int32)
        rows = rows_pad[picked]
        grads = grad_pad[picked]
        weight = gate_pad[picked].astype(f32)[:, None]
        w_gate = lax.dynamic_slice_in_dim(gate_w, 2 * index, 2, 0)
        w_up = lax.dynamic_slice_in_dim(up_w, 2 * index, 2, 0)
        w_down = lax.dynamic_slice_in_dim(down_w, 2 * index, 2, 0)
        score = jnp.zeros((slots,), f32)
        inputs = jnp.zeros((slots, D), f32)
        parts = []
        for half in range(2):
            a_val = jnp.dot(rows, w_gate[half], preferred_element_type=f32)
            b_val = jnp.dot(rows, w_up[half], preferred_element_type=f32)
            sg = jax.nn.sigmoid(a_val)
            hidden = (a_val * sg * b_val).astype(bf16)
            t_val = jnp.dot(grads, w_down[half].T, preferred_element_type=f32)
            score = score + lax.optimization_barrier(jnp.sum(hidden.astype(f32) * t_val, -1)).astype(bf16).astype(f32)
            d_hidden = weight * t_val
            d_a = (d_hidden * b_val * sg * (1.0 + a_val * (1.0 - sg))).astype(bf16)
            d_b = (d_hidden * a_val * sg).astype(bf16)
            scaled = (weight * grads.astype(f32)).astype(bf16)
            g_gate = jnp.dot(rows.T, d_a, preferred_element_type=f32).astype(bf16)
            g_up = jnp.dot(rows.T, d_b, preferred_element_type=f32).astype(bf16)
            g_down = jnp.dot(hidden.T, scaled, preferred_element_type=f32).astype(bf16)
            part = jnp.dot(d_a, w_gate[half].T, preferred_element_type=f32) + jnp.dot(d_b, w_up[half].T, preferred_element_type=f32)
            inputs = inputs + part.astype(bf16).astype(f32)
            parts.append((g_gate, g_up, g_down))
        stack_gate = jnp.stack([parts[0][0], parts[1][0]])
        stack_up = jnp.stack([parts[0][1], parts[1][1]])
        stack_down = jnp.stack([parts[0][2], parts[1][2]])
        return (picked, score, inputs, stack_gate, stack_up, stack_down)
    picked, score, inputs, g_gate, g_up, g_down = lax.map(expert, jnp.arange(EXPERTS, dtype=jnp.int32))
    score_all = jnp.zeros((total + 1,), f32).at[picked.reshape(-1)].add(score.reshape(-1))[:total]
    input_all = jnp.zeros((total + 1, D), f32).at[picked.reshape(-1)].add(inputs.reshape(-1, D))[:total]
    d_logit = score_all.reshape(frames, 2) * sig * (1.0 - sig)
    logit_grad = lax.optimization_barrier(jnp.sum(onehot * d_logit[:, :, None], 1)).astype(bf16)
    d_routed = jnp.dot(logit_grad, router_w.T, preferred_element_type=f32) + lax.optimization_barrier(jnp.sum(input_all.reshape(frames, 2, D), 1))
    router_grad = jnp.dot(routed_in.T, logit_grad, preferred_element_type=f32)
    gain_grad = lax.optimization_barrier(jnp.sum(d_routed * normed, 0))
    scaled_g = d_routed * norm_gain
    stream_grad = (grads_flat.astype(f32) + rstd * (scaled_g - normed * lax.optimization_barrier(jnp.mean(scaled_g * normed, -1, keepdims=True)))).astype(bf16)
    stream_grad = stream_grad.reshape(SEQS, LEN, D)

    def backward_seq(items):
        query, keys, values, seg, attended_seq, grad_seq = items
        probs = probabilities(query, keys, seg)
        probs_b = probs.astype(bf16)
        grad_h = split_heads(grad_seq)
        d_probs = jnp.einsum('qhd,khd->hqk', grad_h, split_heads(values))
        delta = lax.optimization_barrier(jnp.sum(grad_h * attended_seq.reshape(LEN, HEADS, HD), -1)).T
        d_scores = (probs * (d_probs - delta[:, :, None])).astype(bf16).astype(f32)
        q_grad = (scale * jnp.einsum('hqk,khd->qhd', d_scores, split_heads(keys))).astype(bf16).reshape(LEN, D)
        blocks = d_scores.reshape(HEADS, N_OUTER, TOK_DEV, LEN)
        q_blocks = split_heads(query).reshape(N_OUTER, TOK_DEV, HEADS, HD)
        k_parts = (scale * jnp.einsum('hnqk,nqhd->nkhd', blocks, q_blocks)).astype(bf16).astype(f32)
        p_blocks = probs_b.astype(f32).reshape(HEADS, N_OUTER, TOK_DEV, LEN)
        g_blocks = grad_h.reshape(N_OUTER, TOK_DEV, HEADS, HD)
        v_parts = jnp.einsum('hnqk,nqhd->nkhd', p_blocks, g_blocks).astype(bf16).astype(f32)
        k_grad = lax.optimization_barrier(jnp.sum(k_parts, 0)).astype(bf16).reshape(LEN, D)
        v_grad = lax.optimization_barrier(jnp.sum(v_parts, 0)).astype(bf16).reshape(LEN, D)
        return (q_grad, k_grad, v_grad)
    query_grad, key_grad, value_grad = lax.map(backward_seq, (queries, key_rows, value_rows, segment_ids, attended, stream_grad))
    gate_grad = g_gate.reshape(PIECES, D, HALF)
    up_grad = g_up.reshape(PIECES, D, HALF)
    down_grad = g_down.reshape(PIECES, HALF, D)
    return (stream_grad, query_grad, key_grad, value_grad, gain_grad, router_grad, gate_grad, up_grad, down_grad)
```

```python
import jax
import jax.numpy as jnp
import numpy as np
from jax import lax
from jax.experimental import pallas as pl
from jax.experimental.pallas import tpu as pltpu
from jax.sharding import Mesh, PartitionSpec as P

F32 = jnp.float32
BF16 = jnp.bfloat16
HEADS = 20
HD = 128
NB = 8
TOK = 128
LEN = 1024
WIDTH = 2560
EXPERTS = 64
SLOTS = 6
QROWS = 320
KVROWS = 384
CHUNK = 128
BACK = 160
SCALE = HD**-0.5
NT = (((1,), (1,)), ((), ()))
TN = (((0,), (0,)), ((), ()))
MIB = 1 << 20


def params(mib):
    return pltpu.CompilerParams(vmem_limit_bytes=mib * MIB)


def dot(a, b):
    return jnp.dot(a, b, preferred_element_type=F32)


def owned(dev):
    pair, odd = dev // 2, dev % 2
    return (5 * pair + 3 * odd, 5 * pair + 3 * odd + 1), 5 * pair + 2, odd


def cols(index):
    return slice(index * HD, (index + 1) * HD)


def tile_kinds(t):
    first, second = 2 * t, 2 * t + 1
    return (first // 3, first % 3), (second // 3, second % 3)


def selections(group):
    rows = group * SLOTS
    plain = np.zeros((2, rows, group * 16), np.float32)
    extra = np.zeros((2, 3, rows, group * 16), np.float32)
    for par in range(2):
        for s in range(group):
            for k in range(SLOTS):
                plain[par, s * SLOTS + k, s * 16 + par * 8 + k] = 1
                extra[par, k // 2, s * SLOTS + k, s * 16 + par * 8 + 6 + k % 2] = 1
    take = np.stack(
        [np.concatenate([extra[(u + v) % 2, v] for v in range(3)], 1) for u in range(2)]
    )
    packs = []
    for t in (0, 1, 2, 7):
        (_, v0), (_, v1) = tile_kinds(t)
        last = 0.0 if t == 7 else 1.0
        packs.append(
            np.concatenate(
                [plain[0].T, last * plain[1].T, extra[0, v0].T, last * extra[1, v1].T], 1
            )
        )
    return plain, take, np.stack(packs)


GROUP = 16
PLAIN, TAKE, PACK = selections(GROUP)


def pack_heads_kernel(q_ref, k_ref, v_ref, out_ref):
    for odd in range(2):
        heads, shared, _ = owned(odd)
        for i, h in enumerate(heads):
            out_ref[odd, i * HD : (i + 1) * HD, :] = q_ref[:, cols(h)]
        out_ref[odd, 256:320, :] = q_ref[64 * odd : 64 * odd + 64, cols(shared)]
        for base, ref in ((QROWS, k_ref), (QROWS + KVROWS, v_ref)):
            for i, h in enumerate(heads + (shared,)):
                out_ref[odd, base + i * HD : base + (i + 1) * HD, :] = ref[:, cols(h)]


def pack_heads(q, k, v):
    rows = QROWS + 2 * KVROWS
    return pl.pallas_call(
        pack_heads_kernel,
        grid=(4,),
        in_specs=[pl.BlockSpec((TOK, 5 * HD), lambda p: (0, p))] * 3,
        out_specs=pl.BlockSpec((2, rows, HD), lambda p: (p, 0, 0)),
        out_shape=jax.ShapeDtypeStruct((NB, rows, HD), BF16),
        compiler_params=params(24),
        name="pack_heads",
    )(q, k, v)


def unpack_grads_kernel(in_ref, q_ref, k_ref, v_ref):
    halves = []
    for odd in range(2):
        heads, shared, _ = owned(odd)
        for i, h in enumerate(heads):
            q_ref[:, cols(h)] = in_ref[odd, i * HD : (i + 1) * HD, :]
        q_ref[64 * odd : 64 * odd + 64, cols(shared)] = in_ref[odd, 256:320, :]
        for base, ref in ((QROWS, k_ref), (QROWS + KVROWS, v_ref)):
            for i, h in enumerate(heads):
                ref[:, cols(h)] = in_ref[odd, base + i * HD : base + (i + 1) * HD, :]
    for base, ref in ((QROWS, k_ref), (QROWS + KVROWS, v_ref)):
        halves = [in_ref[odd, base + 256 : base + 384, :].astype(F32) for odd in range(2)]
        ref[:, cols(2)] = (halves[0] + halves[1]).astype(BF16)


def unpack_grads(buf):
    rows = QROWS + 2 * KVROWS
    return pl.pallas_call(
        unpack_grads_kernel,
        grid=(4,),
        in_specs=[pl.BlockSpec((2, rows, HD), lambda p: (p, 0, 0))],
        out_specs=[pl.BlockSpec((TOK, 5 * HD), lambda p: (0, p))] * 3,
        out_shape=[jax.ShapeDtypeStruct((TOK, WIDTH), BF16)] * 3,
        compiler_params=params(24),
        name="unpack_grads",
    )(buf)


def query_tiles():
    tiles = [(hi, slice(2 * t, 2 * t + 2), slice(hi * HD, (hi + 1) * HD), t) for hi in range(2) for t in range(4)]
    return tiles + [(2, slice(4 * t, 4 * t + 4), slice(256, 320), t) for t in range(2)]


def same_segment(hi, t, split, odd, keys_seg):
    lane = lax.broadcasted_iota(jnp.int32, (1, 256), 1)
    if hi < 2:
        frame = 256 * t + lane
    else:
        frame = 512 * t + (lane >> 6) * 128 + odd * 64 + (lane & 63)
    return keys_seg == (frame >= split).astype(jnp.int32)


def attention_kernel(info_ref, buf_ref, o_ref, lse_ref):
    split, odd = info_ref[0], info_ref[1]
    keys_seg = (lax.broadcasted_iota(jnp.int32, (LEN, 1), 0) >= split).astype(jnp.int32)
    held = None
    for number, (hi, blocks, rows, t) in enumerate(query_tiles()):
        if hi != held:
            held = hi
            k = buf_ref[:, QROWS + hi * HD : QROWS + (hi + 1) * HD, :].reshape(LEN, HD)
            v = buf_ref[:, QROWS + KVROWS + hi * HD : QROWS + KVROWS + (hi + 1) * HD, :].reshape(LEN, HD)
            v_t = v.astype(F32).T.astype(BF16)
        q = buf_ref[blocks, rows, :].reshape(256, HD)
        scores = lax.dot_general(k, q, NT, preferred_element_type=F32) * SCALE
        scores = jnp.where(same_segment(hi, t, split, odd, keys_seg), scores, -1e30)
        top = jnp.max(scores, 0, keepdims=True)
        e = jnp.exp(scores - top)
        total = jnp.sum(e, 0, keepdims=True)
        out = dot(v_t, e.astype(BF16)) / total
        o_ref[blocks, rows, :] = out.T.astype(BF16).reshape(o_ref[blocks, rows, :].shape)
        lse_ref[number] = jnp.broadcast_to(top + jnp.log(total), (8, 256))


def attention(info, buf):
    return pl.pallas_call(
        attention_kernel,
        in_specs=[pl.BlockSpec(memory_space=pltpu.SMEM), pl.BlockSpec(memory_space=pltpu.VMEM)],
        out_specs=[pl.BlockSpec(memory_space=pltpu.VMEM)] * 2,
        out_shape=[
            jax.ShapeDtypeStruct((NB, QROWS, HD), BF16),
            jax.ShapeDtypeStruct((10, 8, 256), F32),
        ],
        compiler_params=params(40),
        name="attention",
    )(info, buf)


def attention_grad_kernel(info_ref, buf_ref, do_ref, o_ref, lse_ref, out_ref):
    split, odd = info_ref[0], info_ref[1]
    keys_seg = (lax.broadcasted_iota(jnp.int32, (LEN, 1), 0) >= split).astype(jnp.int32)
    held = None
    sums = None

    def flush(hi):
        at = QROWS + hi * HD
        out_ref[:, at : at + HD, :] = (sums[0] * SCALE).astype(BF16).reshape(NB, TOK, HD)
        at = at + KVROWS
        out_ref[:, at : at + HD, :] = sums[1].astype(BF16).reshape(NB, TOK, HD)

    for number, (hi, blocks, rows, t) in enumerate(query_tiles()):
        if hi != held:
            if held is not None:
                flush(held)
            held = hi
            sums = None
            k = buf_ref[:, QROWS + hi * HD : QROWS + (hi + 1) * HD, :].reshape(LEN, HD)
            v = buf_ref[:, QROWS + KVROWS + hi * HD : QROWS + KVROWS + (hi + 1) * HD, :].reshape(LEN, HD)
            k_t = k.astype(F32).T.astype(BF16)
        q = buf_ref[blocks, rows, :].reshape(256, HD)
        grad = do_ref[blocks, rows, :].reshape(256, HD)
        out = o_ref[blocks, rows, :].reshape(256, HD)
        delta = jnp.sum((grad.astype(F32) * out.astype(F32)).T, 0, keepdims=True)
        scores = lax.dot_general(k, q, NT, preferred_element_type=F32) * SCALE
        scores = jnp.where(same_segment(hi, t, split, odd, keys_seg), scores, -1e30)
        probs = jnp.exp(scores - lse_ref[number, 0:1, :])
        d_probs = lax.dot_general(v, grad, NT, preferred_element_type=F32)
        d_scores = (probs * (d_probs - delta)).astype(BF16)
        terms = (dot(d_scores, q), dot(probs.astype(BF16), grad))
        sums = terms if sums is None else (sums[0] + terms[0], sums[1] + terms[1])
        d_q = (dot(k_t, d_scores) * SCALE).T.astype(BF16)
        out_ref[blocks, rows, :] = d_q.reshape(out_ref[blocks, rows, :].shape)
    flush(held)


def attention_grad(info, buf, grad, out, lse):
    return pl.pallas_call(
        attention_grad_kernel,
        in_specs=[pl.BlockSpec(memory_space=pltpu.SMEM)] + [pl.BlockSpec(memory_space=pltpu.VMEM)] * 4,
        out_specs=pl.BlockSpec(memory_space=pltpu.VMEM),
        out_shape=jax.ShapeDtypeStruct((NB, QROWS + 2 * KVROWS, HD), BF16),
        compiler_params=params(44),
        name="attention_grad",
    )(info, buf, grad, out, lse)


def place_kernel(ids_ref, out_ref):
    expert = lax.broadcasted_iota(jnp.int32, (EXPERTS, TOK), 0)
    chosen = ((ids_ref[0:1, :] == expert) | (ids_ref[1:2, :] == expert)).astype(F32)
    before = lax.broadcasted_iota(jnp.int32, (TOK, TOK), 0) < lax.broadcasted_iota(jnp.int32, (TOK, TOK), 1)
    slot = dot(chosen.astype(BF16), before.astype(BF16))
    slot = jnp.where(chosen > 0.5, slot, -100.0).astype(jnp.int32)
    slot = slot.reshape(EXPERTS, 1, TOK)
    row = lax.broadcasted_iota(jnp.int32, (EXPERTS, 16, TOK), 1)

    def put(index, mask):
        out_ref[index] = mask.astype(F32).astype(BF16).reshape(EXPERTS * 16, TOK)

    for par in range(2):
        put(par, (slot == row - 8 * par) & (row >= 8 * par) & (row < 8 * par + 6))
        for v in range(3):
            here = (row >= 8 * par + 6) & (row < 8 * par + 8)
            put(2 + 3 * par + v, (slot == row - 8 * par - 6 + 2 * v) & here)


def place_rows(ids):
    return pl.pallas_call(
        place_kernel,
        out_shape=jax.ShapeDtypeStruct((8, EXPERTS * 16, TOK), BF16),
        compiler_params=params(24),
        name="place_rows",
    )(ids)


def dispatch(place_ref, block_of, out_ref):
    for t in range(8):
        (u0, v0), (u1, v1) = tile_kinds(t)
        if t < 7:
            left = jnp.concatenate([place_ref[0], place_ref[1], place_ref[2 + v0], place_ref[5 + v1]], 1)
            right = [block_of(2 * t), block_of(2 * t + 1), block_of(15 + u0), block_of(15 + u1)]
        else:
            left = jnp.concatenate([place_ref[0], place_ref[2 + v0]], 1)
            right = [block_of(2 * t), block_of(15 + u0)]
        rows = dot(left, jnp.concatenate(right, 0))
        out_ref[:, t * 16 : (t + 1) * 16, :] = rows.astype(BF16).reshape(EXPERTS, 16, HD)


def send_grads_kernel(place_ref, grad_ref, out_ref):
    dispatch(place_ref, lambda c: grad_ref[:, cols(c)], out_ref)


def send_grads(place, grad):
    return pl.pallas_call(
        send_grads_kernel,
        out_shape=jax.ShapeDtypeStruct((EXPERTS, CHUNK, HD), BF16),
        compiler_params=params(32),
        name="send_grads",
    )(place, grad)


def norm_kernel(place_ref, att_ref, stream_ref, gain_ref, mixed_ref, out_ref, routed_ref):
    for dev in range(NB):
        heads, shared, odd = owned(dev)
        for i, h in enumerate(heads):
            att = att_ref[dev, i * HD : (i + 1) * HD, :].astype(F32)
            mixed_ref[:, cols(h)] = (stream_ref[:, cols(h)].astype(F32) + att).astype(BF16)
        half = slice(64 * odd, 64 * odd + 64)
        att = att_ref[dev, 256:320, :].astype(F32)
        mixed_ref[half, cols(shared)] = (stream_ref[half, cols(shared)].astype(F32) + att).astype(BF16)
    mixed = mixed_ref[...].astype(F32)
    rstd = lax.rsqrt(jnp.mean(mixed * mixed, -1, keepdims=True) + 1e-06)
    routed_ref[...] = (mixed * rstd * gain_ref[...]).astype(BF16)
    dispatch(place_ref, lambda c: routed_ref[:, cols(c)], out_ref)


def norm_and_send(place, att, stream, gain):
    return pl.pallas_call(
        norm_kernel,
        out_shape=[
            jax.ShapeDtypeStruct((TOK, WIDTH), BF16),
            jax.ShapeDtypeStruct((EXPERTS, CHUNK, HD), BF16),
        ],
        scratch_shapes=[pltpu.VMEM((TOK, WIDTH), BF16)],
        compiler_params=params(40),
        name="norm_and_send",
    )(place, att, stream, gain)


def unpack_kernel(plain_ref, take_ref, mine_ref, other_ref, out_ref):
    for side, ref in enumerate((mine_ref, other_ref)):
        tiles = [ref[:, t * 16 : (t + 1) * 16, :].reshape(GROUP * 16, HD) for t in range(8)]
        wide = jnp.concatenate(tiles, 1)
        for par in range(2):
            rows = dot(plain_ref[par], wide).astype(BF16)
            for t in range(8):
                if 2 * t + par < 15:
                    out_ref[side, :, cols(2 * t + par)] = rows[:, cols(t)]
        for u in range(5):
            tall = jnp.concatenate([tiles[(3 * u + v) // 2] for v in range(3)], 0)
            out_ref[side, :, cols(15 + u)] = dot(take_ref[u % 2], tall).astype(BF16)


def unpack_rows(mine, other):
    rows = GROUP * SLOTS
    whole = lambda shape: pl.BlockSpec(shape, lambda g: (0,) * len(shape))
    return pl.pallas_call(
        unpack_kernel,
        grid=(EXPERTS // GROUP,),
        in_specs=[whole(PLAIN.shape), whole(TAKE.shape)] + [pl.BlockSpec((GROUP, CHUNK, HD), lambda g: (g, 0, 0))] * 2,
        out_specs=pl.BlockSpec((2, rows, WIDTH), lambda g: (0, g, 0)),
        out_shape=jax.ShapeDtypeStruct((2, EXPERTS * SLOTS, WIDTH), BF16),
        compiler_params=params(32),
        name="unpack_rows",
    )(jnp.asarray(PLAIN, BF16), jnp.asarray(TAKE, BF16), mine, other)


def pack_back_kernel(pack_ref, in_ref, sums_ref, mine_ref, other_ref):
    for side, ref in enumerate((mine_ref, other_ref)):
        block_of = lambda c: in_ref[side, :, cols(c)]
        for t in range(8):
            (u0, _), (u1, _) = tile_kinds(t)
            last = t == 7
            right = [block_of(2 * t), block_of(2 * t + 1), block_of(15 + u0), block_of(19 if last else 15 + u1)]
            rows = dot(pack_ref[3 if last else t % 3], jnp.concatenate(right, 0)).reshape(GROUP, 16, HD)
            if last:
                top = jnp.concatenate([jnp.zeros((8, HD), F32), sums_ref[0:8, :]], 0)
                rows = rows + top[None]
            ref[:, t * 16 : (t + 1) * 16, :] = rows.astype(BF16)
        ref[:, 128:160, :] = jnp.broadcast_to(sums_ref[8:40, :].astype(BF16)[None], (GROUP, 32, HD))


def pack_back(inputs, sums):
    rows = GROUP * SLOTS
    return pl.pallas_call(
        pack_back_kernel,
        grid=(EXPERTS // GROUP,),
        in_specs=[
            pl.BlockSpec(PACK.shape, lambda g: (0, 0, 0)),
            pl.BlockSpec((2, rows, WIDTH), lambda g: (0, g, 0)),
            pl.BlockSpec((40, HD), lambda g: (0, 0)),
        ],
        out_specs=[pl.BlockSpec((GROUP, BACK, HD), lambda g: (g, 0, 0))] * 2,
        out_shape=[jax.ShapeDtypeStruct((EXPERTS, BACK, HD), BF16)] * 2,
        compiler_params=params(32),
        name="pack_back",
    )(jnp.asarray(PACK, BF16), inputs, sums)


def combine_kernel(place_ref, back_ref, mixed_ref, grad_ref, gain_ref, stream_ref, out_ref, d_ref):
    tiles = [back_ref[:, t * 16 : (t + 1) * 16, :].reshape(EXPERTS * 16, HD) for t in range(8)]
    wide = jnp.concatenate(tiles, 1)
    for par in range(2):
        rows = lax.dot_general(place_ref[par], wide, TN, preferred_element_type=F32)
        for t in range(8):
            if 2 * t + par < 15:
                d_ref[:, cols(2 * t + par)] = rows[:, cols(t)]
    for u in range(5):
        total = None
        for v in range(3):
            j = 3 * u + v
            term = lax.dot_general(place_ref[2 + 3 * (j % 2) + v], tiles[j // 2], TN, preferred_element_type=F32)
            total = term if total is None else total + term
        d_ref[:, cols(15 + u)] = total
    mixed = mixed_ref[...].astype(F32)
    rstd = lax.rsqrt(jnp.mean(mixed * mixed, -1, keepdims=True) + 1e-06)
    normed = mixed * rstd
    g = d_ref[...] * gain_ref[...]
    inner = jnp.mean(g * normed, -1, keepdims=True)
    stream_ref[...] = (grad_ref[...].astype(F32) + rstd * (g - normed * inner)).astype(BF16)
    for dev in range(NB):
        heads, shared, odd = owned(dev)
        for i, h in enumerate(heads):
            out_ref[dev, i * HD : (i + 1) * HD, :] = stream_ref[:, cols(h)]
        out_ref[dev, 256:320, :] = stream_ref[64 * odd : 64 * odd + 64, cols(shared)]


def combine(place, back, mixed, grad, gain):
    return pl.pallas_call(
        combine_kernel,
        out_shape=[
            jax.ShapeDtypeStruct((TOK, WIDTH), BF16),
            jax.ShapeDtypeStruct((NB, QROWS, HD), BF16),
        ],
        scratch_shapes=[pltpu.VMEM((TOK, WIDTH), F32)],
        compiler_params=params(48),
        name="combine",
    )(place, back, mixed, grad, gain)


def swap_cores(x):
    return lax.ppermute(x, "core", [(0, 1), (1, 0)])


def over_outer(x):
    return lax.all_to_all(x, "outer", split_axis=0, concat_axis=0, tiled=True)


def over_chips(x):
    return lax.all_to_all(x, ("outer", "chip"), split_axis=0, concat_axis=0, tiled=True)


def body(
    stream_in,
    queries,
    key_rows,
    value_rows,
    segment_ids,
    norm_gain,
    router_w,
    expert_ids,
    gate_w,
    up_w,
    down_w,
    out_grad,
):
    at = lax.axis_index("outer")
    split = jnp.sum((segment_ids[0] == 0).astype(jnp.int32))
    info = jnp.stack([split, at % 2]).astype(jnp.int32)
    gain = norm_gain.reshape(1, WIDTH)
    grads_local = out_grad[0]

    qkv = over_outer(pack_heads(queries[0], key_rows[0], value_rows[0]))
    place = place_rows(expert_ids[0].T)
    grads_mine = over_chips(send_grads(place, grads_local))
    grads_other = swap_cores(grads_mine)
    att, lse = attention(info, qkv)
    att_back = over_outer(att)
    mixed, rows_buf = norm_and_send(place, att_back, stream_in[0], gain)
    rows_mine = over_chips(rows_buf)
    rows_other = swap_cores(rows_mine)

    grads = unpack_rows(grads_mine, grads_other).reshape(2 * EXPERTS * SLOTS, WIDTH)
    rows = unpack_rows(rows_mine, rows_other).reshape(2 * EXPERTS * SLOTS, WIDTH)
    expert = at * 8 + lax.axis_index("chip")
    router_col = lax.dynamic_slice_in_dim(router_w.T, expert, 1, 0)
    w_gate, w_up, w_down = gate_w[0], up_w[0], down_w[0]
    a_val = dot(rows, w_gate)
    b_val = dot(rows, w_up)
    t_val = lax.dot_general(grads, w_down, NT, preferred_element_type=F32)
    logit = lax.dot_general(rows, router_col, NT, preferred_element_type=F32)
    sig = jax.nn.sigmoid(logit)
    gate = sig.astype(BF16).astype(F32)
    sg = jax.nn.sigmoid(a_val)
    hidden = (a_val * sg * b_val).astype(BF16)
    part_score = jnp.sum(hidden.astype(F32) * t_val, -1, keepdims=True).astype(BF16).astype(F32)
    d_hidden = gate * t_val
    d_a = (d_hidden * b_val * sg * (1.0 + a_val * (1.0 - sg))).astype(BF16)
    d_b = (d_hidden * a_val * sg).astype(BF16)
    scaled = (gate * grads.astype(F32)).astype(BF16)
    d_logit = part_score * sig * (1.0 - sig)
    part = (
        lax.dot_general(d_a, w_gate, NT, preferred_element_type=F32)
        + lax.dot_general(d_b, w_up, NT, preferred_element_type=F32)
        + d_logit * router_col.astype(F32)
    )
    gain_part = jnp.sum(part * rows.astype(F32), 0) / norm_gain
    router_part = lax.dot_general(d_logit.astype(BF16), rows, TN, preferred_element_type=F32)[0]
    sums = jnp.concatenate([router_part, gain_part]).reshape(40, HD)
    back_mine, back_other = pack_back(part.astype(BF16).reshape(2, EXPERTS * SLOTS, WIDTH), sums)
    back = over_chips(back_mine + swap_cores(back_other))

    gate_grad = lax.dot_general(rows, d_a, TN, preferred_element_type=F32).astype(BF16)
    up_grad = lax.dot_general(rows, d_b, TN, preferred_element_type=F32).astype(BF16)
    down_grad = lax.dot_general(hidden, scaled, TN, preferred_element_type=F32).astype(BF16)

    stream_grad, grad_heads = combine(place, back, mixed, grads_local, gain)
    router_grad = back[:, 120:140, :].reshape(EXPERTS, WIDTH).T.astype(F32)
    gain_grad = jnp.sum(back[:, 140:160, :].astype(F32), 0).reshape(WIDTH)
    grad_in = over_outer(grad_heads)
    grads_out = over_outer(attention_grad(info, qkv, grad_in, att, lse))
    query_grad, key_grad, value_grad = unpack_grads(grads_out)
    return (
        stream_grad[None],
        query_grad[None],
        key_grad[None],
        value_grad[None],
        gain_grad,
        router_grad,
        gate_grad[None],
        up_grad[None],
        down_grad[None],
    )


def solution(mesh):
    chips = Mesh(mesh.devices.reshape(8, 8, 2), ("outer", "chip", "core"))
    inner = ("chip", "core")
    every = ("outer", "chip", "core")
    frames = P(inner, "outer", None)
    pieces = P(every, None, None)
    placed = (
        frames,
        frames,
        frames,
        frames,
        P(inner, None),
        P(),
        P(),
        frames,
        pieces,
        pieces,
        pieces,
        frames,
    )
    return jax.shard_map(
        body,
        mesh=chips,
        in_specs=placed,
        out_specs=(frames, frames, frames, frames, P(), P(), pieces, pieces, pieces),
        check_vma=False,
    )
```

```python
import jax
import jax.numpy as jnp
from jax import lax
from jax.experimental import pallas as pl
from jax.experimental.pallas import tpu as pltpu
from jax.sharding import Mesh, PartitionSpec as P

F32 = jnp.float32
BF16 = jnp.bfloat16
HEADS = 20
HD = 128
NB = 8
TOK = 128
LEN = 1024
WIDTH = 2560
EXPERTS = 64
HIDDEN = 512
SLOTS = 6
QROWS = 320
KVROWS = 384
CHUNK = 128
BACK = 160
SCALE = HD**-0.5
NT = (((1,), (1,)), ((), ()))
TN = (((0,), (0,)), ((), ()))
MIB = 1 << 20


def params(mib):
    return pltpu.CompilerParams(vmem_limit_bytes=mib * MIB)


def shape(*dims, dtype=BF16):
    return pltpu.HBM(dims, dtype)


def hbm(*arrays):
    return [pltpu.with_memory_space_constraint(x, pltpu.HBM) for x in arrays]


def vmem(*arrays):
    return [pltpu.with_memory_space_constraint(x, pltpu.VMEM) for x in arrays]


def dot(a, b):
    return jnp.dot(a, b, preferred_element_type=F32)


def owned(dev):
    pair, odd = dev // 2, dev % 2
    return (5 * pair + 3 * odd, 5 * pair + 3 * odd + 1), 5 * pair + 2, odd


def cols(index):
    return slice(index * HD, (index + 1) * HD)


GROUP = 16


def pack_heads_kernel(q_ref, k_ref, v_ref, out_ref):
    for odd in range(2):
        heads, shared, _ = owned(odd)
        for i, h in enumerate(heads):
            out_ref[odd, i * HD : (i + 1) * HD, :] = q_ref[:, cols(h)]
        out_ref[odd, 256:320, :] = q_ref[64 * odd : 64 * odd + 64, cols(shared)]
        for base, ref in ((QROWS, k_ref), (QROWS + KVROWS, v_ref)):
            for i, h in enumerate(heads + (shared,)):
                out_ref[odd, base + i * HD : base + (i + 1) * HD, :] = ref[:, cols(h)]


def pack_heads(q, k, v):
    rows = QROWS + 2 * KVROWS
    return pl.pallas_call(
        pack_heads_kernel,
        grid=(4,),
        in_specs=[pl.BlockSpec((TOK, 5 * HD), lambda p: (0, p))] * 3,
        out_specs=pl.BlockSpec((2, rows, HD), lambda p: (p, 0, 0)),
        out_shape=shape(NB, rows, HD),
        compiler_params=params(24),
        name="pack_heads",
    )(*hbm(q, k, v))


def unpack_grads_kernel(in_ref, q_ref, k_ref, v_ref):
    halves = []
    for odd in range(2):
        heads, shared, _ = owned(odd)
        for i, h in enumerate(heads):
            q_ref[:, cols(h)] = in_ref[odd, i * HD : (i + 1) * HD, :]
        q_ref[64 * odd : 64 * odd + 64, cols(shared)] = in_ref[odd, 256:320, :]
        for base, ref in ((QROWS, k_ref), (QROWS + KVROWS, v_ref)):
            for i, h in enumerate(heads):
                ref[:, cols(h)] = in_ref[odd, base + i * HD : base + (i + 1) * HD, :]
    for base, ref in ((QROWS, k_ref), (QROWS + KVROWS, v_ref)):
        halves = [in_ref[odd, base + 256 : base + 384, :].astype(F32) for odd in range(2)]
        ref[:, cols(2)] = (halves[0] + halves[1]).astype(BF16)


def unpack_grads(buf):
    rows = QROWS + 2 * KVROWS
    return pl.pallas_call(
        unpack_grads_kernel,
        grid=(4,),
        in_specs=[pl.BlockSpec((2, rows, HD), lambda p: (p, 0, 0))],
        out_specs=[pl.BlockSpec((TOK, 5 * HD), lambda p: (0, p))] * 3,
        out_shape=[shape(TOK, WIDTH)] * 3,
        compiler_params=params(24),
        name="unpack_grads",
    )(*hbm(buf))


def query_tiles():
    tiles = [(hi, slice(2 * t, 2 * t + 2), slice(hi * HD, (hi + 1) * HD), t) for hi in range(2) for t in range(4)]
    return tiles + [(2, slice(4 * t, 4 * t + 4), slice(256, 320), t) for t in range(2)]


def same_segment(hi, t, split, odd, keys_seg):
    lane = lax.broadcasted_iota(jnp.int32, (1, 256), 1)
    if hi < 2:
        frame = 256 * t + lane
    else:
        frame = 512 * t + (lane >> 6) * 128 + odd * 64 + (lane & 63)
    return keys_seg == (frame >= split).astype(jnp.int32)


def attention_kernel(info_ref, buf_ref, o_ref, lse_ref):
    split, odd = info_ref[0], info_ref[1]
    keys_seg = (lax.broadcasted_iota(jnp.int32, (LEN, 1), 0) >= split).astype(jnp.int32)
    held = None
    for number, (hi, blocks, rows, t) in enumerate(query_tiles()):
        if hi != held:
            held = hi
            k = buf_ref[:, QROWS + hi * HD : QROWS + (hi + 1) * HD, :].reshape(LEN, HD)
            v = buf_ref[:, QROWS + KVROWS + hi * HD : QROWS + KVROWS + (hi + 1) * HD, :].reshape(LEN, HD)
            v_t = v.astype(F32).T.astype(BF16)
        q = buf_ref[blocks, rows, :].reshape(256, HD)
        scores = lax.dot_general(k, q, NT, preferred_element_type=F32) * SCALE
        scores = jnp.where(same_segment(hi, t, split, odd, keys_seg), scores, -1e30)
        top = jnp.max(scores, 0, keepdims=True)
        e = jnp.exp(scores - top)
        total = jnp.sum(e, 0, keepdims=True)
        out = dot(v_t, e.astype(BF16)) / total
        o_ref[blocks, rows, :] = out.T.astype(BF16).reshape(o_ref[blocks, rows, :].shape)
        lse_ref[number] = jnp.broadcast_to(top + jnp.log(total), (8, 256))


def attention(info, buf):
    return pl.pallas_call(
        attention_kernel,
        in_specs=[pl.BlockSpec(memory_space=pltpu.SMEM), pl.BlockSpec(memory_space=pltpu.VMEM)],
        out_specs=[pl.BlockSpec(memory_space=pltpu.VMEM)] * 2,
        out_shape=[
            shape(NB, QROWS, HD),
            shape(10, 8, 256, dtype=F32),
        ],
        compiler_params=params(40),
        name="attention",
    )(info, *hbm(buf))


def attention_grad_kernel(info_ref, buf_ref, do_ref, o_ref, lse_ref, out_ref):
    split, odd = info_ref[0], info_ref[1]
    keys_seg = (lax.broadcasted_iota(jnp.int32, (LEN, 1), 0) >= split).astype(jnp.int32)
    held = None
    sums = None

    def flush(hi):
        at = QROWS + hi * HD
        out_ref[:, at : at + HD, :] = (sums[0] * SCALE).astype(BF16).reshape(NB, TOK, HD)
        at = at + KVROWS
        out_ref[:, at : at + HD, :] = sums[1].astype(BF16).reshape(NB, TOK, HD)

    for number, (hi, blocks, rows, t) in enumerate(query_tiles()):
        if hi != held:
            if held is not None:
                flush(held)
            held = hi
            sums = None
            k = buf_ref[:, QROWS + hi * HD : QROWS + (hi + 1) * HD, :].reshape(LEN, HD)
            v = buf_ref[:, QROWS + KVROWS + hi * HD : QROWS + KVROWS + (hi + 1) * HD, :].reshape(LEN, HD)
            k_t = k.astype(F32).T.astype(BF16)
        q = buf_ref[blocks, rows, :].reshape(256, HD)
        grad = do_ref[blocks, rows, :].reshape(256, HD)
        out = o_ref[blocks, rows, :].reshape(256, HD)
        delta = jnp.sum((grad.astype(F32) * out.astype(F32)).T, 0, keepdims=True)
        scores = lax.dot_general(k, q, NT, preferred_element_type=F32) * SCALE
        scores = jnp.where(same_segment(hi, t, split, odd, keys_seg), scores, -1e30)
        probs = jnp.exp(scores - lse_ref[number, 0:1, :])
        d_probs = lax.dot_general(v, grad, NT, preferred_element_type=F32)
        d_scores = (probs * (d_probs - delta)).astype(BF16)
        terms = (dot(d_scores, q), dot(probs.astype(BF16), grad))
        sums = terms if sums is None else (sums[0] + terms[0], sums[1] + terms[1])
        d_q = (dot(k_t, d_scores) * SCALE).T.astype(BF16)
        out_ref[blocks, rows, :] = d_q.reshape(out_ref[blocks, rows, :].shape)
    flush(held)


def attention_grad(info, buf, grad, out, lse):
    return pl.pallas_call(
        attention_grad_kernel,
        in_specs=[pl.BlockSpec(memory_space=pltpu.SMEM)] + [pl.BlockSpec(memory_space=pltpu.VMEM)] * 4,
        out_specs=pl.BlockSpec(memory_space=pltpu.VMEM),
        out_shape=shape(NB, QROWS + 2 * KVROWS, HD),
        compiler_params=params(44),
        name="attention_grad",
    )(info, *hbm(buf, grad, out, lse))


def place_kernel(ids_ref, out_ref):
    expert = lax.broadcasted_iota(jnp.int32, (EXPERTS, TOK), 0)
    chosen = ((ids_ref[0:1, :] == expert) | (ids_ref[1:2, :] == expert)).astype(F32)
    before = lax.broadcasted_iota(jnp.int32, (TOK, TOK), 0) < lax.broadcasted_iota(jnp.int32, (TOK, TOK), 1)
    slot = dot(chosen.astype(BF16), before.astype(BF16))
    slot = jnp.where(chosen > 0.5, slot, -100.0).astype(jnp.int32)
    slot = slot.reshape(EXPERTS, 1, TOK)
    row = lax.broadcasted_iota(jnp.int32, (EXPERTS, 8, TOK), 1)
    out_ref[...] = close_up((slot == row).astype(F32)).astype(BF16)


def place_rows(ids):
    return pl.pallas_call(
        place_kernel,
        out_shape=shape(EXPERTS * SLOTS, TOK),
        compiler_params=params(24),
        name="place_rows",
    )(ids)


def close_up(x):
    row = lax.broadcasted_iota(jnp.int32, (1, 8, HD), 1)
    x = x.reshape(16, 4, 8, HD)
    b, c, d = pltpu.roll(x[:, 1], 6, 1), pltpu.roll(x[:, 2], 4, 1), pltpu.roll(x[:, 3], 2, 1)
    parts = (jnp.where(row < 6, x[:, 0], b), jnp.where(row < 4, b, c), jnp.where(row < 2, c, d))
    return jnp.concatenate([p[:, None] for p in parts], 1).reshape(EXPERTS * SLOTS, HD)


def spread(x):
    row = lax.broadcasted_iota(jnp.int32, (1, 8, HD), 1)
    x = x.reshape(16, 3, 8, HD)
    b = pltpu.roll(jnp.where(row >= 6, x[:, 0], x[:, 1]), 2, 1)
    c = pltpu.roll(jnp.where(row >= 4, x[:, 1], x[:, 2]), 4, 1)
    d = pltpu.roll(x[:, 2], 6, 1)
    return jnp.concatenate([p[:, None] for p in (x[:, 0], b, c, d)], 1).reshape(EXPERTS, 8, HD)


def rows_from_chunks(buf_ref, out_ref):
    row = lax.broadcasted_iota(jnp.int32, (1, 8, HD), 1)

    def tile(j):
        pair = buf_ref[:, (j // 2) * 16 : (j // 2 + 1) * 16, :].astype(F32)
        return pair.reshape(EXPERTS, 2, 8, HD)[:, j % 2]

    for u in range(5):
        tiles = [tile(3 * u + v) for v in range(3)]
        for v in range(3):
            out_ref[:, cols(3 * u + v)] = close_up(tiles[v]).astype(BF16)
        r = [pltpu.roll(tiles[v], (2 + 2 * v) % 8, 1) for v in range(3)]
        extra = jnp.where(row < 2, r[0], jnp.where(row < 4, r[1], r[2]))
        out_ref[:, cols(15 + u)] = close_up(extra).astype(BF16)


def chunks_from_rows(in_ref, emit):
    row = lax.broadcasted_iota(jnp.int32, (1, 8, HD), 1)
    before = None
    for u in range(5):
        last = spread(in_ref[:, cols(15 + u)])
        for v in range(3):
            j = 3 * u + v
            now = jnp.where(row < 6, spread(in_ref[:, cols(j)]), pltpu.roll(last, (6 - 2 * v) % 8, 1))
            if j % 2:
                emit(j // 2, jnp.concatenate([before, now], 1).astype(BF16))
            before = now
    emit(7, jnp.concatenate([before, jnp.zeros_like(before)], 1).astype(BF16))


def dispatch(place_ref, x_ref, rows_ref, out_ref):
    for c in range(5):
        at = slice(c * 512, (c + 1) * 512)
        rows_ref[:, at] = dot(place_ref[...], x_ref[:, at])

    def emit(t, pair):
        out_ref[:, t * 16 : (t + 1) * 16, :] = pair

    chunks_from_rows(rows_ref, emit)


def send_grads_kernel(place_ref, grad_ref, out_ref, rows_ref):
    dispatch(place_ref, grad_ref, rows_ref, out_ref)


def send_grads(place, grad):
    return pl.pallas_call(
        send_grads_kernel,
        out_shape=shape(EXPERTS, CHUNK, HD),
        scratch_shapes=[pltpu.VMEM((EXPERTS * SLOTS, WIDTH), F32)],
        compiler_params=params(32),
        name="send_grads",
    )(*hbm(place, grad))


def norm_kernel(place_ref, att_ref, stream_ref, gain_ref, mixed_ref, out_ref, routed_ref, rows_ref):
    for dev in range(NB):
        heads, shared, odd = owned(dev)
        for i, h in enumerate(heads):
            att = att_ref[dev, i * HD : (i + 1) * HD, :].astype(F32)
            mixed_ref[:, cols(h)] = (stream_ref[:, cols(h)].astype(F32) + att).astype(BF16)
        half = slice(64 * odd, 64 * odd + 64)
        att = att_ref[dev, 256:320, :].astype(F32)
        mixed_ref[half, cols(shared)] = (stream_ref[half, cols(shared)].astype(F32) + att).astype(BF16)
    mixed = mixed_ref[...].astype(F32)
    rstd = lax.rsqrt(jnp.mean(mixed * mixed, -1, keepdims=True) + 1e-06)
    routed_ref[...] = (mixed * rstd * gain_ref[...]).astype(BF16)
    dispatch(place_ref, routed_ref, rows_ref, out_ref)


def norm_and_send(place, att, stream, gain):
    return pl.pallas_call(
        norm_kernel,
        out_shape=[shape(TOK, WIDTH), shape(EXPERTS, CHUNK, HD)],
        scratch_shapes=[pltpu.VMEM((TOK, WIDTH), BF16), pltpu.VMEM((EXPERTS * SLOTS, WIDTH), F32)],
        compiler_params=params(40),
        name="norm_and_send",
    )(*hbm(place, att, stream), gain)


def grad_rows_kernel(buf_ref, w_down_ref, rows_ref, t_ref):
    rows_from_chunks(buf_ref, rows_ref)
    for n in range(2):
        half = slice(n * 256, (n + 1) * 256)
        t_ref[:, half] = lax.dot_general(rows_ref[...], w_down_ref[half, :], NT, preferred_element_type=F32)


def grad_rows(buf, w_down):
    rows = EXPERTS * SLOTS
    return pl.pallas_call(
        grad_rows_kernel,
        out_shape=[shape(rows, WIDTH), shape(rows, HIDDEN, dtype=F32)],
        compiler_params=params(32),
        cost_estimate=pl.CostEstimate(flops=2 * rows * WIDTH * HIDDEN, bytes_accessed=8 * MIB, transcendentals=0),
        name="grad_rows",
    )(*hbm(buf, w_down))


def expert_kernel(buf_ref, t_ref, w_gate_ref, w_up_ref, router_ref, gain_ref, sums_in_ref, *refs):
    *held, sums_ref = refs[:6]
    rows_ref, d_a_ref, d_b_ref, hidden_ref, back_ref, part_ref, sem = refs[6:]
    kept = (rows_ref, d_a_ref, d_b_ref, hidden_ref)
    copies = [pltpu.make_async_copy(x, y, sem.at[i]) for i, (x, y) in enumerate(zip(kept, held))]
    rows_from_chunks(buf_ref, rows_ref)
    copies[0].start()
    logit = lax.dot_general(rows_ref[...], router_ref[...], NT, preferred_element_type=F32)[:, 0:1]
    sig = jax.nn.sigmoid(logit)
    gate = sig.astype(BF16).astype(F32)
    score = None
    for n in range(2):
        half = slice(n * 256, (n + 1) * 256)
        a_val = dot(rows_ref[...], w_gate_ref[:, half])
        b_val = dot(rows_ref[...], w_up_ref[:, half])
        t_val = t_ref[:, half]
        sg = jax.nn.sigmoid(a_val)
        silu = a_val * sg
        hidden = (silu * b_val).astype(BF16).astype(F32)
        term = jnp.sum(hidden * t_val, -1, keepdims=True)
        score = term if score is None else score + term
        d_hidden = gate * t_val
        d_a_ref[:, half] = (d_hidden * b_val * sg * (1.0 + a_val * (1.0 - sg))).astype(BF16)
        d_b_ref[:, half] = (d_hidden * silu).astype(BF16)
        hidden_ref[:, half] = (gate * hidden).astype(BF16)
    for copy in copies[1:]:
        copy.start()
    d_logit = score.astype(BF16).astype(F32) * sig * (1.0 - sig)
    for c in range(5):
        at = slice(c * 512, (c + 1) * 512)
        part = (
            lax.dot_general(d_a_ref[...], w_gate_ref[at, :], NT, preferred_element_type=F32)
            + lax.dot_general(d_b_ref[...], w_up_ref[at, :], NT, preferred_element_type=F32)
            + d_logit * router_ref[0:1, at].astype(F32)
        )
        part_ref[:, at] = part
        rows = rows_ref[:, at].astype(F32)
        sums_ref[0:1, at] = sums_in_ref[0:1, at] + jnp.sum(d_logit * rows, 0, keepdims=True)
        sums_ref[1:2, at] = sums_in_ref[1:2, at] + jnp.sum(part * rows, 0, keepdims=True) / gain_ref[:, at]

    def emit(t, pair):
        at = slice(t * 16, (t + 1) * 16)
        back_ref[:, at, :] = pair
        copies.append(pltpu.make_async_copy(back_ref.at[:, at, :], held[4].at[:, at, :], sem.at[4 + t]))
        copies[-1].start()

    chunks_from_rows(part_ref, emit)
    for copy in copies:
        copy.wait()


def expert_rows(buf, t_val, w_gate, w_up, router, gain, sums):
    rows = EXPERTS * SLOTS
    return pl.pallas_call(
        expert_kernel,
        out_specs=[pl.BlockSpec(memory_space=pltpu.HBM)] * 5 + [pl.BlockSpec(memory_space=pltpu.VMEM)],
        out_shape=[
            shape(rows, WIDTH),
            shape(rows, HIDDEN),
            shape(rows, HIDDEN),
            shape(rows, HIDDEN),
            shape(EXPERTS, CHUNK, HD),
            jax.ShapeDtypeStruct((2, WIDTH), F32),
        ],
        scratch_shapes=[
            pltpu.VMEM((rows, WIDTH), BF16),
            pltpu.VMEM((rows, HIDDEN), BF16),
            pltpu.VMEM((rows, HIDDEN), BF16),
            pltpu.VMEM((rows, HIDDEN), BF16),
            pltpu.VMEM((EXPERTS, CHUNK, HD), BF16),
            pltpu.VMEM((rows, WIDTH), F32),
            pltpu.SemaphoreType.DMA((12,)),
        ],
        compiler_params=params(36),
        cost_estimate=pl.CostEstimate(flops=8 * rows * WIDTH * HIDDEN, bytes_accessed=16 * MIB, transcendentals=0),
        name="expert_rows",
    )(*hbm(buf, t_val), *vmem(w_gate, w_up), router, gain, sums)


def weight_grads_kernel(ra, rb, ga, gb, daa, dab, dba, dbb, ha, hb, gate_ref, up_ref, down_ref):
    def product(first, second):
        terms = [lax.dot_general(x[...], y[...], TN, preferred_element_type=F32) for x, y in (first, second)]
        return (terms[0] + terms[1]).astype(BF16)

    gate_ref[...] = product((ra, daa), (rb, dab))
    up_ref[...] = product((ra, dba), (rb, dbb))
    down_ref[...] = product((ha, ga), (hb, gb))


def weight_grads(first, second, grads):
    rows = EXPERTS * SLOTS
    wide = pl.BlockSpec((rows, 512), lambda i: (0, i))
    whole = pl.BlockSpec((rows, HIDDEN), lambda i: (0, 0))
    down = pl.BlockSpec((512, HIDDEN), lambda i: (i, 0))
    return pl.pallas_call(
        weight_grads_kernel,
        grid=(WIDTH // 512,),
        in_specs=[wide] * 4 + [whole] * 6,
        out_specs=[down, down, pl.BlockSpec((HIDDEN, 512), lambda i: (0, i))],
        out_shape=[shape(WIDTH, HIDDEN), shape(WIDTH, HIDDEN), shape(HIDDEN, WIDTH)],
        compiler_params=params(32),
        cost_estimate=pl.CostEstimate(flops=12 * rows * WIDTH * HIDDEN, bytes_accessed=20 * MIB, transcendentals=0),
        name="weight_grads",
    )(*hbm(first[0], second[0], grads[0], grads[1], first[1], second[1], first[2], second[2], first[3], second[3]))


def add_back_kernel(mine_ref, other_ref, sums_ref, out_ref):
    for t in range(8):
        at = slice(t * 16, (t + 1) * 16)
        total = mine_ref[:, at, :].astype(F32) + other_ref[:, at, :].astype(F32)
        if t == 7:
            top = jnp.concatenate([jnp.zeros((8, HD), F32), sums_ref[0:8, :]], 0)
            total = total + top[None]
        out_ref[:, at, :] = total.astype(BF16)
    out_ref[:, 128:160, :] = jnp.broadcast_to(sums_ref[8:40, :].astype(BF16)[None], (GROUP, 32, HD))


def add_back(mine, other, sums):
    block = pl.BlockSpec((GROUP, CHUNK, HD), lambda g: (g, 0, 0))
    return pl.pallas_call(
        add_back_kernel,
        grid=(EXPERTS // GROUP,),
        in_specs=[block, block, pl.BlockSpec((40, HD), lambda g: (0, 0))],
        out_specs=pl.BlockSpec((GROUP, BACK, HD), lambda g: (g, 0, 0)),
        out_shape=shape(EXPERTS, BACK, HD),
        compiler_params=params(16),
        name="add_back",
    )(*hbm(mine, other), sums)


def combine_kernel(place_ref, back_ref, mixed_ref, grad_ref, gain_ref, stream_ref, out_ref, rows_ref, d_ref):
    rows_from_chunks(back_ref, rows_ref)
    for c in range(5):
        at = slice(c * 512, (c + 1) * 512)
        d_ref[:, at] = lax.dot_general(place_ref[...], rows_ref[:, at], TN, preferred_element_type=F32)
    mixed = mixed_ref[...].astype(F32)
    rstd = lax.rsqrt(jnp.mean(mixed * mixed, -1, keepdims=True) + 1e-06)
    normed = mixed * rstd
    g = d_ref[...] * gain_ref[...]
    inner = jnp.mean(g * normed, -1, keepdims=True)
    stream_ref[...] = (grad_ref[...].astype(F32) + rstd * (g - normed * inner)).astype(BF16)
    for dev in range(NB):
        heads, shared, odd = owned(dev)
        for i, h in enumerate(heads):
            out_ref[dev, i * HD : (i + 1) * HD, :] = stream_ref[:, cols(h)]
        out_ref[dev, 256:320, :] = stream_ref[64 * odd : 64 * odd + 64, cols(shared)]


def combine(place, back, mixed, grad, gain):
    return pl.pallas_call(
        combine_kernel,
        out_shape=[shape(TOK, WIDTH), shape(NB, QROWS, HD)],
        scratch_shapes=[pltpu.VMEM((EXPERTS * SLOTS, WIDTH), BF16), pltpu.VMEM((TOK, WIDTH), F32)],
        compiler_params=params(40),
        name="combine",
    )(*hbm(place, back, mixed, grad), gain)


def swap_cores(x):
    return lax.ppermute(x, "core", [(0, 1), (1, 0)])


def over_outer(x):
    return lax.all_to_all(x, "outer", split_axis=0, concat_axis=0, tiled=True)


def over_chips(x):
    return lax.all_to_all(x, ("outer", "chip"), split_axis=0, concat_axis=0, tiled=True)


def body(
    stream_in,
    queries,
    key_rows,
    value_rows,
    segment_ids,
    norm_gain,
    router_w,
    expert_ids,
    gate_w,
    up_w,
    down_w,
    out_grad,
):
    at = lax.axis_index("outer")
    split = jnp.sum((segment_ids[0] == 0).astype(jnp.int32))
    info = jnp.stack([split, at % 2]).astype(jnp.int32)
    gain = norm_gain.reshape(1, WIDTH)
    grads_local = out_grad[0]

    together = lax.optimization_barrier
    qkv = over_outer(pack_heads(queries[0], key_rows[0], value_rows[0]))
    place = place_rows(expert_ids[0].T)
    qkv, grads_buf = together((qkv, send_grads(place, grads_local)))
    grads_mine = over_chips(grads_buf)
    att, lse = attention(info, qkv)
    att, grads_mine = together((att, grads_mine))
    grads_other = swap_cores(grads_mine)
    att_back = over_outer(att)
    mixed, rows_buf = norm_and_send(place, att_back, stream_in[0], gain)
    rows_mine = over_chips(rows_buf)

    expert = at * 8 + lax.axis_index("chip")
    router = jnp.broadcast_to(lax.dynamic_slice_in_dim(router_w.T, expert, 1, 0), (8, WIDTH))
    w_gate, w_up, w_down = gate_w[0], up_w[0], down_w[0]
    grads_first = grad_rows(grads_mine, w_down)
    grads_second = grad_rows(grads_other, w_down)
    rows_mine, grads_first, grads_second, router = together((rows_mine, grads_first, grads_second, router))
    rows_other = swap_cores(rows_mine)
    nothing = jnp.zeros((2, WIDTH), F32)
    *first, back_mine, sums = expert_rows(rows_mine, grads_first[1], w_gate, w_up, router, gain, nothing)
    *second, back_other, sums = expert_rows(rows_other, grads_second[1], w_gate, w_up, router, gain, sums)
    sums = sums.reshape(40, HD)
    sums = sums + swap_cores(sums)
    back = over_chips(add_back(back_mine, swap_cores(back_other), sums))
    gate_grad, up_grad, down_grad = weight_grads(first, second, (grads_first[0], grads_second[0]))
    back, gate_grad, up_grad, down_grad = together((back, gate_grad, up_grad, down_grad))

    stream_grad, grad_heads = combine(place, back, mixed, grads_local, gain)
    router_grad = back[:, 120:140, :].reshape(EXPERTS, WIDTH).T.astype(F32)
    gain_grad = jnp.sum(back[:, 140:160, :].astype(F32), 0).reshape(WIDTH)
    grad_in = over_outer(grad_heads)
    grads_out = over_outer(attention_grad(info, qkv, grad_in, att, lse))
    query_grad, key_grad, value_grad = unpack_grads(grads_out)
    return (
        stream_grad[None],
        query_grad[None],
        key_grad[None],
        value_grad[None],
        gain_grad,
        router_grad,
        gate_grad[None],
        up_grad[None],
        down_grad[None],
    )


def solution(mesh):
    chips = Mesh(mesh.devices.reshape(8, 8, 2), ("outer", "chip", "core"))
    inner = ("chip", "core")
    every = ("outer", "chip", "core")
    frames = P(inner, "outer", None)
    pieces = P(every, None, None)
    placed = (
        frames,
        frames,
        frames,
        frames,
        P(inner, None),
        P(),
        P(),
        frames,
        pieces,
        pieces,
        pieces,
        frames,
    )
    return jax.shard_map(
        body,
        mesh=chips,
        in_specs=placed,
        out_specs=(frames, frames, frames, frames, P(), P(), pieces, pieces, pieces),
        check_vma=False,
    )
```

```python
import jax
import jax.numpy as jnp
from jax import lax
from jax.experimental import pallas as pl
from jax.experimental.pallas import tpu as pltpu
from jax.sharding import Mesh, PartitionSpec as P

F32 = jnp.float32
BF16 = jnp.bfloat16
HEADS = 20
HD = 128
NB = 8
TOK = 128
LEN = 1024
WIDTH = 2560
EXPERTS = 64
HIDDEN = 512
SLOTS = 6
QROWS = 320
KVROWS = 384
CHUNK = 128
BACK = 160
SCALE = HD**-0.5
SCALE2 = SCALE * 1.4426950408889634
NT = (((1,), (1,)), ((), ()))
TN = (((0,), (0,)), ((), ()))
MIB = 1 << 20


def params(mib):
    return pltpu.CompilerParams(vmem_limit_bytes=mib * MIB)


def shape(*dims, dtype=BF16):
    return pltpu.HBM(dims, dtype)


def hbm(*arrays):
    return [pltpu.with_memory_space_constraint(x, pltpu.HBM) for x in arrays]


def vmem(*arrays):
    return [pltpu.with_memory_space_constraint(x, pltpu.VMEM) for x in arrays]


class Copies:
    def __init__(self, sem):
        self.sem, self.started = sem, []

    def start(self, source, target):
        copy = pltpu.make_async_copy(source, target, self.sem.at[len(self.started)])
        copy.start()
        self.started.append(copy)
        return copy

    def wait(self):
        for copy in self.started:
            copy.wait()


IN_HBM = pl.BlockSpec(memory_space=pltpu.HBM)
IN_VMEM = pl.BlockSpec(memory_space=pltpu.VMEM)


def sems(count):
    return pltpu.SemaphoreType.DMA((count,))


def dot(a, b):
    return jnp.dot(a, b, preferred_element_type=F32)


def owned(dev):
    pair, odd = dev // 2, dev % 2
    return (5 * pair + 3 * odd, 5 * pair + 3 * odd + 1), 5 * pair + 2, odd


def cols(index):
    return slice(index * HD, (index + 1) * HD)


def pack_heads_kernel(q_hbm, k_hbm, v_hbm, out_hbm, q_ref, k_ref, v_ref, out_ref, in_sem, out_sem):
    sides = ((q_hbm, q_ref), (k_hbm, k_ref), (v_hbm, v_ref))
    at = [pl.ds(5 * HD * p, 5 * HD) for p in range(4)]
    arriving = Copies(in_sem)
    waits = [[arriving.start(x.at[:, at[p]], y.at[:, at[p]]) for x, y in sides] for p in range(4)]
    leaving = Copies(out_sem)
    for p in range(4):
        for copy in waits[p]:
            copy.wait()
        for dev in (2 * p, 2 * p + 1):
            heads, shared, odd = owned(dev)
            for i, h in enumerate(heads):
                out_ref[dev, i * HD : (i + 1) * HD, :] = q_ref[:, cols(h)]
            out_ref[dev, 256:320, :] = q_ref[64 * odd : 64 * odd + 64, cols(shared)]
            for base, ref in ((QROWS, k_ref), (QROWS + KVROWS, v_ref)):
                for i, h in enumerate(heads + (shared,)):
                    out_ref[dev, base + i * HD : base + (i + 1) * HD, :] = ref[:, cols(h)]
        both = pl.ds(2 * p, 2)
        leaving.start(out_ref.at[both], out_hbm.at[both])
    leaving.wait()


def pack_heads(q, k, v):
    rows = QROWS + 2 * KVROWS
    return pl.pallas_call(
        pack_heads_kernel,
        in_specs=[IN_HBM] * 3,
        out_specs=IN_HBM,
        out_shape=shape(NB, rows, HD),
        scratch_shapes=[pltpu.VMEM((TOK, WIDTH), BF16)] * 3 + [pltpu.VMEM((NB, rows, HD), BF16), sems(12), sems(4)],
        compiler_params=params(16),
        name="pack_heads",
    )(*hbm(q, k, v))


def unpack_grads_kernel(in_ref, q_hbm, k_hbm, v_hbm, q_ref, k_ref, v_ref, sem):
    leaving = Copies(sem)
    for p in range(4):
        for dev in (2 * p, 2 * p + 1):
            heads, shared, odd = owned(dev)
            for i, h in enumerate(heads):
                q_ref[:, cols(h)] = in_ref[dev, i * HD : (i + 1) * HD, :]
            q_ref[64 * odd : 64 * odd + 64, cols(shared)] = in_ref[dev, 256:320, :]
            for base, ref in ((QROWS, k_ref), (QROWS + KVROWS, v_ref)):
                for i, h in enumerate(heads):
                    ref[:, cols(h)] = in_ref[dev, base + i * HD : base + (i + 1) * HD, :]
        for base, ref in ((QROWS, k_ref), (QROWS + KVROWS, v_ref)):
            halves = [in_ref[2 * p + odd, base + 256 : base + 384, :].astype(F32) for odd in range(2)]
            ref[:, cols(5 * p + 2)] = (halves[0] + halves[1]).astype(BF16)
        at = pl.ds(5 * HD * p, 5 * HD)
        for x, y in ((q_ref, q_hbm), (k_ref, k_hbm), (v_ref, v_hbm)):
            leaving.start(x.at[:, at], y.at[:, at])
    leaving.wait()


def unpack_grads(buf):
    return pl.pallas_call(
        unpack_grads_kernel,
        in_specs=[IN_VMEM],
        out_specs=[IN_HBM] * 3,
        out_shape=[shape(TOK, WIDTH)] * 3,
        scratch_shapes=[pltpu.VMEM((TOK, WIDTH), BF16)] * 3 + [sems(12)],
        compiler_params=params(16),
        name="unpack_grads",
    )(buf)


def query_tiles():
    tiles = [(hi, slice(2 * t, 2 * t + 2), slice(hi * HD, (hi + 1) * HD), t) for hi in range(2) for t in range(4)]
    return tiles + [(2, slice(4 * t, 4 * t + 4), slice(256, 320), t) for t in range(2)]


def same_segment(hi, t, split, odd, keys_seg):
    lane = lax.broadcasted_iota(jnp.int32, (1, 256), 1)
    if hi < 2:
        frame = 256 * t + lane
    else:
        frame = 512 * t + (lane >> 6) * 128 + odd * 64 + (lane & 63)
    return keys_seg == (frame >= split).astype(jnp.int32)


def attention_kernel(info_ref, buf_ref, o_ref, lse_ref):
    split, odd = info_ref[0], info_ref[1]
    keys_seg = (lax.broadcasted_iota(jnp.int32, (LEN, 1), 0) >= split).astype(jnp.int32)
    held = None
    for number, (hi, blocks, rows, t) in enumerate(query_tiles()):
        if hi != held:
            held = hi
            k = buf_ref[:, QROWS + hi * HD : QROWS + (hi + 1) * HD, :].reshape(LEN, HD)
            v = buf_ref[:, QROWS + KVROWS + hi * HD : QROWS + KVROWS + (hi + 1) * HD, :].reshape(LEN, HD)
            v_t = v.astype(F32).T.astype(BF16)
        q = buf_ref[blocks, rows, :].reshape(256, HD)
        scores = lax.dot_general(k, q, NT, preferred_element_type=F32) * SCALE2
        scores = jnp.where(same_segment(hi, t, split, odd, keys_seg), scores, -1e30)
        top = jnp.max(scores, 0, keepdims=True)
        e = jnp.exp2(scores - top)
        total = jnp.sum(e, 0, keepdims=True)
        out = dot(v_t, e.astype(BF16)) / total
        o_ref[blocks, rows, :] = out.T.astype(BF16).reshape(o_ref[blocks, rows, :].shape)
        lse_ref[number] = jnp.broadcast_to(top + jnp.log2(total), (8, 256))


def attention(info, buf):
    return pl.pallas_call(
        attention_kernel,
        in_specs=[pl.BlockSpec(memory_space=pltpu.SMEM), pl.BlockSpec(memory_space=pltpu.VMEM)],
        out_specs=[pl.BlockSpec(memory_space=pltpu.VMEM)] * 2,
        out_shape=[
            shape(NB, QROWS, HD),
            shape(10, 8, 256, dtype=F32),
        ],
        compiler_params=params(40),
        name="attention",
    )(info, buf)


def attention_grad_kernel(info_ref, buf_ref, do_ref, o_ref, lse_ref, out_hbm, out_ref, sem):
    leaving = Copies(sem)

    split, odd = info_ref[0], info_ref[1]
    keys_seg = (lax.broadcasted_iota(jnp.int32, (LEN, 1), 0) >= split).astype(jnp.int32)
    held = None
    sums = None

    def flush(hi):
        at = QROWS + hi * HD
        out_ref[:, at : at + HD, :] = (sums[0] * SCALE).astype(BF16).reshape(NB, TOK, HD)
        at = at + KVROWS
        out_ref[:, at : at + HD, :] = sums[1].astype(BF16).reshape(NB, TOK, HD)
        parts = [(hi * HD, HD if hi < 2 else 64), (QROWS + hi * HD, HD), (QROWS + KVROWS + hi * HD, HD)]
        for start, size in parts:
            leaving.start(out_ref.at[:, pl.ds(start, size), :], out_hbm.at[:, pl.ds(start, size), :])

    for number, (hi, blocks, rows, t) in enumerate(query_tiles()):
        if hi != held:
            if held is not None:
                flush(held)
            held = hi
            sums = None
            k = buf_ref[:, QROWS + hi * HD : QROWS + (hi + 1) * HD, :].reshape(LEN, HD)
            v = buf_ref[:, QROWS + KVROWS + hi * HD : QROWS + KVROWS + (hi + 1) * HD, :].reshape(LEN, HD)
            k_t = k.astype(F32).T.astype(BF16)
        q = buf_ref[blocks, rows, :].reshape(256, HD)
        grad = do_ref[blocks, rows, :].reshape(256, HD)
        out = o_ref[blocks, rows, :].reshape(256, HD)
        delta = jnp.sum((grad.astype(F32) * out.astype(F32)).T, 0, keepdims=True)
        scores = lax.dot_general(k, q, NT, preferred_element_type=F32) * SCALE2
        scores = jnp.where(same_segment(hi, t, split, odd, keys_seg), scores, -1e30)
        probs = jnp.exp2(scores - lse_ref[number, 0:1, :])
        d_probs = lax.dot_general(v, grad, NT, preferred_element_type=F32)
        d_scores = (probs * (d_probs - delta)).astype(BF16)
        terms = (dot(d_scores, q), dot(probs.astype(BF16), grad))
        sums = terms if sums is None else (sums[0] + terms[0], sums[1] + terms[1])
        d_q = (dot(k_t, d_scores) * SCALE).T.astype(BF16)
        out_ref[blocks, rows, :] = d_q.reshape(out_ref[blocks, rows, :].shape)
    flush(held)
    leaving.wait()


def attention_grad(info, buf, grad, out, lse):
    rows = QROWS + 2 * KVROWS
    return pl.pallas_call(
        attention_grad_kernel,
        in_specs=[pl.BlockSpec(memory_space=pltpu.SMEM)] + [IN_VMEM] * 4,
        out_specs=IN_HBM,
        out_shape=shape(NB, rows, HD),
        scratch_shapes=[pltpu.VMEM((NB, rows, HD), BF16), sems(9)],
        compiler_params=params(40),
        name="attention_grad",
    )(info, buf, grad, *hbm(out, lse))


def place_kernel(ids_ref, out_ref):
    expert = lax.broadcasted_iota(jnp.int32, (EXPERTS, TOK), 0)
    chosen = ((ids_ref[0:1, :] == expert) | (ids_ref[1:2, :] == expert)).astype(F32)
    before = lax.broadcasted_iota(jnp.int32, (TOK, TOK), 0) < lax.broadcasted_iota(jnp.int32, (TOK, TOK), 1)
    slot = dot(chosen.astype(BF16), before.astype(BF16))
    slot = jnp.where(chosen > 0.5, slot, -100.0).astype(jnp.int32)
    slot = slot.reshape(EXPERTS, 1, TOK)
    row = lax.broadcasted_iota(jnp.int32, (EXPERTS, 8, TOK), 1)
    out_ref[...] = close_up((slot == row).astype(F32)).astype(BF16)


def place_rows(ids):
    return pl.pallas_call(
        place_kernel,
        out_shape=shape(EXPERTS * SLOTS, TOK),
        compiler_params=params(24),
        name="place_rows",
    )(ids)


def close_up(x):
    row = lax.broadcasted_iota(jnp.int32, (1, 8, HD), 1)
    x = x.reshape(16, 4, 8, HD)
    b, c, d = pltpu.roll(x[:, 1], 6, 1), pltpu.roll(x[:, 2], 4, 1), pltpu.roll(x[:, 3], 2, 1)
    parts = (jnp.where(row < 6, x[:, 0], b), jnp.where(row < 4, b, c), jnp.where(row < 2, c, d))
    return jnp.concatenate([p[:, None] for p in parts], 1).reshape(EXPERTS * SLOTS, HD)


def spread(x):
    row = lax.broadcasted_iota(jnp.int32, (1, 8, HD), 1)
    x = x.reshape(16, 3, 8, HD)
    b = pltpu.roll(jnp.where(row >= 6, x[:, 0], x[:, 1]), 2, 1)
    c = pltpu.roll(jnp.where(row >= 4, x[:, 1], x[:, 2]), 4, 1)
    d = pltpu.roll(x[:, 2], 6, 1)
    return jnp.concatenate([p[:, None] for p in (x[:, 0], b, c, d)], 1).reshape(EXPERTS, 8, HD)


def rows_from_chunks(buf_ref, out_ref):
    row = lax.broadcasted_iota(jnp.int32, (1, 8, HD), 1)

    def tile(j):
        pair = buf_ref[:, (j // 2) * 16 : (j // 2 + 1) * 16, :].astype(F32)
        return pair.reshape(EXPERTS, 2, 8, HD)[:, j % 2]

    for u in range(5):
        tiles = [tile(3 * u + v) for v in range(3)]
        for v in range(3):
            out_ref[:, cols(3 * u + v)] = close_up(tiles[v]).astype(BF16)
        r = [pltpu.roll(tiles[v], (2 + 2 * v) % 8, 1) for v in range(3)]
        extra = jnp.where(row < 2, r[0], jnp.where(row < 4, r[1], r[2]))
        out_ref[:, cols(15 + u)] = close_up(extra).astype(BF16)


def chunks_from_rows(in_ref, emit):
    row = lax.broadcasted_iota(jnp.int32, (1, 8, HD), 1)
    before = None
    for u in range(5):
        last = spread(in_ref[:, cols(15 + u)])
        for v in range(3):
            j = 3 * u + v
            now = jnp.where(row < 6, spread(in_ref[:, cols(j)]), pltpu.roll(last, (6 - 2 * v) % 8, 1))
            if j % 2:
                emit(j // 2, jnp.concatenate([before, now], 1).astype(BF16))
            before = now
    emit(7, jnp.concatenate([before, jnp.zeros_like(before)], 1).astype(BF16))


def dispatch(place_ref, x_ref, rows_ref, out_ref, out_hbm, leaving):
    for c in range(5):
        at = slice(c * 512, (c + 1) * 512)
        rows_ref[:, at] = dot(place_ref[...], x_ref[:, at])

    def emit(t, pair):
        at = pl.ds(t * 16, 16)
        out_ref[:, at, :] = pair
        leaving.start(out_ref.at[:, at, :], out_hbm.at[:, at, :])

    chunks_from_rows(rows_ref, emit)
    leaving.wait()


def send_grads_kernel(place_ref, grad_ref, out_hbm, rows_ref, out_ref, sem):
    dispatch(place_ref, grad_ref, rows_ref, out_ref, out_hbm, Copies(sem))


def send_grads(place, grad):
    return pl.pallas_call(
        send_grads_kernel,
        out_specs=IN_HBM,
        out_shape=shape(EXPERTS, CHUNK, HD),
        scratch_shapes=[
            pltpu.VMEM((EXPERTS * SLOTS, WIDTH), F32),
            pltpu.VMEM((EXPERTS, CHUNK, HD), BF16),
            sems(8),
        ],
        compiler_params=params(24),
        name="send_grads",
    )(place, *hbm(grad))


def norm_kernel(place_ref, att_ref, stream_ref, gain_ref, mixed_hbm, out_hbm, mixed_ref, routed_ref, rows_ref, out_ref, sem):
    leaving = Copies(sem)
    for dev in range(NB):
        heads, shared, odd = owned(dev)
        for i, h in enumerate(heads):
            att = att_ref[dev, i * HD : (i + 1) * HD, :].astype(F32)
            mixed_ref[:, cols(h)] = (stream_ref[:, cols(h)].astype(F32) + att).astype(BF16)
        half = slice(64 * odd, 64 * odd + 64)
        att = att_ref[dev, 256:320, :].astype(F32)
        mixed_ref[half, cols(shared)] = (stream_ref[half, cols(shared)].astype(F32) + att).astype(BF16)
    leaving.start(mixed_ref, mixed_hbm)
    mixed = mixed_ref[...].astype(F32)
    rstd = lax.rsqrt(jnp.mean(mixed * mixed, -1, keepdims=True) + 1e-06)
    routed_ref[...] = (mixed * rstd * gain_ref[...]).astype(BF16)
    dispatch(place_ref, routed_ref, rows_ref, out_ref, out_hbm, leaving)


def norm_and_send(place, att, stream, gain):
    return pl.pallas_call(
        norm_kernel,
        out_specs=[IN_HBM] * 2,
        out_shape=[shape(TOK, WIDTH), shape(EXPERTS, CHUNK, HD)],
        scratch_shapes=[
            pltpu.VMEM((TOK, WIDTH), BF16),
            pltpu.VMEM((TOK, WIDTH), BF16),
            pltpu.VMEM((EXPERTS * SLOTS, WIDTH), F32),
            pltpu.VMEM((EXPERTS, CHUNK, HD), BF16),
            sems(9),
        ],
        compiler_params=params(24),
        name="norm_and_send",
    )(place, att, *hbm(stream), gain)


def grad_rows_kernel(buf_ref, w_down_ref, rows_ref, t_ref):
    rows_from_chunks(buf_ref, rows_ref)
    for n in range(2):
        half = slice(n * 256, (n + 1) * 256)
        t_ref[:, half] = lax.dot_general(rows_ref[...], w_down_ref[half, :], NT, preferred_element_type=F32)


def grad_rows(buf, w_down):
    rows = EXPERTS * SLOTS
    return pl.pallas_call(
        grad_rows_kernel,
        out_shape=[shape(rows, WIDTH), shape(rows, HIDDEN, dtype=F32)],
        compiler_params=params(32),
        cost_estimate=pl.CostEstimate(flops=2 * rows * WIDTH * HIDDEN, bytes_accessed=8 * MIB, transcendentals=0),
        name="grad_rows",
    )(buf, *hbm(w_down))


def expert_kernel(buf_ref, t_ref, w_gate_ref, w_up_hbm, router_ref, gain_ref, sums_in_ref, *refs):
    *held, sums_ref = refs[:6]
    rows_ref, d_a_ref, d_b_ref, hidden_ref, back_ref, part_ref, w_up_ref, sem, in_sem = refs[6:]
    w_up_copy = Copies(in_sem).start(w_up_hbm, w_up_ref)
    leaving = Copies(sem)
    rows_from_chunks(buf_ref, rows_ref)
    leaving.start(rows_ref, held[0])
    w_up_copy.wait()
    logit = lax.dot_general(rows_ref[...], router_ref[...], NT, preferred_element_type=F32)[:, 0:1]
    sig = jax.nn.sigmoid(logit)
    gate = sig.astype(BF16).astype(F32)
    score = None
    for n in range(2):
        half = slice(n * 256, (n + 1) * 256)
        a_val = dot(rows_ref[...], w_gate_ref[:, half])
        b_val = dot(rows_ref[...], w_up_ref[:, half])
        t_val = t_ref[:, half]
        sg = jax.nn.sigmoid(a_val)
        silu = a_val * sg
        hidden = (silu * b_val).astype(BF16).astype(F32)
        term = jnp.sum(hidden * t_val, -1, keepdims=True)
        score = term if score is None else score + term
        d_hidden = gate * t_val
        d_a_ref[:, half] = (d_hidden * b_val * sg * (1.0 + a_val * (1.0 - sg))).astype(BF16)
        d_b_ref[:, half] = (d_hidden * silu).astype(BF16)
        hidden_ref[:, half] = (gate * hidden).astype(BF16)
    for ref, target in zip((d_a_ref, d_b_ref, hidden_ref), held[1:4]):
        leaving.start(ref, target)
    d_logit = score.astype(BF16).astype(F32) * sig * (1.0 - sig)
    for c in range(5):
        at = slice(c * 512, (c + 1) * 512)
        part = (
            lax.dot_general(d_a_ref[...], w_gate_ref[at, :], NT, preferred_element_type=F32)
            + lax.dot_general(d_b_ref[...], w_up_ref[at, :], NT, preferred_element_type=F32)
            + d_logit * router_ref[0:1, at].astype(F32)
        )
        part_ref[:, at] = part
        rows = rows_ref[:, at].astype(F32)
        sums_ref[0:1, at] = sums_in_ref[0:1, at] + jnp.sum(d_logit * rows, 0, keepdims=True)
        sums_ref[1:2, at] = sums_in_ref[1:2, at] + jnp.sum(part * rows, 0, keepdims=True) / gain_ref[:, at]

    def emit(t, pair):
        at = pl.ds(t * 16, 16)
        back_ref[:, at, :] = pair
        leaving.start(back_ref.at[:, at, :], held[4].at[:, at, :])

    chunks_from_rows(part_ref, emit)
    leaving.wait()


def expert_rows(buf, t_val, w_gate, w_up, router, gain, sums):
    rows = EXPERTS * SLOTS
    return pl.pallas_call(
        expert_kernel,
        in_specs=[IN_VMEM] * 3 + [IN_HBM] + [IN_VMEM] * 3,
        out_specs=[IN_HBM] * 5 + [IN_VMEM],
        out_shape=[
            shape(rows, WIDTH),
            shape(rows, HIDDEN),
            shape(rows, HIDDEN),
            shape(rows, HIDDEN),
            shape(EXPERTS, CHUNK, HD),
            jax.ShapeDtypeStruct((2, WIDTH), F32),
        ],
        scratch_shapes=[
            pltpu.VMEM((rows, WIDTH), BF16),
            pltpu.VMEM((rows, HIDDEN), BF16),
            pltpu.VMEM((rows, HIDDEN), BF16),
            pltpu.VMEM((rows, HIDDEN), BF16),
            pltpu.VMEM((EXPERTS, CHUNK, HD), BF16),
            pltpu.VMEM((rows, WIDTH), F32),
            pltpu.VMEM((WIDTH, HIDDEN), BF16),
            sems(12),
            sems(1),
        ],
        compiler_params=params(36),
        cost_estimate=pl.CostEstimate(flops=8 * rows * WIDTH * HIDDEN, bytes_accessed=16 * MIB, transcendentals=0),
        name="expert_rows",
    )(buf, t_val, *vmem(w_gate), *hbm(w_up), router, gain, sums)


def weight_grads_kernel(ra, rb, ga, gb, daa, dab, dba, dbb, ha, hb, gate_ref, up_ref, down_ref):
    def product(first, second):
        terms = [lax.dot_general(x[...], y[...], TN, preferred_element_type=F32) for x, y in (first, second)]
        return (terms[0] + terms[1]).astype(BF16)

    gate_ref[...] = product((ra, daa), (rb, dab))
    up_ref[...] = product((ra, dba), (rb, dbb))
    down_ref[...] = product((ha, ga), (hb, gb))


def weight_grads(first, second, grads):
    rows = EXPERTS * SLOTS
    wide = pl.BlockSpec((rows, 512), lambda i: (0, i))
    whole = pl.BlockSpec((rows, HIDDEN), lambda i: (0, 0))
    down = pl.BlockSpec((512, HIDDEN), lambda i: (i, 0))
    return pl.pallas_call(
        weight_grads_kernel,
        grid=(WIDTH // 512,),
        in_specs=[wide] * 4 + [whole] * 6,
        out_specs=[down, down, pl.BlockSpec((HIDDEN, 512), lambda i: (0, i))],
        out_shape=[shape(WIDTH, HIDDEN), shape(WIDTH, HIDDEN), shape(HIDDEN, WIDTH)],
        compiler_params=params(32),
        cost_estimate=pl.CostEstimate(flops=12 * rows * WIDTH * HIDDEN, bytes_accessed=20 * MIB, transcendentals=0),
        name="weight_grads",
    )(*hbm(first[0], second[0], grads[0], grads[1], first[1], second[1], first[2], second[2], first[3], second[3]))


def add_back_kernel(mine_hbm, other_ref, sums_ref, out_hbm, mine_ref, out_ref, in_sem, out_sem):
    arriving, leaving = Copies(in_sem), Copies(out_sem)
    at = [pl.ds(t * 16, 16) for t in range(10)]
    for t in range(8):
        arriving.start(mine_hbm.at[:, at[t], :], mine_ref.at[:, at[t], :])
    for t in (8, 9):
        rows = sums_ref[(t - 8) * 16 + 8 : (t - 8) * 16 + 24, :].astype(BF16)
        out_ref[:, at[t], :] = jnp.broadcast_to(rows[None], (EXPERTS, 16, HD))
        leaving.start(out_ref.at[:, at[t], :], out_hbm.at[:, at[t], :])
    for t in range(8):
        arriving.started[t].wait()
        total = mine_ref[:, at[t], :].astype(F32) + other_ref[:, at[t], :].astype(F32)
        if t == 7:
            top = jnp.concatenate([jnp.zeros((8, HD), F32), sums_ref[0:8, :]], 0)
            total = total + top[None]
        out_ref[:, at[t], :] = total.astype(BF16)
        leaving.start(out_ref.at[:, at[t], :], out_hbm.at[:, at[t], :])
    leaving.wait()


def add_back(mine, other, sums):
    return pl.pallas_call(
        add_back_kernel,
        in_specs=[IN_HBM, IN_VMEM, IN_VMEM],
        out_specs=IN_HBM,
        out_shape=shape(EXPERTS, BACK, HD),
        scratch_shapes=[
            pltpu.VMEM((EXPERTS, CHUNK, HD), BF16),
            pltpu.VMEM((EXPERTS, BACK, HD), BF16),
            sems(8),
            sems(10),
        ],
        compiler_params=params(16),
        name="add_back",
    )(*hbm(mine), other, sums)


def combine_kernel(place_ref, back_ref, mixed_ref, grad_ref, gain_ref, stream_hbm, out_ref, rows_ref, d_ref, stream_ref, sem):
    rows_from_chunks(back_ref, rows_ref)
    for c in range(5):
        at = slice(c * 512, (c + 1) * 512)
        d_ref[:, at] = lax.dot_general(place_ref[...], rows_ref[:, at], TN, preferred_element_type=F32)
    mixed = mixed_ref[...].astype(F32)
    rstd = lax.rsqrt(jnp.mean(mixed * mixed, -1, keepdims=True) + 1e-06)
    normed = mixed * rstd
    g = d_ref[...] * gain_ref[...]
    inner = jnp.mean(g * normed, -1, keepdims=True)
    stream_ref[...] = (grad_ref[...].astype(F32) + rstd * (g - normed * inner)).astype(BF16)
    leaving = Copies(sem)
    leaving.start(stream_ref, stream_hbm)
    for dev in range(NB):
        heads, shared, odd = owned(dev)
        for i, h in enumerate(heads):
            out_ref[dev, i * HD : (i + 1) * HD, :] = stream_ref[:, cols(h)]
        out_ref[dev, 256:320, :] = stream_ref[64 * odd : 64 * odd + 64, cols(shared)]
    leaving.wait()


def combine(place, back, mixed, grad, gain):
    return pl.pallas_call(
        combine_kernel,
        out_specs=[IN_HBM, IN_VMEM],
        out_shape=[shape(TOK, WIDTH), jax.ShapeDtypeStruct((NB, QROWS, HD), BF16)],
        scratch_shapes=[
            pltpu.VMEM((EXPERTS * SLOTS, WIDTH), BF16),
            pltpu.VMEM((TOK, WIDTH), F32),
            pltpu.VMEM((TOK, WIDTH), BF16),
            sems(1),
        ],
        compiler_params=params(24),
        name="combine",
    )(place, back, *hbm(mixed, grad), gain)


def swap_cores(x):
    return lax.ppermute(x, "core", [(0, 1), (1, 0)])


def over_outer(x):
    return lax.all_to_all(x, "outer", split_axis=0, concat_axis=0, tiled=True)


def over_chips(x):
    return lax.all_to_all(x, ("outer", "chip"), split_axis=0, concat_axis=0, tiled=True)


def body(
    stream_in,
    queries,
    key_rows,
    value_rows,
    segment_ids,
    norm_gain,
    router_w,
    expert_ids,
    gate_w,
    up_w,
    down_w,
    out_grad,
):
    at = lax.axis_index("outer")
    split = jnp.sum((segment_ids[0] == 0).astype(jnp.int32))
    info = jnp.stack([split, at % 2]).astype(jnp.int32)
    gain = norm_gain.reshape(1, WIDTH)
    grads_local = out_grad[0]

    together = lax.optimization_barrier
    qkv = over_outer(pack_heads(queries[0], key_rows[0], value_rows[0]))
    place = place_rows(expert_ids[0].T)
    qkv, grads_buf = together((qkv, send_grads(place, grads_local)))
    grads_mine = over_chips(grads_buf)
    att, lse = attention(info, qkv)
    att, grads_mine = together((att, grads_mine))
    grads_other = swap_cores(grads_mine)
    att_back = over_outer(att)
    mixed, rows_buf = norm_and_send(place, att_back, stream_in[0], gain)
    rows_mine = over_chips(rows_buf)

    expert = at * 8 + lax.axis_index("chip")
    router = jnp.broadcast_to(lax.dynamic_slice_in_dim(router_w.T, expert, 1, 0), (8, WIDTH))
    w_gate, w_up, w_down = gate_w[0], up_w[0], down_w[0]
    grads_first = grad_rows(grads_mine, w_down)
    grads_second = grad_rows(grads_other, w_down)
    rows_mine, grads_first, grads_second, router = together((rows_mine, grads_first, grads_second, router))
    rows_other = swap_cores(rows_mine)
    nothing = jnp.zeros((2, WIDTH), F32)
    *first, back_mine, sums = expert_rows(rows_mine, grads_first[1], w_gate, w_up, router, gain, nothing)
    *second, back_other, sums = expert_rows(rows_other, grads_second[1], w_gate, w_up, router, gain, sums)
    sums = sums.reshape(40, HD)
    sums = sums + swap_cores(sums)
    back = over_chips(add_back(back_mine, swap_cores(back_other), sums))
    gate_grad, up_grad, down_grad = weight_grads(first, second, (grads_first[0], grads_second[0]))
    back, gate_grad, up_grad, down_grad = together((back, gate_grad, up_grad, down_grad))

    stream_grad, grad_heads = combine(place, back, mixed, grads_local, gain)
    router_grad = back[:, 120:140, :].reshape(EXPERTS, WIDTH).T.astype(F32)
    gain_grad = jnp.sum(back[:, 140:160, :].astype(F32), 0).reshape(WIDTH)
    grad_in = over_outer(grad_heads)
    grads_out = over_outer(attention_grad(info, qkv, grad_in, att, lse))
    query_grad, key_grad, value_grad = unpack_grads(grads_out)
    return (
        stream_grad[None],
        query_grad[None],
        key_grad[None],
        value_grad[None],
        gain_grad,
        router_grad,
        gate_grad[None],
        up_grad[None],
        down_grad[None],
    )


def solution(mesh):
    chips = Mesh(mesh.devices.reshape(8, 8, 2), ("outer", "chip", "core"))
    inner = ("chip", "core")
    every = ("outer", "chip", "core")
    frames = P(inner, "outer", None)
    pieces = P(every, None, None)
    placed = (
        frames,
        frames,
        frames,
        frames,
        P(inner, None),
        P(),
        P(),
        frames,
        pieces,
        pieces,
        pieces,
        frames,
    )
    return jax.shard_map(
        body,
        mesh=chips,
        in_specs=placed,
        out_specs=(frames, frames, frames, frames, P(), P(), pieces, pieces, pieces),
        check_vma=False,
    )
```

```python
import functools

import jax
import jax.numpy as jnp
from jax import lax
from jax.experimental import pallas as pl
from jax.experimental.pallas import tpu as pltpu
from jax.sharding import Mesh, PartitionSpec as P

F32 = jnp.float32
BF16 = jnp.bfloat16
HEADS = 20
HD = 128
NB = 8
TOK = 128
LEN = 1024
WIDTH = 2560
EXPERTS = 64
HIDDEN = 512
SLOTS = 6
QROWS = 320
KVROWS = 384
CHUNK = 128
BACK = 160
SCALE = HD**-0.5
SCALE2 = SCALE * 1.4426950408889634
NT = (((1,), (1,)), ((), ()))
TN = (((0,), (0,)), ((), ()))
MIB = 1 << 20


def params(mib):
    return pltpu.CompilerParams(vmem_limit_bytes=mib * MIB)


def shape(*dims, dtype=BF16):
    return pltpu.HBM(dims, dtype)


def kept(*dims, dtype=BF16):
    return pltpu.VMEM(dims, dtype)


def hbm(*arrays):
    return [pltpu.with_memory_space_constraint(x, pltpu.HBM) for x in arrays]


class Copies:
    def __init__(self, sem):
        self.sem, self.started = sem, []

    def start(self, source, target):
        copy = pltpu.make_async_copy(source, target, self.sem.at[len(self.started)])
        copy.start()
        self.started.append(copy)
        return copy

    def wait(self):
        for copy in self.started:
            copy.wait()


IN_HBM = pl.BlockSpec(memory_space=pltpu.HBM)
IN_VMEM = pl.BlockSpec(memory_space=pltpu.VMEM)


def sems(count):
    return pltpu.SemaphoreType.DMA((count,))


def dot(a, b):
    return jnp.dot(a, b, preferred_element_type=F32)


def owned(dev):
    pair, odd = dev // 2, dev % 2
    return (5 * pair + 3 * odd, 5 * pair + 3 * odd + 1), 5 * pair + 2, odd


def cols(index):
    return slice(index * HD, (index + 1) * HD)


def pack_heads_kernel(q_hbm, k_hbm, v_hbm, out_hbm, q_ref, k_ref, v_ref, out_ref, in_sem, out_sem):
    sides = ((q_hbm, q_ref), (k_hbm, k_ref), (v_hbm, v_ref))
    at = [pl.ds(5 * HD * p, 5 * HD) for p in range(4)]
    arriving = Copies(in_sem)
    waits = [[arriving.start(x.at[:, at[p]], y.at[:, at[p]]) for x, y in sides] for p in range(4)]
    leaving = Copies(out_sem)
    for p in range(4):
        for copy in waits[p]:
            copy.wait()
        for dev in (2 * p, 2 * p + 1):
            heads, shared, odd = owned(dev)
            for i, h in enumerate(heads):
                out_ref[dev, i * HD : (i + 1) * HD, :] = q_ref[:, cols(h)]
            out_ref[dev, 256:320, :] = q_ref[64 * odd : 64 * odd + 64, cols(shared)]
            for base, ref in ((QROWS, k_ref), (QROWS + KVROWS, v_ref)):
                for i, h in enumerate(heads + (shared,)):
                    out_ref[dev, base + i * HD : base + (i + 1) * HD, :] = ref[:, cols(h)]
        both = pl.ds(2 * p, 2)
        leaving.start(out_ref.at[both], out_hbm.at[both])
    leaving.wait()


def pack_heads(q, k, v):
    rows = QROWS + 2 * KVROWS
    return pl.pallas_call(
        pack_heads_kernel,
        in_specs=[IN_HBM] * 3,
        out_specs=IN_HBM,
        out_shape=shape(NB, rows, HD),
        scratch_shapes=[pltpu.VMEM((TOK, WIDTH), BF16)] * 3 + [pltpu.VMEM((NB, rows, HD), BF16), sems(12), sems(4)],
        compiler_params=params(16),
        name="pack_heads",
    )(*hbm(q, k, v))


def unpack_grads_kernel(in_ref, q_hbm, k_hbm, v_hbm, q_ref, k_ref, v_ref, sem):
    leaving = Copies(sem)
    for p in range(4):
        for dev in (2 * p, 2 * p + 1):
            heads, shared, odd = owned(dev)
            for i, h in enumerate(heads):
                q_ref[:, cols(h)] = in_ref[dev, i * HD : (i + 1) * HD, :]
            q_ref[64 * odd : 64 * odd + 64, cols(shared)] = in_ref[dev, 256:320, :]
            for base, ref in ((QROWS, k_ref), (QROWS + KVROWS, v_ref)):
                for i, h in enumerate(heads):
                    ref[:, cols(h)] = in_ref[dev, base + i * HD : base + (i + 1) * HD, :]
        for base, ref in ((QROWS, k_ref), (QROWS + KVROWS, v_ref)):
            halves = [in_ref[2 * p + odd, base + 256 : base + 384, :].astype(F32) for odd in range(2)]
            ref[:, cols(5 * p + 2)] = (halves[0] + halves[1]).astype(BF16)
        at = pl.ds(5 * HD * p, 5 * HD)
        for x, y in ((q_ref, q_hbm), (k_ref, k_hbm), (v_ref, v_hbm)):
            leaving.start(x.at[:, at], y.at[:, at])
    leaving.wait()


def unpack_grads(buf):
    return pl.pallas_call(
        unpack_grads_kernel,
        in_specs=[IN_VMEM],
        out_specs=[IN_HBM] * 3,
        out_shape=[shape(TOK, WIDTH)] * 3,
        scratch_shapes=[pltpu.VMEM((TOK, WIDTH), BF16)] * 3 + [sems(12)],
        compiler_params=params(16),
        name="unpack_grads",
    )(buf)


def query_tiles():
    tiles = [(hi, slice(2 * t, 2 * t + 2), slice(hi * HD, (hi + 1) * HD), t) for hi in range(2) for t in range(4)]
    return tiles + [(2, slice(4 * t, 4 * t + 4), slice(256, 320), t) for t in range(2)]


def same_segment(hi, t, split, odd, keys_seg):
    lane = lax.broadcasted_iota(jnp.int32, (1, 256), 1)
    if hi < 2:
        frame = 256 * t + lane
    else:
        frame = 512 * t + (lane >> 6) * 128 + odd * 64 + (lane & 63)
    return keys_seg == (frame >= split).astype(jnp.int32)


def attention_kernel(info_ref, buf_ref, o_hbm, lse_hbm, o_ref, lse_ref, sem):
    split, odd = info_ref[0], info_ref[1]
    keys_seg = (lax.broadcasted_iota(jnp.int32, (LEN, 1), 0) >= split).astype(jnp.int32)
    held = None
    for number, (hi, blocks, rows, t) in enumerate(query_tiles()):
        if hi != held:
            held = hi
            k = buf_ref[:, QROWS + hi * HD : QROWS + (hi + 1) * HD, :].reshape(LEN, HD)
            v = buf_ref[:, QROWS + KVROWS + hi * HD : QROWS + KVROWS + (hi + 1) * HD, :].reshape(LEN, HD)
            v_t = v.astype(F32).T.astype(BF16)
        q = buf_ref[blocks, rows, :].reshape(256, HD)
        scores = lax.dot_general(k, q, NT, preferred_element_type=F32) * SCALE2
        scores = jnp.where(same_segment(hi, t, split, odd, keys_seg), scores, -1e30)
        top = jnp.max(scores, 0, keepdims=True)
        e = jnp.exp2(scores - top)
        total = jnp.sum(e, 0, keepdims=True)
        out = dot(v_t, e.astype(BF16)) / total
        o_ref[blocks, rows, :] = out.T.astype(BF16).reshape(o_ref[blocks, rows, :].shape)
        lse_ref[number] = jnp.broadcast_to(top + jnp.log2(total), (8, 256))
    leaving = Copies(sem)
    leaving.start(o_ref, o_hbm)
    leaving.start(lse_ref, lse_hbm)
    leaving.wait()


def attention(info, buf):
    return pl.pallas_call(
        attention_kernel,
        in_specs=[pl.BlockSpec(memory_space=pltpu.SMEM), IN_VMEM],
        out_specs=[IN_HBM] * 2,
        out_shape=[shape(NB, QROWS, HD), shape(10, 8, 256, dtype=F32)],
        scratch_shapes=[pltpu.VMEM((NB, QROWS, HD), BF16), pltpu.VMEM((10, 8, 256), F32), sems(2)],
        compiler_params=params(40),
        name="attention",
    )(info, buf)


def head_parts(hi):
    return [(hi * HD, HD if hi < 2 else 64), (QROWS + hi * HD, HD), (QROWS + KVROWS + hi * HD, HD)]


def attention_grad_kernel(info_ref, buf_hbm, do_ref, o_hbm, lse_hbm, out_hbm, buf_ref, o_ref, lse_ref, out_ref, in_sem, sem):
    leaving, arriving = Copies(sem), Copies(in_sem)

    def load(hi):
        parts = [pl.ds(*part) for part in head_parts(hi)]
        return [arriving.start(buf_hbm.at[:, at, :], buf_ref.at[:, at, :]) for at in parts]

    waits = [load(0) + [arriving.start(lse_hbm, lse_ref), arriving.start(o_hbm, o_ref)], load(1), load(2)]

    split, odd = info_ref[0], info_ref[1]
    keys_seg = (lax.broadcasted_iota(jnp.int32, (LEN, 1), 0) >= split).astype(jnp.int32)
    held = None
    sums = None

    def flush(hi):
        at = QROWS + hi * HD
        out_ref[:, at : at + HD, :] = (sums[0] * SCALE).astype(BF16).reshape(NB, TOK, HD)
        at = at + KVROWS
        out_ref[:, at : at + HD, :] = sums[1].astype(BF16).reshape(NB, TOK, HD)
        for part in head_parts(hi):
            at = pl.ds(*part)
            leaving.start(out_ref.at[:, at, :], out_hbm.at[:, at, :])

    for number, (hi, blocks, rows, t) in enumerate(query_tiles()):
        if hi != held:
            if held is not None:
                flush(held)
            held = hi
            sums = None
            for copy in waits[hi]:
                copy.wait()
            k = buf_ref[:, QROWS + hi * HD : QROWS + (hi + 1) * HD, :].reshape(LEN, HD)
            v = buf_ref[:, QROWS + KVROWS + hi * HD : QROWS + KVROWS + (hi + 1) * HD, :].reshape(LEN, HD)
            k_t = k.astype(F32).T.astype(BF16)
        q = buf_ref[blocks, rows, :].reshape(256, HD)
        grad = do_ref[blocks, rows, :].reshape(256, HD)
        out = o_ref[blocks, rows, :].reshape(256, HD)
        delta = jnp.sum((grad.astype(F32) * out.astype(F32)).T, 0, keepdims=True)
        scores = lax.dot_general(k, q, NT, preferred_element_type=F32) * SCALE2
        scores = jnp.where(same_segment(hi, t, split, odd, keys_seg), scores, -1e30)
        probs = jnp.exp2(scores - lse_ref[number, 0:1, :])
        d_probs = lax.dot_general(v, grad, NT, preferred_element_type=F32)
        d_scores = (probs * (d_probs - delta)).astype(BF16)
        terms = (dot(d_scores, q), dot(probs.astype(BF16), grad))
        sums = terms if sums is None else (sums[0] + terms[0], sums[1] + terms[1])
        d_q = (dot(k_t, d_scores) * SCALE).T.astype(BF16)
        out_ref[blocks, rows, :] = d_q.reshape(out_ref[blocks, rows, :].shape)
    flush(held)
    leaving.wait()


def attention_grad(info, buf, grad, out, lse):
    rows = QROWS + 2 * KVROWS
    return pl.pallas_call(
        attention_grad_kernel,
        in_specs=[pl.BlockSpec(memory_space=pltpu.SMEM), IN_HBM, IN_VMEM, IN_HBM, IN_HBM],
        out_specs=IN_HBM,
        out_shape=shape(NB, rows, HD),
        scratch_shapes=[
            pltpu.VMEM((NB, rows, HD), BF16),
            pltpu.VMEM((NB, QROWS, HD), BF16),
            pltpu.VMEM((10, 8, 256), F32),
            pltpu.VMEM((NB, rows, HD), BF16),
            sems(11),
            sems(9),
        ],
        compiler_params=params(40),
        name="attention_grad",
    )(info, *hbm(buf), grad, *hbm(out, lse))


def place_kernel(ids_ref, out_ref):
    expert = lax.broadcasted_iota(jnp.int32, (EXPERTS, TOK), 0)
    chosen = ((ids_ref[0:1, :] == expert) | (ids_ref[1:2, :] == expert)).astype(F32)
    before = lax.broadcasted_iota(jnp.int32, (TOK, TOK), 0) < lax.broadcasted_iota(jnp.int32, (TOK, TOK), 1)
    slot = dot(chosen.astype(BF16), before.astype(BF16))
    slot = jnp.where(chosen > 0.5, slot, -100.0).astype(jnp.int32)
    slot = slot.reshape(EXPERTS, 1, TOK)
    row = lax.broadcasted_iota(jnp.int32, (EXPERTS, 8, TOK), 1)
    out_ref[...] = close_up((slot == row).astype(F32)).astype(BF16)


def place_rows(ids):
    return pl.pallas_call(
        place_kernel,
        out_shape=shape(EXPERTS * SLOTS, TOK),
        compiler_params=params(24),
        name="place_rows",
    )(ids)


def close_up(x):
    row = lax.broadcasted_iota(jnp.int32, (1, 8, HD), 1)
    x = x.reshape(16, 4, 8, HD)
    b, c, d = pltpu.roll(x[:, 1], 6, 1), pltpu.roll(x[:, 2], 4, 1), pltpu.roll(x[:, 3], 2, 1)
    parts = (jnp.where(row < 6, x[:, 0], b), jnp.where(row < 4, b, c), jnp.where(row < 2, c, d))
    return jnp.concatenate([p[:, None] for p in parts], 1).reshape(EXPERTS * SLOTS, HD)


def spread(x):
    row = lax.broadcasted_iota(jnp.int32, (1, 8, HD), 1)
    x = x.reshape(16, 3, 8, HD)
    b = pltpu.roll(jnp.where(row >= 6, x[:, 0], x[:, 1]), 2, 1)
    c = pltpu.roll(jnp.where(row >= 4, x[:, 1], x[:, 2]), 4, 1)
    d = pltpu.roll(x[:, 2], 6, 1)
    return jnp.concatenate([p[:, None] for p in (x[:, 0], b, c, d)], 1).reshape(EXPERTS, 8, HD)


def rows_from_chunks(buf_ref, out_ref, ready=lambda at: None):
    row = lax.broadcasted_iota(jnp.int32, (1, 8, HD), 1)

    def tile(j):
        pair = buf_ref[:, (j // 2) * 16 : (j // 2 + 1) * 16, :].astype(F32)
        return pair.reshape(EXPERTS, 2, 8, HD)[:, j % 2]

    for u in range(5):
        tiles = [tile(3 * u + v) for v in range(3)]
        for v in range(3):
            out_ref[:, cols(3 * u + v)] = close_up(tiles[v]).astype(BF16)
        r = [pltpu.roll(tiles[v], (2 + 2 * v) % 8, 1) for v in range(3)]
        extra = jnp.where(row < 2, r[0], jnp.where(row < 4, r[1], r[2]))
        out_ref[:, cols(15 + u)] = close_up(extra).astype(BF16)
        ready(pl.ds(3 * u * HD, 3 * HD))
    ready(pl.ds(15 * HD, 5 * HD))


def chunks_from_rows(in_ref, emit):
    row = lax.broadcasted_iota(jnp.int32, (1, 8, HD), 1)
    before = None
    for u in range(5):
        last = spread(in_ref[:, cols(15 + u)])
        for v in range(3):
            j = 3 * u + v
            now = jnp.where(row < 6, spread(in_ref[:, cols(j)]), pltpu.roll(last, (6 - 2 * v) % 8, 1))
            if j % 2:
                emit(j // 2, jnp.concatenate([before, now], 1).astype(BF16))
            before = now
    emit(7, jnp.concatenate([before, jnp.zeros_like(before)], 1).astype(BF16))


def dispatch(place_ref, x_ref, rows_ref, out_ref, out_hbm, leaving):
    for c in range(5):
        at = slice(c * 512, (c + 1) * 512)
        rows_ref[:, at] = dot(place_ref[...], x_ref[:, at])

    def emit(t, pair):
        at = pl.ds(t * 16, 16)
        out_ref[:, at, :] = pair
        leaving.start(out_ref.at[:, at, :], out_hbm.at[:, at, :])

    chunks_from_rows(rows_ref, emit)
    leaving.wait()


def send_grads_kernel(place_ref, grad_ref, out_hbm, rows_ref, out_ref, sem):
    dispatch(place_ref, grad_ref, rows_ref, out_ref, out_hbm, Copies(sem))


def send_grads(place, grad):
    return pl.pallas_call(
        send_grads_kernel,
        out_specs=IN_HBM,
        out_shape=shape(EXPERTS, CHUNK, HD),
        scratch_shapes=[
            pltpu.VMEM((EXPERTS * SLOTS, WIDTH), F32),
            pltpu.VMEM((EXPERTS, CHUNK, HD), BF16),
            sems(8),
        ],
        compiler_params=params(24),
        name="send_grads",
    )(place, *hbm(grad))


def norm_kernel(place_ref, att_ref, stream_ref, gain_ref, mixed_hbm, out_hbm, mixed_ref, routed_ref, rows_ref, out_ref, sem):
    leaving = Copies(sem)
    for dev in range(NB):
        heads, shared, odd = owned(dev)
        for i, h in enumerate(heads):
            att = att_ref[dev, i * HD : (i + 1) * HD, :].astype(F32)
            mixed_ref[:, cols(h)] = (stream_ref[:, cols(h)].astype(F32) + att).astype(BF16)
        half = slice(64 * odd, 64 * odd + 64)
        att = att_ref[dev, 256:320, :].astype(F32)
        mixed_ref[half, cols(shared)] = (stream_ref[half, cols(shared)].astype(F32) + att).astype(BF16)
    leaving.start(mixed_ref, mixed_hbm)
    mixed = mixed_ref[...].astype(F32)
    rstd = lax.rsqrt(jnp.mean(mixed * mixed, -1, keepdims=True) + 1e-06)
    routed_ref[...] = (mixed * rstd * gain_ref[...]).astype(BF16)
    dispatch(place_ref, routed_ref, rows_ref, out_ref, out_hbm, leaving)


def norm_and_send(place, att, stream, gain):
    return pl.pallas_call(
        norm_kernel,
        out_specs=[IN_HBM] * 2,
        out_shape=[shape(TOK, WIDTH), shape(EXPERTS, CHUNK, HD)],
        scratch_shapes=[
            pltpu.VMEM((TOK, WIDTH), BF16),
            pltpu.VMEM((TOK, WIDTH), BF16),
            pltpu.VMEM((EXPERTS * SLOTS, WIDTH), F32),
            pltpu.VMEM((EXPERTS, CHUNK, HD), BF16),
            sems(9),
        ],
        compiler_params=params(24),
        name="norm_and_send",
    )(place, att, *hbm(stream), gain)


def unpack_rows_kernel(buf_ref, *refs):
    half = len(refs) // 2 - 2
    sources, rows_hbm, targets = refs[:half], refs[half], refs[half + 1 : 2 * half + 1]
    rows_ref, sem, in_sem = refs[2 * half + 1 :]
    arriving, leaving = Copies(in_sem), Copies(sem)
    for x, y in zip(sources, targets):
        arriving.start(x, y)
    rows_from_chunks(buf_ref, rows_ref, lambda at: leaving.start(rows_ref.at[:, at], rows_hbm.at[:, at]))
    leaving.wait()
    arriving.wait()


def unpack_rows(buf, *others):
    rows = EXPERTS * SLOTS
    count = len(others)
    outs = pl.pallas_call(
        unpack_rows_kernel,
        in_specs=[IN_VMEM] + [IN_HBM] * count,
        out_specs=[IN_HBM] + [IN_VMEM] * (count + 1),
        out_shape=[shape(rows, WIDTH)]
        + [kept(*x.shape, dtype=x.dtype) for x in others]
        + [kept(rows, WIDTH)],
        scratch_shapes=[sems(6), sems(max(count, 1))],
        compiler_params=params(24),
        name="unpack_rows",
    )(buf, *hbm(*others))
    return outs[0], outs[-1], *outs[1:-1]


def grad_rows_kernel(mine_ref, other_ref, down_ref, t_mine_hbm, t_other_hbm, t_mine_ref, t_other_ref, sem):
    leaving = Copies(sem)
    sides = ((mine_ref, t_mine_ref, t_mine_hbm), (other_ref, t_other_ref, t_other_hbm))
    for ref, t_ref, t_hbm in sides:
        for n in range(2):
            half = slice(n * 256, (n + 1) * 256)
            t_ref[:, half] = lax.dot_general(ref[...], down_ref[half, :], NT, preferred_element_type=F32)
        leaving.start(t_ref, t_hbm)
    leaving.wait()


def grad_rows(mine, other, w_down):
    rows = EXPERTS * SLOTS
    return pl.pallas_call(
        grad_rows_kernel,
        in_specs=[IN_VMEM] * 3,
        out_specs=[IN_HBM] * 2,
        out_shape=[shape(rows, HIDDEN, dtype=F32)] * 2,
        scratch_shapes=[pltpu.VMEM((rows, HIDDEN), F32)] * 2 + [sems(2)],
        compiler_params=params(32),
        cost_estimate=pl.CostEstimate(flops=4 * rows * WIDTH * HIDDEN, bytes_accessed=16 * MIB, transcendentals=0),
        name="grad_rows",
    )(*hbm(mine, other, w_down))


def expert_kernel(loads, rows_ref, t_ref, w_gate_ref, w_up_ref, router_ref, gain_ref, sums_in_ref, *refs):
    *held, back_out, sums_ref = refs[:5]
    d_a_ref, d_b_ref, hidden_ref, part_ref, back_ref, sem = refs[5:11]
    leaving = Copies(sem)
    if loads:
        arriving = Copies(refs[11])
        pairs = zip((w_gate_ref, w_up_ref, t_ref), refs[12:15])
        waits = [arriving.start(x, y) for x, y in pairs]
        w_gate_ref, w_up_ref, t_ref = refs[12:15]
    logit = lax.dot_general(rows_ref[...], router_ref[...], NT, preferred_element_type=F32)[:, 0:1]
    sig = jax.nn.sigmoid(logit)
    gate = sig.astype(BF16).astype(F32)
    score = None
    for n in range(2):
        half = slice(n * 256, (n + 1) * 256)
        if loads and n == 0:
            waits[0].wait()
        a_val = dot(rows_ref[...], w_gate_ref[:, half])
        if loads and n == 0:
            waits[1].wait()
            waits[2].wait()
        b_val = dot(rows_ref[...], w_up_ref[:, half])
        t_val = t_ref[:, half]
        sg = jax.nn.sigmoid(a_val)
        silu = a_val * sg
        hidden = (silu * b_val).astype(BF16).astype(F32)
        term = jnp.sum(hidden * t_val, -1, keepdims=True)
        score = term if score is None else score + term
        d_hidden = gate * t_val
        d_a_ref[:, half] = (d_hidden * b_val * sg * (1.0 + a_val * (1.0 - sg))).astype(BF16)
        d_b_ref[:, half] = (d_hidden * silu).astype(BF16)
        hidden_ref[:, half] = (gate * hidden).astype(BF16)
    for ref, target in zip((d_a_ref, d_b_ref, hidden_ref), held):
        leaving.start(ref, target)
    d_logit = score.astype(BF16).astype(F32) * sig * (1.0 - sig)
    for c in range(5):
        at = slice(c * 512, (c + 1) * 512)
        part = (
            lax.dot_general(d_a_ref[...], w_gate_ref[at, :], NT, preferred_element_type=F32)
            + lax.dot_general(d_b_ref[...], w_up_ref[at, :], NT, preferred_element_type=F32)
            + d_logit * router_ref[0:1, at].astype(F32)
        )
        part_ref[:, at] = part
        rows = rows_ref[:, at].astype(F32)
        sums_ref[0:1, at] = sums_in_ref[0:1, at] + jnp.sum(d_logit * rows, 0, keepdims=True)
        sums_ref[1:2, at] = sums_in_ref[1:2, at] + jnp.sum(part * rows, 0, keepdims=True) / gain_ref[:, at]

    def emit(t, pair):
        at = pl.ds(t * 16, 16)
        back_ref[:, at, :] = pair
        leaving.start(back_ref.at[:, at, :], back_out.at[:, at, :])

    chunks_from_rows(part_ref, emit)
    leaving.wait()


def expert_rows(loads, rows_in, t_val, w_gate, w_up, router, gain, sums):
    rows = EXPERTS * SLOTS
    scratch = [pltpu.VMEM((rows, HIDDEN), BF16)] * 3
    scratch += [pltpu.VMEM((rows, WIDTH), F32), pltpu.VMEM((EXPERTS, CHUNK, HD), BF16), sems(11)]
    if loads:
        scratch += [sems(3)] + [pltpu.VMEM((WIDTH, HIDDEN), BF16)] * 2 + [pltpu.VMEM((rows, HIDDEN), F32)]
        t_val, w_gate, w_up = hbm(t_val, w_gate, w_up)
    return pl.pallas_call(
        functools.partial(expert_kernel, loads),
        in_specs=[IN_VMEM] + [IN_HBM if loads else IN_VMEM] * 3 + [IN_VMEM] * 3,
        out_specs=[IN_HBM] * 4 + [IN_VMEM],
        out_shape=[
            shape(rows, HIDDEN),
            shape(rows, HIDDEN),
            shape(rows, HIDDEN),
            shape(EXPERTS, CHUNK, HD),
            jax.ShapeDtypeStruct((2, WIDTH), F32),
        ],
        scratch_shapes=scratch,
        compiler_params=params(24),
        cost_estimate=pl.CostEstimate(flops=8 * rows * WIDTH * HIDDEN, bytes_accessed=16 * MIB, transcendentals=0),
        name="expert_rows",
    )(rows_in, t_val, w_gate, w_up, router, gain, sums)


def weight_grads_kernel(ra, rb, ga, gb, daa, dab, dba, dbb, ha, hb, gate_ref, up_ref, down_ref):
    def product(first, second):
        terms = [lax.dot_general(x[...], y[...], TN, preferred_element_type=F32) for x, y in (first, second)]
        return (terms[0] + terms[1]).astype(BF16)

    gate_ref[...] = product((ra, daa), (rb, dab))
    up_ref[...] = product((ra, dba), (rb, dbb))
    down_ref[...] = product((ha, ga), (hb, gb))


def weight_grads(rows_in, grads, first, second):
    rows = EXPERTS * SLOTS
    wide = pl.BlockSpec((rows, 512), lambda i: (0, i))
    whole = pl.BlockSpec((rows, HIDDEN), lambda i: (0, 0))
    down = pl.BlockSpec((512, HIDDEN), lambda i: (i, 0))
    return pl.pallas_call(
        weight_grads_kernel,
        grid=(WIDTH // 512,),
        in_specs=[wide] * 4 + [whole] * 6,
        out_specs=[down, down, pl.BlockSpec((HIDDEN, 512), lambda i: (0, i))],
        out_shape=[shape(WIDTH, HIDDEN), shape(WIDTH, HIDDEN), shape(HIDDEN, WIDTH)],
        compiler_params=params(32),
        cost_estimate=pl.CostEstimate(flops=12 * rows * WIDTH * HIDDEN, bytes_accessed=20 * MIB, transcendentals=0),
        name="weight_grads",
    )(*hbm(*rows_in, *grads, first[0], second[0], first[1], second[1], first[2], second[2]))


def add_back_kernel(mine_hbm, other_ref, sums_ref, out_hbm, mine_ref, out_ref, in_sem, sem):
    arriving, leaving = Copies(in_sem), Copies(sem)
    groups = [pl.ds(g * 16, 16) for g in range(EXPERTS // 16)]
    for g in groups:
        arriving.start(mine_hbm.at[g], mine_ref.at[g])
    top = jnp.concatenate([jnp.zeros((8, HD), F32), sums_ref[0:8, :]], 0)
    for i, g in enumerate(groups):
        out_ref[g, 128:160, :] = jnp.broadcast_to(sums_ref[8:40, :].astype(BF16)[None], (16, 32, HD))
        arriving.started[i].wait()
        for t in range(8):
            at = slice(t * 16, (t + 1) * 16)
            total = mine_ref[g, at, :].astype(F32) + other_ref[g, at, :].astype(F32)
            out_ref[g, at, :] = (total if t < 7 else total + top[None]).astype(BF16)
        leaving.start(out_ref.at[g], out_hbm.at[g])
    leaving.wait()


def add_back(mine, other, sums):
    return pl.pallas_call(
        add_back_kernel,
        in_specs=[IN_HBM, IN_VMEM, IN_VMEM],
        out_specs=IN_HBM,
        out_shape=shape(EXPERTS, BACK, HD),
        scratch_shapes=[
            pltpu.VMEM((EXPERTS, CHUNK, HD), BF16),
            pltpu.VMEM((EXPERTS, BACK, HD), BF16),
            sems(4),
            sems(4),
        ],
        compiler_params=params(16),
        name="add_back",
    )(*hbm(mine), other, sums)


def combine_kernel(place_ref, back_ref, mixed_hbm, grad_hbm, gain_ref, stream_hbm, out_ref, *scratch):
    rows_ref, d_ref, stream_ref, grad_ref, mixed_ref, sem, out_sem = scratch
    arriving, leaving = Copies(sem), Copies(out_sem)
    arriving.start(mixed_hbm, mixed_ref)
    arriving.start(grad_hbm, grad_ref)
    rows_from_chunks(back_ref, rows_ref)
    for c in range(5):
        at = slice(c * 512, (c + 1) * 512)
        d_ref[:, at] = lax.dot_general(place_ref[...], rows_ref[:, at], TN, preferred_element_type=F32)
    arriving.wait()
    mixed = mixed_ref[...].astype(F32)
    rstd = lax.rsqrt(jnp.mean(mixed * mixed, -1, keepdims=True) + 1e-06)
    normed = mixed * rstd
    g = d_ref[...] * gain_ref[...]
    inner = jnp.mean(g * normed, -1, keepdims=True)
    stream_ref[...] = (grad_ref[...].astype(F32) + rstd * (g - normed * inner)).astype(BF16)
    leaving.start(stream_ref, stream_hbm)
    for dev in range(NB):
        heads, shared, odd = owned(dev)
        for i, h in enumerate(heads):
            out_ref[dev, i * HD : (i + 1) * HD, :] = stream_ref[:, cols(h)]
        out_ref[dev, 256:320, :] = stream_ref[64 * odd : 64 * odd + 64, cols(shared)]
    leaving.wait()


def combine(place, back, mixed, grad, gain):
    return pl.pallas_call(
        combine_kernel,
        in_specs=[IN_VMEM] * 2 + [IN_HBM] * 2 + [IN_VMEM],
        out_specs=[IN_HBM, IN_VMEM],
        out_shape=[shape(TOK, WIDTH), jax.ShapeDtypeStruct((NB, QROWS, HD), BF16)],
        scratch_shapes=[
            pltpu.VMEM((EXPERTS * SLOTS, WIDTH), BF16),
            pltpu.VMEM((TOK, WIDTH), F32),
            pltpu.VMEM((TOK, WIDTH), BF16),
            pltpu.VMEM((TOK, WIDTH), BF16),
            pltpu.VMEM((TOK, WIDTH), BF16),
            sems(2),
            sems(1),
        ],
        compiler_params=params(24),
        name="combine",
    )(place, back, *hbm(mixed, grad), gain)


def swap_cores(x):
    return lax.ppermute(x, "core", [(0, 1), (1, 0)])


def over_outer(x):
    return lax.all_to_all(x, "outer", split_axis=0, concat_axis=0, tiled=True)


def over_chips(x):
    return lax.all_to_all(x, ("outer", "chip"), split_axis=0, concat_axis=0, tiled=True)


def body(
    stream_in,
    queries,
    key_rows,
    value_rows,
    segment_ids,
    norm_gain,
    router_w,
    expert_ids,
    gate_w,
    up_w,
    down_w,
    out_grad,
):
    at = lax.axis_index("outer")
    split = jnp.sum((segment_ids[0] == 0).astype(jnp.int32))
    info = jnp.stack([split, at % 2]).astype(jnp.int32)
    gain = norm_gain.reshape(1, WIDTH)
    grads_local = out_grad[0]

    together = lax.optimization_barrier
    qkv = over_outer(pack_heads(queries[0], key_rows[0], value_rows[0]))
    place = place_rows(expert_ids[0].T)
    qkv, grads_buf = together((qkv, send_grads(place, grads_local)))
    grads_mine = over_chips(grads_buf)
    att, lse = attention(info, qkv)
    att, grads_mine = together((att, grads_mine))
    att_back = over_outer(att)
    mixed, rows_buf = norm_and_send(place, att_back, stream_in[0], gain)
    grads_first, _ = unpack_rows(grads_mine)
    rows_buf, grads_first = together((rows_buf, grads_first))
    rows_mine = over_chips(rows_buf)

    expert = at * 8 + lax.axis_index("chip")
    router = jnp.broadcast_to(lax.dynamic_slice_in_dim(router_w.T, expert, 1, 0), (8, WIDTH))
    grads_second = swap_cores(grads_first)
    t_first, t_second = grad_rows(grads_first, grads_second, down_w[0])
    rows_mine, t_first, t_second, router = together((rows_mine, t_first, t_second, router))
    weights = gate_w[0], up_w[0]
    rows_first, rows_here, *held = unpack_rows(rows_mine, t_first, *weights)
    rows_second = swap_cores(rows_first)
    nothing = jnp.zeros((2, WIDTH), F32)
    *first, back_mine, sums = expert_rows(False, rows_here, *held, router, gain, nothing)
    *second, back_other, sums = expert_rows(True, rows_second, t_second, *weights, router, gain, sums)
    sums = sums.reshape(40, HD)
    sums = sums + swap_cores(sums)
    back = over_chips(add_back(back_mine, swap_cores(back_other), sums))
    gate_grad, up_grad, down_grad = weight_grads((rows_first, rows_second), (grads_first, grads_second), first, second)
    back, gate_grad, up_grad, down_grad = together((back, gate_grad, up_grad, down_grad))

    stream_grad, grad_heads = combine(place, back, mixed, grads_local, gain)
    router_grad = back[:, 120:140, :].reshape(EXPERTS, WIDTH).T.astype(F32)
    gain_grad = jnp.sum(back[:, 140:160, :].astype(F32), 0).reshape(WIDTH)
    grad_in = over_outer(grad_heads)
    grads_out = over_outer(attention_grad(info, qkv, grad_in, att, lse))
    query_grad, key_grad, value_grad = unpack_grads(grads_out)
    return (
        stream_grad[None],
        query_grad[None],
        key_grad[None],
        value_grad[None],
        gain_grad,
        router_grad,
        gate_grad[None],
        up_grad[None],
        down_grad[None],
    )


def solution(mesh):
    chips = Mesh(mesh.devices.reshape(8, 8, 2), ("outer", "chip", "core"))
    inner = ("chip", "core")
    every = ("outer", "chip", "core")
    frames = P(inner, "outer", None)
    pieces = P(every, None, None)
    placed = (
        frames,
        frames,
        frames,
        frames,
        P(inner, None),
        P(),
        P(),
        frames,
        pieces,
        pieces,
        pieces,
        frames,
    )
    return jax.shard_map(
        body,
        mesh=chips,
        in_specs=placed,
        out_specs=(frames, frames, frames, frames, P(), P(), pieces, pieces, pieces),
        check_vma=False,
    )
```

```python
import functools

import jax
import jax.numpy as jnp
from jax import lax
from jax.experimental import pallas as pl
from jax.experimental.pallas import tpu as pltpu
from jax.sharding import Mesh, PartitionSpec as P

F32 = jnp.float32
BF16 = jnp.bfloat16
HEADS = 20
HD = 128
NB = 8
TOK = 128
LEN = 1024
WIDTH = 2560
EXPERTS = 64
HIDDEN = 512
SLOTS = 6
QROWS = 320
KVROWS = 384
CHUNK = 120
BACK = 160
SCALE = HD**-0.5
SCALE2 = SCALE * 1.4426950408889634
NT = (((1,), (1,)), ((), ()))
TN = (((0,), (0,)), ((), ()))
MIB = 1 << 20


def params(mib):
    return pltpu.CompilerParams(vmem_limit_bytes=mib * MIB)


def shape(*dims, dtype=BF16):
    return pltpu.HBM(dims, dtype)


def kept(*dims, dtype=BF16):
    return pltpu.VMEM(dims, dtype)


def vmem(x):
    return pltpu.with_memory_space_constraint(x, pltpu.VMEM)


def hbm(*arrays):
    return [pltpu.with_memory_space_constraint(x, pltpu.HBM) for x in arrays]


class Copies:
    def __init__(self, sem):
        self.sem, self.started = sem, []

    def start(self, source, target):
        copy = pltpu.make_async_copy(source, target, self.sem.at[len(self.started)])
        copy.start()
        self.started.append(copy)
        return copy

    def wait(self):
        for copy in self.started:
            copy.wait()


IN_HBM = pl.BlockSpec(memory_space=pltpu.HBM)
IN_VMEM = pl.BlockSpec(memory_space=pltpu.VMEM)


def sems(count):
    return pltpu.SemaphoreType.DMA((count,))


def dot(a, b):
    return jnp.dot(a, b, preferred_element_type=F32)


def owned(dev):
    pair, odd = dev // 2, dev % 2
    return (5 * pair + 3 * odd, 5 * pair + 3 * odd + 1), 5 * pair + 2, odd


def cols(index):
    return slice(index * HD, (index + 1) * HD)


def pack_heads_kernel(q_hbm, k_hbm, v_hbm, out_hbm, q_ref, k_ref, v_ref, out_ref, in_sem, out_sem):
    sides = ((q_hbm, q_ref), (k_hbm, k_ref), (v_hbm, v_ref))
    at = [pl.ds(5 * HD * p, 5 * HD) for p in range(4)]
    arriving = Copies(in_sem)
    waits = [[arriving.start(x.at[:, at[p]], y.at[:, at[p]]) for x, y in sides] for p in range(4)]
    leaving = Copies(out_sem)
    for p in range(4):
        for copy in waits[p]:
            copy.wait()
        for dev in (2 * p, 2 * p + 1):
            heads, shared, odd = owned(dev)
            for i, h in enumerate(heads):
                out_ref[dev, i * HD : (i + 1) * HD, :] = q_ref[:, cols(h)]
            out_ref[dev, 256:320, :] = q_ref[64 * odd : 64 * odd + 64, cols(shared)]
            for base, ref in ((QROWS, k_ref), (QROWS + KVROWS, v_ref)):
                for i, h in enumerate(heads + (shared,)):
                    out_ref[dev, base + i * HD : base + (i + 1) * HD, :] = ref[:, cols(h)]
        both = pl.ds(2 * p, 2)
        leaving.start(out_ref.at[both], out_hbm.at[both])
    leaving.wait()


def pack_heads(q, k, v):
    rows = QROWS + 2 * KVROWS
    return pl.pallas_call(
        pack_heads_kernel,
        in_specs=[IN_HBM] * 3,
        out_specs=IN_HBM,
        out_shape=shape(NB, rows, HD),
        scratch_shapes=[pltpu.VMEM((TOK, WIDTH), BF16)] * 3 + [pltpu.VMEM((NB, rows, HD), BF16), sems(12), sems(4)],
        compiler_params=params(16),
        name="pack_heads",
    )(*hbm(q, k, v))


def unpack_grads_kernel(in_ref, q_hbm, k_hbm, v_hbm, q_ref, k_ref, v_ref, sem):
    leaving = Copies(sem)
    for p in range(4):
        for dev in (2 * p, 2 * p + 1):
            heads, shared, odd = owned(dev)
            for i, h in enumerate(heads):
                q_ref[:, cols(h)] = in_ref[dev, i * HD : (i + 1) * HD, :]
            q_ref[64 * odd : 64 * odd + 64, cols(shared)] = in_ref[dev, 256:320, :]
            for base, ref in ((QROWS, k_ref), (QROWS + KVROWS, v_ref)):
                for i, h in enumerate(heads):
                    ref[:, cols(h)] = in_ref[dev, base + i * HD : base + (i + 1) * HD, :]
        for base, ref in ((QROWS, k_ref), (QROWS + KVROWS, v_ref)):
            halves = [in_ref[2 * p + odd, base + 256 : base + 384, :].astype(F32) for odd in range(2)]
            ref[:, cols(5 * p + 2)] = (halves[0] + halves[1]).astype(BF16)
        at = pl.ds(5 * HD * p, 5 * HD)
        for x, y in ((q_ref, q_hbm), (k_ref, k_hbm), (v_ref, v_hbm)):
            leaving.start(x.at[:, at], y.at[:, at])
    leaving.wait()


def unpack_grads(buf):
    return pl.pallas_call(
        unpack_grads_kernel,
        in_specs=[IN_VMEM],
        out_specs=[IN_HBM] * 3,
        out_shape=[shape(TOK, WIDTH)] * 3,
        scratch_shapes=[pltpu.VMEM((TOK, WIDTH), BF16)] * 3 + [sems(12)],
        compiler_params=params(16),
        name="unpack_grads",
    )(vmem(buf))


def query_tiles():
    tiles = [(hi, slice(2 * t, 2 * t + 2), slice(hi * HD, (hi + 1) * HD), t) for hi in range(2) for t in range(4)]
    return tiles + [(2, slice(4 * t, 4 * t + 4), slice(256, 320), t) for t in range(2)]


def key_range(hi, t):
    return (0, 768) if hi < 2 and t == 0 else (256, 1024) if hi < 2 and t == 3 else (0, 1024)


def same_segment(hi, t, split, odd, keys_seg):
    lane = lax.broadcasted_iota(jnp.int32, (1, 256), 1)
    if hi < 2:
        frame = 256 * t + lane
    else:
        frame = 512 * t + (lane >> 6) * 128 + odd * 64 + (lane & 63)
    return keys_seg == (frame >= split).astype(jnp.int32)


def attention_kernel(info_ref, buf_ref, o_hbm, lse_hbm, o_ref, lse_ref, sem):
    split, odd = info_ref[0], info_ref[1]
    keys_seg = (lax.broadcasted_iota(jnp.int32, (LEN, 1), 0) >= split).astype(jnp.int32)
    held = None
    for number, (hi, blocks, rows, t) in enumerate(query_tiles()):
        if hi != held:
            held = hi
            k = buf_ref[:, QROWS + hi * HD : QROWS + (hi + 1) * HD, :].reshape(LEN, HD)
            v = buf_ref[:, QROWS + KVROWS + hi * HD : QROWS + KVROWS + (hi + 1) * HD, :].reshape(LEN, HD)
            v_t = v.astype(F32).T.astype(BF16)
        q = buf_ref[blocks, rows, :].reshape(256, HD)
        low, high = key_range(hi, t)
        scores = lax.dot_general(k[low:high], q, NT, preferred_element_type=F32) * SCALE2
        scores = jnp.where(same_segment(hi, t, split, odd, keys_seg[low:high]), scores, -1e30)
        top = jnp.max(scores, 0, keepdims=True)
        e = jnp.exp2(scores - top)
        total = jnp.sum(e, 0, keepdims=True)
        out = dot(v_t[:, low:high], e.astype(BF16)) / total
        o_ref[blocks, rows, :] = out.T.astype(BF16).reshape(o_ref[blocks, rows, :].shape)
        lse_ref[number] = jnp.broadcast_to(top + jnp.log2(total), (8, 256))
    leaving = Copies(sem)
    leaving.start(o_ref, o_hbm)
    leaving.start(lse_ref, lse_hbm)
    leaving.wait()


def attention(info, buf):
    return pl.pallas_call(
        attention_kernel,
        in_specs=[pl.BlockSpec(memory_space=pltpu.SMEM), IN_VMEM],
        out_specs=[IN_HBM] * 2,
        out_shape=[shape(NB, QROWS, HD), shape(10, 8, 256, dtype=F32)],
        scratch_shapes=[pltpu.VMEM((NB, QROWS, HD), BF16), pltpu.VMEM((10, 8, 256), F32), sems(2)],
        compiler_params=params(40),
        name="attention",
    )(info, buf)


def attention_grad_kernel(info_ref, buf_ref, do_ref, o_ref, lse_ref, out_hbm, out_ref, sem):
    leaving = Copies(sem)
    split, odd = info_ref[0], info_ref[1]
    keys_seg = (lax.broadcasted_iota(jnp.int32, (LEN, 1), 0) >= split).astype(jnp.int32)
    held = None
    sums = None

    def flush(hi):
        k_at, v_at = QROWS + hi * HD, QROWS + KVROWS + hi * HD
        for c in range(4):
            blocks = slice(2 * c, 2 * c + 2)
            out_ref[blocks, k_at : k_at + HD, :] = (sums[c][0] * SCALE).astype(BF16).reshape(2, TOK, HD)
            out_ref[blocks, v_at : v_at + HD, :] = sums[c][1].astype(BF16).reshape(2, TOK, HD)
        for part in ((hi * HD, HD if hi < 2 else 64), (k_at, HD), (v_at, HD)):
            at = pl.ds(*part)
            leaving.start(out_ref.at[:, at, :], out_hbm.at[:, at, :])

    for number, (hi, blocks, rows, t) in enumerate(query_tiles()):
        if hi != held:
            if held is not None:
                flush(held)
            held = hi
            sums = [None] * 4
            k = buf_ref[:, QROWS + hi * HD : QROWS + (hi + 1) * HD, :].reshape(LEN, HD)
            v = buf_ref[:, QROWS + KVROWS + hi * HD : QROWS + KVROWS + (hi + 1) * HD, :].reshape(LEN, HD)
            k_t = k.astype(F32).T.astype(BF16)
        q = buf_ref[blocks, rows, :].reshape(256, HD)
        grad = do_ref[blocks, rows, :].reshape(256, HD)
        out = o_ref[blocks, rows, :].reshape(256, HD)
        delta = jnp.sum((grad.astype(F32) * out.astype(F32)).T, 0, keepdims=True)
        low, high = key_range(hi, t)
        scores = lax.dot_general(k[low:high], q, NT, preferred_element_type=F32) * SCALE2
        scores = jnp.where(same_segment(hi, t, split, odd, keys_seg[low:high]), scores, -1e30)
        probs = jnp.exp2(scores - lse_ref[number, 0:1, :])
        d_probs = lax.dot_general(v[low:high], grad, NT, preferred_element_type=F32)
        d_scores = (probs * (d_probs - delta)).astype(BF16)
        terms = (dot(d_scores, q), dot(probs.astype(BF16), grad))
        for c in range(low // 256, high // 256):
            at = slice(c * 256 - low, c * 256 - low + 256)
            parts = [term[at] for term in terms]
            sums[c] = parts if sums[c] is None else [x + y for x, y in zip(sums[c], parts)]
        d_q = (dot(k_t[:, low:high], d_scores) * SCALE).T.astype(BF16)
        out_ref[blocks, rows, :] = d_q.reshape(out_ref[blocks, rows, :].shape)
    flush(held)
    leaving.wait()


def attention_grad(info, buf, grad, out, lse):
    rows = QROWS + 2 * KVROWS
    return pl.pallas_call(
        attention_grad_kernel,
        in_specs=[pl.BlockSpec(memory_space=pltpu.SMEM)] + [IN_VMEM] * 4,
        out_specs=IN_HBM,
        out_shape=shape(NB, rows, HD),
        scratch_shapes=[pltpu.VMEM((NB, rows, HD), BF16), sems(9)],
        compiler_params=params(40),
        name="attention_grad",
    )(info, buf, grad, out, lse)


def place_kernel(ids_ref, out_ref):
    expert = lax.broadcasted_iota(jnp.int32, (EXPERTS, TOK), 0)
    chosen = ((ids_ref[0:1, :] == expert) | (ids_ref[1:2, :] == expert)).astype(F32)
    before = lax.broadcasted_iota(jnp.int32, (TOK, TOK), 0) < lax.broadcasted_iota(jnp.int32, (TOK, TOK), 1)
    slot = dot(chosen.astype(BF16), before.astype(BF16))
    slot = jnp.where(chosen > 0.5, slot, -100.0).astype(jnp.int32)
    slot = slot.reshape(EXPERTS, 1, TOK)
    row = lax.broadcasted_iota(jnp.int32, (EXPERTS, 8, TOK), 1)
    out_ref[...] = close_up((slot == row).astype(F32)).astype(BF16)


def place_rows(ids):
    return pl.pallas_call(
        place_kernel,
        out_shape=shape(EXPERTS * SLOTS, TOK),
        compiler_params=params(24),
        name="place_rows",
    )(ids)


def close_up(x):
    count = x.shape[0] // 4
    row = lax.broadcasted_iota(jnp.int32, (1, 8, HD), 1)
    x = x.reshape(count, 4, 8, HD)
    b, c, d = pltpu.roll(x[:, 1], 6, 1), pltpu.roll(x[:, 2], 4, 1), pltpu.roll(x[:, 3], 2, 1)
    parts = (jnp.where(row < 6, x[:, 0], b), jnp.where(row < 4, b, c), jnp.where(row < 2, c, d))
    return jnp.concatenate([p[:, None] for p in parts], 1).reshape(count * 24, HD)


def spread(x):
    count = x.shape[0] // 24
    row = lax.broadcasted_iota(jnp.int32, (1, 8, HD), 1)
    x = x.reshape(count, 3, 8, HD)
    b = pltpu.roll(jnp.where(row >= 6, x[:, 0], x[:, 1]), 2, 1)
    c = pltpu.roll(jnp.where(row >= 4, x[:, 1], x[:, 2]), 4, 1)
    d = pltpu.roll(x[:, 2], 6, 1)
    return jnp.concatenate([p[:, None] for p in (x[:, 0], b, c, d)], 1).reshape(count * 4, 8, HD)


GROUPS = [(slice(g * 16, g * 16 + 16), slice(g * 96, g * 96 + 96)) for g in range(4)]


def rows_from_chunks(buf_ref, out_ref, ready=lambda g: None):
    row = lax.broadcasted_iota(jnp.int32, (1, 8, HD), 1)
    for g, (chunks, rows) in enumerate(GROUPS):

        def tile(j):
            if j == 14:
                return buf_ref[chunks, 112:120, :].astype(F32)
            pair = buf_ref[chunks, (j // 2) * 16 : (j // 2 + 1) * 16, :].astype(F32)
            return pair.reshape(16, 2, 8, HD)[:, j % 2]

        for u in range(5):
            tiles = [tile(3 * u + v) for v in range(3)]
            for v in range(3):
                out_ref[rows, cols(3 * u + v)] = close_up(tiles[v]).astype(BF16)
            r = [pltpu.roll(tiles[v], (2 + 2 * v) % 8, 1) for v in range(3)]
            extra = jnp.where(row < 2, r[0], jnp.where(row < 4, r[1], r[2]))
            out_ref[rows, cols(15 + u)] = close_up(extra).astype(BF16)
        ready(g)


def chunks_from_rows(in_ref, out_ref, out_hbm, leaving):
    row = lax.broadcasted_iota(jnp.int32, (1, 8, HD), 1)
    for g, (chunks, rows) in enumerate(GROUPS):
        before = None
        for u in range(5):
            last = spread(in_ref[rows, cols(15 + u)])
            for v in range(3):
                j = 3 * u + v
                now = jnp.where(row < 6, spread(in_ref[rows, cols(j)]), pltpu.roll(last, (6 - 2 * v) % 8, 1))
                if j % 2:
                    both = jnp.concatenate([before, now], 1).astype(BF16)
                    out_ref[chunks, (j // 2) * 16 : (j // 2 + 1) * 16, :] = both
                before = now
        out_ref[chunks, 112:120, :] = before.astype(BF16)
        at = pl.ds(16 * g, 16)
        leaving.start(out_ref.at[at], out_hbm.at[at])


def dispatch(place_ref, x_ref, rows_ref, out_ref, out_hbm, leaving):
    for c in range(5):
        at = slice(c * 512, (c + 1) * 512)
        rows_ref[:, at] = dot(place_ref[...], x_ref[:, at])
    chunks_from_rows(rows_ref, out_ref, out_hbm, leaving)
    leaving.wait()


def send_grads_kernel(place_ref, grad_ref, out_hbm, rows_ref, out_ref, sem):
    dispatch(place_ref, grad_ref, rows_ref, out_ref, out_hbm, Copies(sem))


def send_grads(place, grad):
    return pl.pallas_call(
        send_grads_kernel,
        out_specs=IN_HBM,
        out_shape=shape(EXPERTS, CHUNK, HD),
        scratch_shapes=[
            pltpu.VMEM((EXPERTS * SLOTS, WIDTH), F32),
            pltpu.VMEM((EXPERTS, CHUNK, HD), BF16),
            sems(8),
        ],
        compiler_params=params(24),
        name="send_grads",
    )(place, *hbm(grad))


def norm_kernel(place_ref, att_ref, stream_ref, gain_ref, mixed_hbm, out_hbm, mixed_ref, routed_ref, rows_ref, out_ref, sem):
    leaving = Copies(sem)
    for dev in range(NB):
        heads, shared, odd = owned(dev)
        for i, h in enumerate(heads):
            att = att_ref[dev, i * HD : (i + 1) * HD, :].astype(F32)
            mixed_ref[:, cols(h)] = (stream_ref[:, cols(h)].astype(F32) + att).astype(BF16)
        half = slice(64 * odd, 64 * odd + 64)
        att = att_ref[dev, 256:320, :].astype(F32)
        mixed_ref[half, cols(shared)] = (stream_ref[half, cols(shared)].astype(F32) + att).astype(BF16)
    leaving.start(mixed_ref, mixed_hbm)
    mixed = mixed_ref[...].astype(F32)
    rstd = lax.rsqrt(jnp.mean(mixed * mixed, -1, keepdims=True) + 1e-06)
    routed_ref[...] = (mixed * rstd * gain_ref[...]).astype(BF16)
    dispatch(place_ref, routed_ref, rows_ref, out_ref, out_hbm, leaving)


def norm_and_send(place, att, stream, gain):
    return pl.pallas_call(
        norm_kernel,
        out_specs=[IN_HBM] * 2,
        out_shape=[shape(TOK, WIDTH), shape(EXPERTS, CHUNK, HD)],
        scratch_shapes=[
            pltpu.VMEM((TOK, WIDTH), BF16),
            pltpu.VMEM((TOK, WIDTH), BF16),
            pltpu.VMEM((EXPERTS * SLOTS, WIDTH), F32),
            pltpu.VMEM((EXPERTS, CHUNK, HD), BF16),
            sems(9),
        ],
        compiler_params=params(24),
        name="norm_and_send",
    )(place, att, *hbm(stream), gain)


def unpack_into(buf_ref, rows_ref, rows_hbm, leaving):
    def ready(g):
        at = pl.ds(96 * g, 96)
        leaving.start(rows_ref.at[at], rows_hbm.at[at])

    rows_from_chunks(buf_ref, rows_ref, ready)


def unpack_rows_kernel(buf_ref, rows_hbm, rows_ref, sem):
    leaving = Copies(sem)
    unpack_into(buf_ref, rows_ref, rows_hbm, leaving)
    leaving.wait()


def unpack_rows(buf):
    rows = EXPERTS * SLOTS
    return pl.pallas_call(
        unpack_rows_kernel,
        in_specs=[IN_VMEM],
        out_specs=IN_HBM,
        out_shape=shape(rows, WIDTH),
        scratch_shapes=[pltpu.VMEM((rows, WIDTH), BF16), sems(4)],
        compiler_params=params(16),
        cost_estimate=pl.CostEstimate(flops=0, bytes_accessed=6 * MIB, transcendentals=0),
        name="unpack_rows",
    )(buf)


def grad_rows_kernel(mine_ref, other_ref, down_ref, t_mine_hbm, t_other_hbm, t_mine_ref, t_other_ref, sem):
    leaving = Copies(sem)
    sides = ((mine_ref, t_mine_ref, t_mine_hbm), (other_ref, t_other_ref, t_other_hbm))
    for ref, t_ref, t_hbm in sides:
        for n in range(2):
            half = slice(n * 256, (n + 1) * 256)
            t_ref[:, half] = lax.dot_general(ref[...], down_ref[half, :], NT, preferred_element_type=F32)
        leaving.start(t_ref, t_hbm)
    leaving.wait()


def grad_rows(mine, other, w_down):
    rows = EXPERTS * SLOTS
    return pl.pallas_call(
        grad_rows_kernel,
        in_specs=[IN_VMEM] * 3,
        out_specs=[IN_HBM] * 2,
        out_shape=[shape(rows, HIDDEN, dtype=F32)] * 2,
        scratch_shapes=[pltpu.VMEM((rows, HIDDEN), F32)] * 2 + [sems(2)],
        compiler_params=params(32),
        cost_estimate=pl.CostEstimate(flops=4 * rows * WIDTH * HIDDEN, bytes_accessed=16 * MIB, transcendentals=0),
        name="grad_rows",
    )(*hbm(mine, other, w_down))


def expert_kernel(first, rows_ref, t_ref, w_gate_ref, w_up_ref, router_ref, gain_ref, sums_in_ref, *refs):
    *held, back_out, sums_ref = refs[:5]
    refs = refs[5:]
    if first:
        rows_hbm, refs = refs[0], refs[1:]
    d_a_ref, d_b_ref, hidden_ref, part_ref, back_ref, sem = refs[:6]
    leaving = Copies(sem)
    if first:
        arriving = Copies(refs[6])
        pairs = zip((w_gate_ref, w_up_ref, t_ref), refs[7:10])
        waits = [arriving.start(x, y) for x, y in pairs]
        w_gate_ref, w_up_ref, t_ref = refs[7:10]
        unpack_into(rows_ref, refs[10], rows_hbm, leaving)
        rows_ref = refs[10]
    logit = lax.dot_general(rows_ref[...], router_ref[...], NT, preferred_element_type=F32)[:, 0:1]
    sig = jax.nn.sigmoid(logit)
    gate = sig.astype(BF16).astype(F32)
    score = None
    for n in range(2):
        half = slice(n * 256, (n + 1) * 256)
        if first and n == 0:
            waits[0].wait()
        a_val = dot(rows_ref[...], w_gate_ref[:, half])
        if first and n == 0:
            waits[1].wait()
            waits[2].wait()
        b_val = dot(rows_ref[...], w_up_ref[:, half])
        t_val = t_ref[:, half]
        sg = jax.nn.sigmoid(a_val)
        silu = a_val * sg
        hidden = (silu * b_val).astype(BF16).astype(F32)
        term = jnp.sum(hidden * t_val, -1, keepdims=True)
        score = term if score is None else score + term
        d_hidden = gate * t_val
        d_a_ref[:, half] = (d_hidden * b_val * sg * (1.0 + a_val * (1.0 - sg))).astype(BF16)
        d_b_ref[:, half] = (d_hidden * silu).astype(BF16)
        hidden_ref[:, half] = (gate * hidden).astype(BF16)
    for ref, target in zip((d_a_ref, d_b_ref, hidden_ref), held):
        leaving.start(ref, target)
    d_logit = score.astype(BF16).astype(F32) * sig * (1.0 - sig)
    for c in range(5):
        at = slice(c * 512, (c + 1) * 512)
        part = (
            lax.dot_general(d_a_ref[...], w_gate_ref[at, :], NT, preferred_element_type=F32)
            + lax.dot_general(d_b_ref[...], w_up_ref[at, :], NT, preferred_element_type=F32)
            + d_logit * router_ref[0:1, at].astype(F32)
        )
        part_ref[:, at] = part
        rows = rows_ref[:, at].astype(F32)
        sums_ref[0:1, at] = sums_in_ref[0:1, at] + jnp.sum(d_logit * rows, 0, keepdims=True)
        sums_ref[1:2, at] = sums_in_ref[1:2, at] + jnp.sum(part * rows, 0, keepdims=True) / gain_ref[:, at]

    chunks_from_rows(part_ref, back_ref, back_out, leaving)
    leaving.wait()


def expert_rows(first, rows_in, t_val, w_gate, w_up, router, gain, sums):
    rows = EXPERTS * SLOTS
    scratch = [pltpu.VMEM((rows, HIDDEN), BF16)] * 3
    scratch += [pltpu.VMEM((rows, WIDTH), F32), pltpu.VMEM((EXPERTS, CHUNK, HD), BF16), sems(11)]
    out_specs = [IN_HBM] * 4 + [IN_VMEM]
    out_shape = [shape(rows, HIDDEN)] * 3 + [shape(EXPERTS, CHUNK, HD), jax.ShapeDtypeStruct((2, WIDTH), F32)]
    if first:
        scratch += [sems(3)] + [pltpu.VMEM((WIDTH, HIDDEN), BF16)] * 2
        scratch += [pltpu.VMEM((rows, HIDDEN), F32), pltpu.VMEM((rows, WIDTH), BF16)]
        t_val, w_gate, w_up = hbm(t_val, w_gate, w_up)
        out_specs.append(IN_HBM)
        out_shape.append(shape(rows, WIDTH))
    return pl.pallas_call(
        functools.partial(expert_kernel, first),
        in_specs=[IN_VMEM] + [IN_HBM if first else IN_VMEM] * 3 + [IN_VMEM] * 3,
        out_specs=out_specs,
        out_shape=out_shape,
        scratch_shapes=scratch,
        compiler_params=params(24),
        cost_estimate=pl.CostEstimate(flops=8 * rows * WIDTH * HIDDEN, bytes_accessed=16 * MIB, transcendentals=0),
        name="expert_rows",
    )(rows_in, t_val, w_gate, w_up, router, gain, sums)


def weight_grads_kernel(ra, rb, ga, gb, daa, dab, dba, dbb, ha, hb, gate_ref, up_ref, down_ref):
    def product(first, second):
        terms = [lax.dot_general(x[...], y[...], TN, preferred_element_type=F32) for x, y in (first, second)]
        return (terms[0] + terms[1]).astype(BF16)

    gate_ref[...] = product((ra, daa), (rb, dab))
    up_ref[...] = product((ra, dba), (rb, dbb))
    down_ref[...] = product((ha, ga), (hb, gb))


def weight_grads(rows_in, grads, first, second):
    rows = EXPERTS * SLOTS
    wide = pl.BlockSpec((rows, 512), lambda i: (0, i))
    whole = pl.BlockSpec((rows, HIDDEN), lambda i: (0, 0))
    down = pl.BlockSpec((512, HIDDEN), lambda i: (i, 0))
    return pl.pallas_call(
        weight_grads_kernel,
        grid=(WIDTH // 512,),
        in_specs=[wide] * 4 + [whole] * 6,
        out_specs=[down, down, pl.BlockSpec((HIDDEN, 512), lambda i: (0, i))],
        out_shape=[shape(WIDTH, HIDDEN), shape(WIDTH, HIDDEN), shape(HIDDEN, WIDTH)],
        compiler_params=params(32),
        cost_estimate=pl.CostEstimate(flops=12 * rows * WIDTH * HIDDEN, bytes_accessed=20 * MIB, transcendentals=0),
        name="weight_grads",
    )(*hbm(*rows_in, *grads, first[0], second[0], first[1], second[1], first[2], second[2]))


def add_back_kernel(mine_hbm, other_hbm, sums_ref, out_hbm, mine_ref, other_ref, out_ref, in_sem, sem):
    arriving, leaving = Copies(in_sem), Copies(sem)
    groups = [pl.ds(g * 16, 16) for g in range(EXPERTS // 16)]
    for g in groups:
        arriving.start(mine_hbm.at[g], mine_ref.at[g])
        arriving.start(other_hbm.at[g], other_ref.at[g])
    for i, g in enumerate(groups):
        out_ref[g, 128:160, :] = jnp.broadcast_to(sums_ref[8:40, :].astype(BF16)[None], (16, 32, HD))
        arriving.started[2 * i].wait()
        arriving.started[2 * i + 1].wait()
        for t in range(7):
            at = slice(t * 16, (t + 1) * 16)
            out_ref[g, at, :] = (mine_ref[g, at, :].astype(F32) + other_ref[g, at, :].astype(F32)).astype(BF16)
        total = mine_ref[g, 112:120, :].astype(F32) + other_ref[g, 112:120, :].astype(F32)
        top = jnp.broadcast_to(sums_ref[0:8, :][None], (16, 8, HD))
        out_ref[g, 112:128, :] = jnp.concatenate([total, top], 1).astype(BF16)
        leaving.start(out_ref.at[g], out_hbm.at[g])
    leaving.wait()


def add_back(mine, other, sums):
    return pl.pallas_call(
        add_back_kernel,
        in_specs=[IN_HBM, IN_HBM, IN_VMEM],
        out_specs=IN_HBM,
        out_shape=shape(EXPERTS, BACK, HD),
        scratch_shapes=[
            pltpu.VMEM((EXPERTS, CHUNK, HD), BF16),
            pltpu.VMEM((EXPERTS, CHUNK, HD), BF16),
            pltpu.VMEM((EXPERTS, BACK, HD), BF16),
            sems(8),
            sems(4),
        ],
        compiler_params=params(16),
        name="add_back",
    )(*hbm(mine, other), sums)


def combine_kernel(place_ref, back_ref, mixed_hbm, grad_hbm, gain_ref, stream_hbm, out_ref, *scratch):
    rows_ref, d_ref, stream_ref, grad_ref, mixed_ref, sem, out_sem = scratch
    arriving, leaving = Copies(sem), Copies(out_sem)
    arriving.start(mixed_hbm, mixed_ref)
    arriving.start(grad_hbm, grad_ref)
    rows_from_chunks(back_ref, rows_ref)
    for c in range(5):
        at = slice(c * 512, (c + 1) * 512)
        d_ref[:, at] = lax.dot_general(place_ref[...], rows_ref[:, at], TN, preferred_element_type=F32)
    arriving.wait()
    mixed = mixed_ref[...].astype(F32)
    rstd = lax.rsqrt(jnp.mean(mixed * mixed, -1, keepdims=True) + 1e-06)
    normed = mixed * rstd
    g = d_ref[...] * gain_ref[...]
    inner = jnp.mean(g * normed, -1, keepdims=True)
    stream_ref[...] = (grad_ref[...].astype(F32) + rstd * (g - normed * inner)).astype(BF16)
    leaving.start(stream_ref, stream_hbm)
    for dev in range(NB):
        heads, shared, odd = owned(dev)
        for i, h in enumerate(heads):
            out_ref[dev, i * HD : (i + 1) * HD, :] = stream_ref[:, cols(h)]
        out_ref[dev, 256:320, :] = stream_ref[64 * odd : 64 * odd + 64, cols(shared)]
    leaving.wait()


def combine(place, back, mixed, grad, gain):
    return pl.pallas_call(
        combine_kernel,
        in_specs=[IN_VMEM] * 2 + [IN_HBM] * 2 + [IN_VMEM],
        out_specs=[IN_HBM, IN_VMEM],
        out_shape=[shape(TOK, WIDTH), jax.ShapeDtypeStruct((NB, QROWS, HD), BF16)],
        scratch_shapes=[
            pltpu.VMEM((EXPERTS * SLOTS, WIDTH), BF16),
            pltpu.VMEM((TOK, WIDTH), F32),
            pltpu.VMEM((TOK, WIDTH), BF16),
            pltpu.VMEM((TOK, WIDTH), BF16),
            pltpu.VMEM((TOK, WIDTH), BF16),
            sems(2),
            sems(1),
        ],
        compiler_params=params(24),
        name="combine",
    )(place, back, *hbm(mixed, grad), gain)


def swap_cores(x):
    return lax.ppermute(x, "core", [(0, 1), (1, 0)])


def over_outer(x):
    return lax.all_to_all(x, "outer", split_axis=0, concat_axis=0, tiled=True)


def over_chips(x):
    return lax.all_to_all(x, ("outer", "chip"), split_axis=0, concat_axis=0, tiled=True)


def body(
    stream_in,
    queries,
    key_rows,
    value_rows,
    segment_ids,
    norm_gain,
    router_w,
    expert_ids,
    gate_w,
    up_w,
    down_w,
    out_grad,
):
    at = lax.axis_index("outer")
    split = jnp.sum((segment_ids[0] == 0).astype(jnp.int32))
    info = jnp.stack([split, at % 2]).astype(jnp.int32)
    gain = norm_gain.reshape(1, WIDTH)
    grads_local = out_grad[0]

    together = lax.optimization_barrier
    qkv = over_outer(pack_heads(queries[0], key_rows[0], value_rows[0]))
    place = place_rows(expert_ids[0].T)
    qkv, grads_buf = together((qkv, send_grads(place, grads_local)))
    grads_mine = over_chips(grads_buf)
    att, lse = attention(info, qkv)
    att, grads_mine = together((att, grads_mine))
    att_back = over_outer(att)
    mixed, rows_buf = norm_and_send(place, att_back, stream_in[0], gain)
    grads_first = unpack_rows(grads_mine)
    rows_buf, grads_first = together((rows_buf, grads_first))
    rows_mine = over_chips(rows_buf)

    expert = at * 8 + lax.axis_index("chip")
    router = jnp.broadcast_to(lax.dynamic_slice_in_dim(router_w.T, expert, 1, 0), (8, WIDTH))
    grads_second = swap_cores(grads_first)
    t_first, t_second = grad_rows(grads_first, grads_second, down_w[0])
    rows_mine, t_first, t_second, router = together((rows_mine, t_first, t_second, router))
    weights = gate_w[0], up_w[0]
    rows_other = swap_cores(rows_mine)
    rows_first = unpack_rows(rows_mine)
    rows_other, rows_first = together((rows_other, rows_first))
    nothing = jnp.zeros((2, WIDTH), F32)
    *second, back_other, sums, rows_second = expert_rows(
        True, rows_other, t_second, *weights, router, gain, nothing
    )
    back_other = swap_cores(back_other)
    *first, back_mine, sums = expert_rows(False, rows_first, t_first, *weights, router, gain, sums)
    back = over_chips(add_back(back_mine, back_other, sums.reshape(40, HD)))
    gate_grad, up_grad, down_grad = weight_grads(
        (rows_first, rows_second), (grads_first, grads_second), first, second
    )
    back, gate_grad, up_grad, down_grad = together((back, gate_grad, up_grad, down_grad))

    stream_grad, grad_heads = combine(place, back, mixed, grads_local, gain)
    grad_in = over_outer(grad_heads)
    grads_buf = attention_grad(info, qkv, grad_in, att, lse)
    grads_buf, back = together((grads_buf, back))
    router_part = back[:, 120:140, :].astype(F32).reshape(EXPERTS * 20, HD)
    gain_part = jnp.sum(back[:, 140:160, :].astype(F32), 0)
    parts = jnp.concatenate([router_part, gain_part])
    parts = parts + swap_cores(parts)
    router_grad = parts[: EXPERTS * 20].reshape(EXPERTS, WIDTH).T
    gain_grad = parts[EXPERTS * 20 :].reshape(WIDTH)
    query_grad, key_grad, value_grad = unpack_grads(over_outer(grads_buf))
    return (
        stream_grad[None],
        query_grad[None],
        key_grad[None],
        value_grad[None],
        gain_grad,
        router_grad,
        gate_grad[None],
        up_grad[None],
        down_grad[None],
    )


def solution(mesh):
    chips = Mesh(mesh.devices.reshape(8, 8, 2), ("outer", "chip", "core"))
    inner = ("chip", "core")
    every = ("outer", "chip", "core")
    frames = P(inner, "outer", None)
    pieces = P(every, None, None)
    placed = (
        frames,
        frames,
        frames,
        frames,
        P(inner, None),
        P(),
        P(),
        frames,
        pieces,
        pieces,
        pieces,
        frames,
    )
    return jax.shard_map(
        body,
        mesh=chips,
        in_specs=placed,
        out_specs=(frames, frames, frames, frames, P(), P(), pieces, pieces, pieces),
        check_vma=False,
    )
```

```python
import functools

import jax
import jax.numpy as jnp
from jax import lax
from jax.experimental import pallas as pl
from jax.experimental.pallas import tpu as pltpu
from jax.sharding import Mesh, PartitionSpec as P

F32 = jnp.float32
BF16 = jnp.bfloat16
HEADS = 20
HD = 128
NB = 8
TOK = 128
LEN = 1024
WIDTH = 2560
EXPERTS = 64
HIDDEN = 512
SLOTS = 6
QROWS = 320
KVROWS = 384
CHUNK = 120
BACK = 160
SCALE = HD**-0.5
SCALE2 = SCALE * 1.4426950408889634
NT = (((1,), (1,)), ((), ()))
TN = (((0,), (0,)), ((), ()))
MIB = 1 << 20


def params(mib):
    return pltpu.CompilerParams(vmem_limit_bytes=mib * MIB)


def shape(*dims, dtype=BF16):
    return pltpu.HBM(dims, dtype)


def kept(*dims, dtype=BF16):
    return pltpu.VMEM(dims, dtype)


def vmem(x):
    return pltpu.with_memory_space_constraint(x, pltpu.VMEM)


def hbm(*arrays):
    return [pltpu.with_memory_space_constraint(x, pltpu.HBM) for x in arrays]


class Copies:
    def __init__(self, sem):
        self.sem, self.started = sem, []

    def start(self, source, target):
        copy = pltpu.make_async_copy(source, target, self.sem.at[len(self.started)])
        copy.start()
        self.started.append(copy)
        return copy

    def wait(self):
        for copy in self.started:
            copy.wait()


IN_HBM = pl.BlockSpec(memory_space=pltpu.HBM)
IN_VMEM = pl.BlockSpec(memory_space=pltpu.VMEM)


def sems(count):
    return pltpu.SemaphoreType.DMA((count,))


def dot(a, b):
    return jnp.dot(a, b, preferred_element_type=F32)


def owned(dev):
    pair, odd = dev // 2, dev % 2
    return (5 * pair + 3 * odd, 5 * pair + 3 * odd + 1), 5 * pair + 2, odd


def cols(index):
    return slice(index * HD, (index + 1) * HD)


def pack_heads_kernel(q_hbm, k_hbm, v_hbm, out_hbm, q_ref, k_ref, v_ref, out_ref, in_sem, out_sem):
    sides = ((q_hbm, q_ref), (k_hbm, k_ref), (v_hbm, v_ref))
    at = [pl.ds(5 * HD * p, 5 * HD) for p in range(4)]
    arriving = Copies(in_sem)
    waits = [[arriving.start(x.at[:, at[p]], y.at[:, at[p]]) for x, y in sides] for p in range(4)]
    leaving = Copies(out_sem)
    for p in range(4):
        for copy in waits[p]:
            copy.wait()
        for dev in (2 * p, 2 * p + 1):
            heads, shared, odd = owned(dev)
            for i, h in enumerate(heads):
                out_ref[dev, i * HD : (i + 1) * HD, :] = q_ref[:, cols(h)]
            out_ref[dev, 256:320, :] = q_ref[64 * odd : 64 * odd + 64, cols(shared)]
            for base, ref in ((QROWS, k_ref), (QROWS + KVROWS, v_ref)):
                for i, h in enumerate(heads + (shared,)):
                    out_ref[dev, base + i * HD : base + (i + 1) * HD, :] = ref[:, cols(h)]
        both = pl.ds(2 * p, 2)
        leaving.start(out_ref.at[both], out_hbm.at[both])
    leaving.wait()


def pack_heads(q, k, v):
    rows = QROWS + 2 * KVROWS
    return pl.pallas_call(
        pack_heads_kernel,
        in_specs=[IN_HBM] * 3,
        out_specs=IN_HBM,
        out_shape=shape(NB, rows, HD),
        scratch_shapes=[pltpu.VMEM((TOK, WIDTH), BF16)] * 3 + [pltpu.VMEM((NB, rows, HD), BF16), sems(12), sems(4)],
        compiler_params=params(16),
        name="pack_heads",
    )(*hbm(q, k, v))


def unpack_grads_kernel(in_ref, q_hbm, k_hbm, v_hbm, q_ref, k_ref, v_ref, sem):
    leaving = Copies(sem)
    for p in range(4):
        for dev in (2 * p, 2 * p + 1):
            heads, shared, odd = owned(dev)
            for i, h in enumerate(heads):
                q_ref[:, cols(h)] = in_ref[dev, i * HD : (i + 1) * HD, :]
            q_ref[64 * odd : 64 * odd + 64, cols(shared)] = in_ref[dev, 256:320, :]
            for base, ref in ((QROWS, k_ref), (QROWS + KVROWS, v_ref)):
                for i, h in enumerate(heads):
                    ref[:, cols(h)] = in_ref[dev, base + i * HD : base + (i + 1) * HD, :]
        for base, ref in ((QROWS, k_ref), (QROWS + KVROWS, v_ref)):
            halves = [in_ref[2 * p + odd, base + 256 : base + 384, :].astype(F32) for odd in range(2)]
            ref[:, cols(5 * p + 2)] = (halves[0] + halves[1]).astype(BF16)
        at = pl.ds(5 * HD * p, 5 * HD)
        for x, y in ((q_ref, q_hbm), (k_ref, k_hbm), (v_ref, v_hbm)):
            leaving.start(x.at[:, at], y.at[:, at])
    leaving.wait()


def unpack_grads(buf):
    return pl.pallas_call(
        unpack_grads_kernel,
        in_specs=[IN_VMEM],
        out_specs=[IN_HBM] * 3,
        out_shape=[shape(TOK, WIDTH)] * 3,
        scratch_shapes=[pltpu.VMEM((TOK, WIDTH), BF16)] * 3 + [sems(12)],
        compiler_params=params(16),
        name="unpack_grads",
    )(vmem(buf))


def query_tiles():
    tiles = [(hi, slice(2 * t, 2 * t + 2), slice(hi * HD, (hi + 1) * HD), t) for hi in range(2) for t in range(4)]
    return tiles + [(2, slice(4 * t, 4 * t + 4), slice(256, 320), t) for t in range(2)]


def key_range(hi, t):
    return (0, 768) if hi < 2 and t == 0 else (256, 1024) if hi < 2 and t == 3 else (0, 1024)


def same_segment(hi, t, split, odd, keys_seg):
    lane = lax.broadcasted_iota(jnp.int32, (1, 256), 1)
    if hi < 2:
        frame = 256 * t + lane
    else:
        frame = 512 * t + (lane >> 6) * 128 + odd * 64 + (lane & 63)
    return keys_seg == (frame >= split).astype(jnp.int32)


def attention_kernel(info_ref, buf_ref, o_hbm, lse_hbm, o_ref, lse_ref, sem):
    split, odd = info_ref[0], info_ref[1]
    keys_seg = (lax.broadcasted_iota(jnp.int32, (LEN, 1), 0) >= split).astype(jnp.int32)
    held = None
    for number, (hi, blocks, rows, t) in enumerate(query_tiles()):
        if hi != held:
            held = hi
            k = buf_ref[:, QROWS + hi * HD : QROWS + (hi + 1) * HD, :].reshape(LEN, HD)
            v = buf_ref[:, QROWS + KVROWS + hi * HD : QROWS + KVROWS + (hi + 1) * HD, :].reshape(LEN, HD)
            v_t = v.astype(F32).T.astype(BF16)
        q = buf_ref[blocks, rows, :].reshape(256, HD)
        low, high = key_range(hi, t)
        scores = lax.dot_general(k[low:high], q, NT, preferred_element_type=F32) * SCALE2
        scores = jnp.where(same_segment(hi, t, split, odd, keys_seg[low:high]), scores, -1e30)
        top = jnp.max(scores, 0, keepdims=True)
        e = jnp.exp2(scores - top)
        total = jnp.sum(e, 0, keepdims=True)
        out = dot(v_t[:, low:high], e.astype(BF16)) / total
        o_ref[blocks, rows, :] = out.T.astype(BF16).reshape(o_ref[blocks, rows, :].shape)
        lse_ref[number] = jnp.broadcast_to(top + jnp.log2(total), (8, 256))
    leaving = Copies(sem)
    leaving.start(o_ref, o_hbm)
    leaving.start(lse_ref, lse_hbm)
    leaving.wait()


def attention(info, buf):
    return pl.pallas_call(
        attention_kernel,
        in_specs=[pl.BlockSpec(memory_space=pltpu.SMEM), IN_VMEM],
        out_specs=[IN_HBM] * 2,
        out_shape=[shape(NB, QROWS, HD), shape(10, 8, 256, dtype=F32)],
        scratch_shapes=[pltpu.VMEM((NB, QROWS, HD), BF16), pltpu.VMEM((10, 8, 256), F32), sems(2)],
        compiler_params=params(40),
        name="attention",
    )(info, buf)


def attention_grad_kernel(info_ref, buf_ref, do_ref, o_ref, lse_ref, out_hbm, out_ref, sem):
    leaving = Copies(sem)
    split, odd = info_ref[0], info_ref[1]
    keys_seg = (lax.broadcasted_iota(jnp.int32, (LEN, 1), 0) >= split).astype(jnp.int32)
    held = None
    sums = None

    def flush(hi):
        k_at, v_at = QROWS + hi * HD, QROWS + KVROWS + hi * HD
        for c in range(4):
            blocks = slice(2 * c, 2 * c + 2)
            out_ref[blocks, k_at : k_at + HD, :] = (sums[c][0] * SCALE).astype(BF16).reshape(2, TOK, HD)
            out_ref[blocks, v_at : v_at + HD, :] = sums[c][1].astype(BF16).reshape(2, TOK, HD)
        for part in ((hi * HD, HD if hi < 2 else 64), (k_at, HD), (v_at, HD)):
            at = pl.ds(*part)
            leaving.start(out_ref.at[:, at, :], out_hbm.at[:, at, :])

    for number, (hi, blocks, rows, t) in enumerate(query_tiles()):
        if hi != held:
            if held is not None:
                flush(held)
            held = hi
            sums = [None] * 4
            k = buf_ref[:, QROWS + hi * HD : QROWS + (hi + 1) * HD, :].reshape(LEN, HD)
            v = buf_ref[:, QROWS + KVROWS + hi * HD : QROWS + KVROWS + (hi + 1) * HD, :].reshape(LEN, HD)
            k_t = k.astype(F32).T.astype(BF16)
        q = buf_ref[blocks, rows, :].reshape(256, HD)
        grad = do_ref[blocks, rows, :].reshape(256, HD)
        out = o_ref[blocks, rows, :].reshape(256, HD)
        delta = jnp.sum((grad.astype(F32) * out.astype(F32)).T, 0, keepdims=True)
        low, high = key_range(hi, t)
        scores = lax.dot_general(k[low:high], q, NT, preferred_element_type=F32) * SCALE2
        scores = jnp.where(same_segment(hi, t, split, odd, keys_seg[low:high]), scores, -1e30)
        probs = jnp.exp2(scores - lse_ref[number, 0:1, :])
        d_probs = lax.dot_general(v[low:high], grad, NT, preferred_element_type=F32)
        d_scores = (probs * (d_probs - delta)).astype(BF16)
        terms = (dot(d_scores, q), dot(probs.astype(BF16), grad))
        for c in range(low // 256, high // 256):
            at = slice(c * 256 - low, c * 256 - low + 256)
            parts = [term[at] for term in terms]
            sums[c] = parts if sums[c] is None else [x + y for x, y in zip(sums[c], parts)]
        d_q = (dot(k_t[:, low:high], d_scores) * SCALE).T.astype(BF16)
        out_ref[blocks, rows, :] = d_q.reshape(out_ref[blocks, rows, :].shape)
    flush(held)
    leaving.wait()


def attention_grad(info, buf, grad, out, lse):
    rows = QROWS + 2 * KVROWS
    return pl.pallas_call(
        attention_grad_kernel,
        in_specs=[pl.BlockSpec(memory_space=pltpu.SMEM)] + [IN_VMEM] * 4,
        out_specs=IN_HBM,
        out_shape=shape(NB, rows, HD),
        scratch_shapes=[pltpu.VMEM((NB, rows, HD), BF16), sems(9)],
        compiler_params=params(40),
        name="attention_grad",
    )(info, buf, grad, out, lse)


def place_kernel(ids_ref, out_ref):
    expert = lax.broadcasted_iota(jnp.int32, (EXPERTS, TOK), 0)
    chosen = ((ids_ref[0:1, :] == expert) | (ids_ref[1:2, :] == expert)).astype(F32)
    before = lax.broadcasted_iota(jnp.int32, (TOK, TOK), 0) < lax.broadcasted_iota(jnp.int32, (TOK, TOK), 1)
    slot = dot(chosen.astype(BF16), before.astype(BF16))
    slot = jnp.where(chosen > 0.5, slot, -100.0).astype(jnp.int32)
    slot = slot.reshape(EXPERTS, 1, TOK)
    row = lax.broadcasted_iota(jnp.int32, (EXPERTS, 8, TOK), 1)
    out_ref[...] = close_up((slot == row).astype(F32)).astype(BF16)


def place_rows(ids):
    return pl.pallas_call(
        place_kernel,
        out_shape=shape(EXPERTS * SLOTS, TOK),
        compiler_params=params(24),
        name="place_rows",
    )(ids)


def close_up(x):
    count = x.shape[0] // 4
    row = lax.broadcasted_iota(jnp.int32, (1, 8, HD), 1)
    x = x.reshape(count, 4, 8, HD)
    b, c, d = pltpu.roll(x[:, 1], 6, 1), pltpu.roll(x[:, 2], 4, 1), pltpu.roll(x[:, 3], 2, 1)
    parts = (jnp.where(row < 6, x[:, 0], b), jnp.where(row < 4, b, c), jnp.where(row < 2, c, d))
    return jnp.concatenate([p[:, None] for p in parts], 1).reshape(count * 24, HD)


def spread(x):
    count = x.shape[0] // 24
    row = lax.broadcasted_iota(jnp.int32, (1, 8, HD), 1)
    x = x.reshape(count, 3, 8, HD)
    b = pltpu.roll(jnp.where(row >= 6, x[:, 0], x[:, 1]), 2, 1)
    c = pltpu.roll(jnp.where(row >= 4, x[:, 1], x[:, 2]), 4, 1)
    d = pltpu.roll(x[:, 2], 6, 1)
    return jnp.concatenate([p[:, None] for p in (x[:, 0], b, c, d)], 1).reshape(count * 4, 8, HD)


GROUPS = [(slice(g * 16, g * 16 + 16), slice(g * 96, g * 96 + 96)) for g in range(4)]


def load_chunks(buf_hbm, buf_ref, arriving):
    for g in range(4):
        at = pl.ds(16 * g, 16)
        arriving.start(buf_hbm.at[at], buf_ref.at[at])
    return lambda g: arriving.started[g].wait()


def rows_from_chunks(buf_ref, out_ref, needed=lambda g: None, ready=lambda g: None):
    row = lax.broadcasted_iota(jnp.int32, (1, 8, HD), 1)
    for g, (chunks, rows) in enumerate(GROUPS):
        needed(g)

        def tile(j):
            if j == 14:
                return buf_ref[chunks, 112:120, :].astype(F32)
            pair = buf_ref[chunks, (j // 2) * 16 : (j // 2 + 1) * 16, :].astype(F32)
            return pair.reshape(16, 2, 8, HD)[:, j % 2]

        for u in range(5):
            tiles = [tile(3 * u + v) for v in range(3)]
            for v in range(3):
                out_ref[rows, cols(3 * u + v)] = close_up(tiles[v]).astype(BF16)
            r = [pltpu.roll(tiles[v], (2 + 2 * v) % 8, 1) for v in range(3)]
            extra = jnp.where(row < 2, r[0], jnp.where(row < 4, r[1], r[2]))
            out_ref[rows, cols(15 + u)] = close_up(extra).astype(BF16)
        ready(g)


def chunks_from_rows(in_ref, out_ref, out_hbm, leaving):
    row = lax.broadcasted_iota(jnp.int32, (1, 8, HD), 1)
    for g, (chunks, rows) in enumerate(GROUPS):
        before = None
        for u in range(5):
            last = spread(in_ref[rows, cols(15 + u)])
            for v in range(3):
                j = 3 * u + v
                now = jnp.where(row < 6, spread(in_ref[rows, cols(j)]), pltpu.roll(last, (6 - 2 * v) % 8, 1))
                if j % 2:
                    both = jnp.concatenate([before, now], 1).astype(BF16)
                    out_ref[chunks, (j // 2) * 16 : (j // 2 + 1) * 16, :] = both
                before = now
        out_ref[chunks, 112:120, :] = before.astype(BF16)
        at = pl.ds(16 * g, 16)
        leaving.start(out_ref.at[at], out_hbm.at[at])


def dispatch(place_ref, x_ref, rows_ref, out_ref, out_hbm, leaving):
    for c in range(5):
        at = slice(c * 512, (c + 1) * 512)
        rows_ref[:, at] = dot(place_ref[...], x_ref[:, at])
    chunks_from_rows(rows_ref, out_ref, out_hbm, leaving)
    leaving.wait()


def send_grads_kernel(place_ref, grad_ref, out_hbm, rows_ref, out_ref, sem):
    dispatch(place_ref, grad_ref, rows_ref, out_ref, out_hbm, Copies(sem))


def send_grads(place, grad):
    return pl.pallas_call(
        send_grads_kernel,
        out_specs=IN_HBM,
        out_shape=shape(EXPERTS, CHUNK, HD),
        scratch_shapes=[
            pltpu.VMEM((EXPERTS * SLOTS, WIDTH), F32),
            pltpu.VMEM((EXPERTS, CHUNK, HD), BF16),
            sems(8),
        ],
        compiler_params=params(24),
        name="send_grads",
    )(place, *hbm(grad))


def norm_kernel(place_ref, att_ref, stream_ref, gain_ref, mixed_hbm, out_hbm, mixed_ref, routed_ref, rows_ref, out_ref, sem):
    leaving = Copies(sem)
    for dev in range(NB):
        heads, shared, odd = owned(dev)
        for i, h in enumerate(heads):
            att = att_ref[dev, i * HD : (i + 1) * HD, :].astype(F32)
            mixed_ref[:, cols(h)] = (stream_ref[:, cols(h)].astype(F32) + att).astype(BF16)
        half = slice(64 * odd, 64 * odd + 64)
        att = att_ref[dev, 256:320, :].astype(F32)
        mixed_ref[half, cols(shared)] = (stream_ref[half, cols(shared)].astype(F32) + att).astype(BF16)
    leaving.start(mixed_ref, mixed_hbm)
    mixed = mixed_ref[...].astype(F32)
    rstd = lax.rsqrt(jnp.mean(mixed * mixed, -1, keepdims=True) + 1e-06)
    routed_ref[...] = (mixed * rstd * gain_ref[...]).astype(BF16)
    dispatch(place_ref, routed_ref, rows_ref, out_ref, out_hbm, leaving)


def norm_and_send(place, att, stream, gain):
    return pl.pallas_call(
        norm_kernel,
        out_specs=[IN_HBM] * 2,
        out_shape=[shape(TOK, WIDTH), shape(EXPERTS, CHUNK, HD)],
        scratch_shapes=[
            pltpu.VMEM((TOK, WIDTH), BF16),
            pltpu.VMEM((TOK, WIDTH), BF16),
            pltpu.VMEM((EXPERTS * SLOTS, WIDTH), F32),
            pltpu.VMEM((EXPERTS, CHUNK, HD), BF16),
            sems(9),
        ],
        compiler_params=params(24),
        name="norm_and_send",
    )(place, att, *hbm(stream), gain)


def unpack_into(buf_ref, rows_ref, rows_hbm, leaving, needed=lambda g: None):
    def ready(g):
        at = pl.ds(96 * g, 96)
        leaving.start(rows_ref.at[at], rows_hbm.at[at])

    rows_from_chunks(buf_ref, rows_ref, needed, ready)


def unpack_rows_kernel(buf_hbm, rows_hbm, buf_ref, rows_ref, in_sem, sem):
    leaving = Copies(sem)
    unpack_into(buf_ref, rows_ref, rows_hbm, leaving, load_chunks(buf_hbm, buf_ref, Copies(in_sem)))
    leaving.wait()


def unpack_rows(buf):
    rows = EXPERTS * SLOTS
    return pl.pallas_call(
        unpack_rows_kernel,
        in_specs=[IN_HBM],
        out_specs=IN_HBM,
        out_shape=shape(rows, WIDTH),
        scratch_shapes=[pltpu.VMEM((EXPERTS, CHUNK, HD), BF16), pltpu.VMEM((rows, WIDTH), BF16), sems(4), sems(4)],
        compiler_params=params(16),
        cost_estimate=pl.CostEstimate(flops=0, bytes_accessed=6 * MIB, transcendentals=0),
        name="unpack_rows",
    )(*hbm(buf))


def grad_rows_kernel(mine_ref, other_ref, down_ref, t_mine_hbm, t_other_hbm, t_mine_ref, t_other_ref, sem):
    leaving = Copies(sem)
    sides = ((mine_ref, t_mine_ref, t_mine_hbm), (other_ref, t_other_ref, t_other_hbm))
    for ref, t_ref, t_hbm in sides:
        for n in range(2):
            half = slice(n * 256, (n + 1) * 256)
            t_ref[:, half] = lax.dot_general(ref[...], down_ref[half, :], NT, preferred_element_type=F32)
        leaving.start(t_ref, t_hbm)
    leaving.wait()


def grad_rows(mine, other, w_down):
    rows = EXPERTS * SLOTS
    return pl.pallas_call(
        grad_rows_kernel,
        in_specs=[IN_VMEM] * 3,
        out_specs=[IN_HBM] * 2,
        out_shape=[shape(rows, HIDDEN, dtype=F32)] * 2,
        scratch_shapes=[pltpu.VMEM((rows, HIDDEN), F32)] * 2 + [sems(2)],
        compiler_params=params(32),
        cost_estimate=pl.CostEstimate(flops=4 * rows * WIDTH * HIDDEN, bytes_accessed=16 * MIB, transcendentals=0),
        name="grad_rows",
    )(*hbm(mine, other, w_down))


def expert_kernel(first, rows_ref, t_ref, w_gate_ref, w_up_ref, router_ref, gain_ref, sums_in_ref, *refs):
    *held, back_out, sums_ref = refs[:5]
    refs = refs[5:]
    if first:
        rows_hbm, refs = refs[0], refs[1:]
    d_a_ref, d_b_ref, hidden_ref, part_ref, back_ref, sem = refs[:6]
    leaving = Copies(sem)
    if first:
        unpack_into(rows_ref, refs[6], rows_hbm, leaving)
        rows_ref = refs[6]
    logit = lax.dot_general(rows_ref[...], router_ref[...], NT, preferred_element_type=F32)[:, 0:1]
    sig = jax.nn.sigmoid(logit)
    gate = sig.astype(BF16).astype(F32)
    score = None
    for n in range(2):
        half = slice(n * 256, (n + 1) * 256)
        a_val = dot(rows_ref[...], w_gate_ref[:, half])
        b_val = dot(rows_ref[...], w_up_ref[:, half])
        t_val = t_ref[:, half]
        sg = jax.nn.sigmoid(a_val)
        silu = a_val * sg
        hidden = (silu * b_val).astype(BF16).astype(F32)
        term = jnp.sum(hidden * t_val, -1, keepdims=True)
        score = term if score is None else score + term
        d_hidden = gate * t_val
        d_a_ref[:, half] = (d_hidden * b_val * sg * (1.0 + a_val * (1.0 - sg))).astype(BF16)
        d_b_ref[:, half] = (d_hidden * silu).astype(BF16)
        hidden_ref[:, half] = (gate * hidden).astype(BF16)
    for ref, target in zip((d_a_ref, d_b_ref, hidden_ref), held):
        leaving.start(ref, target)
    d_logit = score.astype(BF16).astype(F32) * sig * (1.0 - sig)
    for c in range(5):
        at = slice(c * 512, (c + 1) * 512)
        part = (
            lax.dot_general(d_a_ref[...], w_gate_ref[at, :], NT, preferred_element_type=F32)
            + lax.dot_general(d_b_ref[...], w_up_ref[at, :], NT, preferred_element_type=F32)
            + d_logit * router_ref[0:1, at].astype(F32)
        )
        part_ref[:, at] = part
        rows = rows_ref[:, at].astype(F32)
        sums_ref[0:1, at] = sums_in_ref[0:1, at] + jnp.sum(d_logit * rows, 0, keepdims=True)
        sums_ref[1:2, at] = sums_in_ref[1:2, at] + jnp.sum(part * rows, 0, keepdims=True) / gain_ref[:, at]

    chunks_from_rows(part_ref, back_ref, back_out, leaving)
    leaving.wait()


def expert_rows(first, rows_in, t_val, w_gate, w_up, router, gain, sums):
    rows = EXPERTS * SLOTS
    scratch = [pltpu.VMEM((rows, HIDDEN), BF16)] * 3
    scratch += [pltpu.VMEM((rows, WIDTH), F32), pltpu.VMEM((EXPERTS, CHUNK, HD), BF16), sems(11)]
    out_specs = [IN_HBM] * 4 + [IN_VMEM]
    out_shape = [shape(rows, HIDDEN)] * 3 + [shape(EXPERTS, CHUNK, HD), jax.ShapeDtypeStruct((2, WIDTH), F32)]
    if first:
        scratch.append(pltpu.VMEM((rows, WIDTH), BF16))
        out_specs.append(IN_HBM)
        out_shape.append(shape(rows, WIDTH))
    return pl.pallas_call(
        functools.partial(expert_kernel, first),
        in_specs=[IN_VMEM] * 7,
        out_specs=out_specs,
        out_shape=out_shape,
        scratch_shapes=scratch,
        compiler_params=params(24),
        cost_estimate=pl.CostEstimate(flops=8 * rows * WIDTH * HIDDEN, bytes_accessed=16 * MIB, transcendentals=0),
        name="expert_rows",
    )(rows_in, t_val, w_gate, w_up, router, gain, sums)


def weight_grads_kernel(ra, rb, ga, gb, daa, dab, dba, dbb, ha, hb, gate_ref, up_ref, down_ref):
    def product(first, second):
        terms = [lax.dot_general(x[...], y[...], TN, preferred_element_type=F32) for x, y in (first, second)]
        return (terms[0] + terms[1]).astype(BF16)

    gate_ref[...] = product((ra, daa), (rb, dab))
    up_ref[...] = product((ra, dba), (rb, dbb))
    down_ref[...] = product((ha, ga), (hb, gb))


def weight_grads(rows_in, grads, first, second):
    rows = EXPERTS * SLOTS
    wide = pl.BlockSpec((rows, 512), lambda i: (0, i))
    whole = pl.BlockSpec((rows, HIDDEN), lambda i: (0, 0))
    down = pl.BlockSpec((512, HIDDEN), lambda i: (i, 0))
    return pl.pallas_call(
        weight_grads_kernel,
        grid=(WIDTH // 512,),
        in_specs=[wide] * 4 + [whole] * 6,
        out_specs=[down, down, pl.BlockSpec((HIDDEN, 512), lambda i: (0, i))],
        out_shape=[shape(WIDTH, HIDDEN), shape(WIDTH, HIDDEN), shape(HIDDEN, WIDTH)],
        compiler_params=params(32),
        cost_estimate=pl.CostEstimate(flops=12 * rows * WIDTH * HIDDEN, bytes_accessed=20 * MIB, transcendentals=0),
        name="weight_grads",
    )(*hbm(*rows_in, *grads, first[0], second[0], first[1], second[1], first[2], second[2]))


def add_back_kernel(mine_hbm, other_hbm, sums_ref, out_hbm, mine_ref, other_ref, out_ref, in_sem, sem):
    arriving, leaving = Copies(in_sem), Copies(sem)
    groups = [pl.ds(g * 16, 16) for g in range(EXPERTS // 16)]
    for g in groups:
        arriving.start(mine_hbm.at[g], mine_ref.at[g])
        arriving.start(other_hbm.at[g], other_ref.at[g])
    for i, g in enumerate(groups):
        out_ref[g, 128:160, :] = jnp.broadcast_to(sums_ref[8:40, :].astype(BF16)[None], (16, 32, HD))
        arriving.started[2 * i].wait()
        arriving.started[2 * i + 1].wait()
        for t in range(7):
            at = slice(t * 16, (t + 1) * 16)
            out_ref[g, at, :] = (mine_ref[g, at, :].astype(F32) + other_ref[g, at, :].astype(F32)).astype(BF16)
        total = mine_ref[g, 112:120, :].astype(F32) + other_ref[g, 112:120, :].astype(F32)
        top = jnp.broadcast_to(sums_ref[0:8, :][None], (16, 8, HD))
        out_ref[g, 112:128, :] = jnp.concatenate([total, top], 1).astype(BF16)
        leaving.start(out_ref.at[g], out_hbm.at[g])
    leaving.wait()


def add_back(mine, other, sums):
    return pl.pallas_call(
        add_back_kernel,
        in_specs=[IN_HBM, IN_HBM, IN_VMEM],
        out_specs=IN_HBM,
        out_shape=shape(EXPERTS, BACK, HD),
        scratch_shapes=[
            pltpu.VMEM((EXPERTS, CHUNK, HD), BF16),
            pltpu.VMEM((EXPERTS, CHUNK, HD), BF16),
            pltpu.VMEM((EXPERTS, BACK, HD), BF16),
            sems(8),
            sems(4),
        ],
        compiler_params=params(16),
        name="add_back",
    )(*hbm(mine, other), sums)


def combine_kernel(place_ref, back_hbm, mixed_hbm, grad_hbm, gain_ref, stream_hbm, out_ref, tail_hbm, *scratch):
    back_ref, rows_ref, d_ref, stream_ref, grad_ref, mixed_ref, tail_ref, back_sem, sem, out_sem = scratch
    arriving, leaving = Copies(sem), Copies(out_sem)
    needed = load_chunks(back_hbm, back_ref, Copies(back_sem))
    arriving.start(mixed_hbm, mixed_ref)
    arriving.start(grad_hbm, grad_ref)
    rows_from_chunks(back_ref, rows_ref, needed)
    tail_ref[:, 0:8, :] = back_ref[:, 112:128, :].astype(F32)[:, 8:16]
    tail_ref[:, 8:40, :] = back_ref[:, 128:160, :].astype(F32)
    leaving.start(tail_ref, tail_hbm)
    for c in range(5):
        at = slice(c * 512, (c + 1) * 512)
        d_ref[:, at] = lax.dot_general(place_ref[...], rows_ref[:, at], TN, preferred_element_type=F32)
    arriving.wait()
    mixed = mixed_ref[...].astype(F32)
    rstd = lax.rsqrt(jnp.mean(mixed * mixed, -1, keepdims=True) + 1e-06)
    normed = mixed * rstd
    g = d_ref[...] * gain_ref[...]
    inner = jnp.mean(g * normed, -1, keepdims=True)
    stream_ref[...] = (grad_ref[...].astype(F32) + rstd * (g - normed * inner)).astype(BF16)
    leaving.start(stream_ref, stream_hbm)
    for dev in range(NB):
        heads, shared, odd = owned(dev)
        for i, h in enumerate(heads):
            out_ref[dev, i * HD : (i + 1) * HD, :] = stream_ref[:, cols(h)]
        out_ref[dev, 256:320, :] = stream_ref[64 * odd : 64 * odd + 64, cols(shared)]
    leaving.wait()


def combine(place, back, mixed, grad, gain):
    return pl.pallas_call(
        combine_kernel,
        in_specs=[IN_VMEM] + [IN_HBM] * 3 + [IN_VMEM],
        out_specs=[IN_HBM, IN_VMEM, IN_HBM],
        out_shape=[
            shape(TOK, WIDTH),
            jax.ShapeDtypeStruct((NB, QROWS, HD), BF16),
            shape(EXPERTS, 40, HD, dtype=F32),
        ],
        scratch_shapes=[
            pltpu.VMEM((EXPERTS, BACK, HD), BF16),
            pltpu.VMEM((EXPERTS * SLOTS, WIDTH), BF16),
            pltpu.VMEM((TOK, WIDTH), F32),
            pltpu.VMEM((TOK, WIDTH), BF16),
            pltpu.VMEM((TOK, WIDTH), BF16),
            pltpu.VMEM((TOK, WIDTH), BF16),
            pltpu.VMEM((EXPERTS, 40, HD), F32),
            sems(4),
            sems(2),
            sems(2),
        ],
        compiler_params=params(24),
        name="combine",
    )(place, *hbm(back, mixed, grad), gain)


def swap_cores(x):
    return lax.ppermute(x, "core", [(0, 1), (1, 0)])


def over_outer(x):
    return lax.all_to_all(x, "outer", split_axis=0, concat_axis=0, tiled=True)


def over_chips(x):
    return lax.all_to_all(x, ("outer", "chip"), split_axis=0, concat_axis=0, tiled=True)


def body(
    stream_in,
    queries,
    key_rows,
    value_rows,
    segment_ids,
    norm_gain,
    router_w,
    expert_ids,
    gate_w,
    up_w,
    down_w,
    out_grad,
):
    at = lax.axis_index("outer")
    split = jnp.sum((segment_ids[0] == 0).astype(jnp.int32))
    info = jnp.stack([split, at % 2]).astype(jnp.int32)
    gain = norm_gain.reshape(1, WIDTH)
    grads_local = out_grad[0]

    together = lax.optimization_barrier
    qkv = over_outer(pack_heads(queries[0], key_rows[0], value_rows[0]))
    place = place_rows(expert_ids[0].T)
    qkv, grads_buf = together((qkv, send_grads(place, grads_local)))
    grads_mine = over_chips(grads_buf)
    att, lse = attention(info, qkv)
    att, grads_mine = together((att, grads_mine))
    att_back = over_outer(att)
    mixed, rows_buf = norm_and_send(place, att_back, stream_in[0], gain)
    grads_first = unpack_rows(grads_mine)
    rows_buf, grads_first = together((rows_buf, grads_first))
    rows_mine = over_chips(rows_buf)

    expert = at * 8 + lax.axis_index("chip")
    router = jnp.broadcast_to(lax.dynamic_slice_in_dim(router_w.T, expert, 1, 0), (8, WIDTH))
    grads_second = swap_cores(grads_first)
    t_first, t_second = grad_rows(grads_first, grads_second, down_w[0])
    rows_mine, t_first, t_second, router = together((rows_mine, t_first, t_second, router))
    weights = gate_w[0], up_w[0]
    rows_other = swap_cores(rows_mine)
    rows_first = unpack_rows(rows_mine)
    rows_other, rows_first = together((rows_other, rows_first))
    nothing = jnp.zeros((2, WIDTH), F32)
    *second, back_other, sums, rows_second = expert_rows(
        True, rows_other, t_second, *weights, router, gain, nothing
    )
    back_other = swap_cores(back_other)
    *first, back_mine, sums = expert_rows(False, rows_first, t_first, *weights, router, gain, sums)
    back = over_chips(add_back(back_mine, back_other, sums.reshape(40, HD)))
    gate_grad, up_grad, down_grad = weight_grads(
        (rows_first, rows_second), (grads_first, grads_second), first, second
    )
    back, gate_grad, up_grad, down_grad = together((back, gate_grad, up_grad, down_grad))

    stream_grad, grad_heads, tail = combine(place, back, mixed, grads_local, gain)
    grad_in = over_outer(grad_heads)
    grads_buf = attention_grad(info, qkv, grad_in, att, lse)
    grads_buf, tail = together((grads_buf, tail))
    router_part = tail[:, :20].reshape(EXPERTS * 20, HD)
    gain_part = jnp.sum(tail[:, 20:], 0)
    parts = jnp.concatenate([router_part, gain_part])
    parts = parts + swap_cores(parts)
    router_grad = parts[: EXPERTS * 20].reshape(EXPERTS, WIDTH).T
    gain_grad = parts[EXPERTS * 20 :].reshape(WIDTH)
    query_grad, key_grad, value_grad = unpack_grads(over_outer(grads_buf))
    return (
        stream_grad[None],
        query_grad[None],
        key_grad[None],
        value_grad[None],
        gain_grad,
        router_grad,
        gate_grad[None],
        up_grad[None],
        down_grad[None],
    )


def solution(mesh):
    chips = Mesh(mesh.devices.reshape(8, 8, 2), ("outer", "chip", "core"))
    inner = ("chip", "core")
    every = ("outer", "chip", "core")
    frames = P(inner, "outer", None)
    pieces = P(every, None, None)
    placed = (
        frames,
        frames,
        frames,
        frames,
        P(inner, None),
        P(),
        P(),
        frames,
        pieces,
        pieces,
        pieces,
        frames,
    )
    return jax.shard_map(
        body,
        mesh=chips,
        in_specs=placed,
        out_specs=(frames, frames, frames, frames, P(), P(), pieces, pieces, pieces),
        check_vma=False,
    )
```

```python
import functools

import jax
import jax.numpy as jnp
from jax import lax
from jax.experimental import pallas as pl
from jax.experimental.pallas import tpu as pltpu
from jax.sharding import Mesh, PartitionSpec as P

F32 = jnp.float32
BF16 = jnp.bfloat16
HEADS = 20
HD = 128
NB = 8
TOK = 128
LEN = 1024
WIDTH = 2560
EXPERTS = 64
HIDDEN = 512
SLOTS = 6
QROWS = 320
KVROWS = 384
CHUNK = 120
BACK = 160
SCALE = HD**-0.5
SCALE2 = SCALE * 1.4426950408889634
NT = (((1,), (1,)), ((), ()))
TN = (((0,), (0,)), ((), ()))
MIB = 1 << 20


def params(mib):
    return pltpu.CompilerParams(vmem_limit_bytes=mib * MIB)


def shape(*dims, dtype=BF16):
    return pltpu.HBM(dims, dtype)


def kept(*dims, dtype=BF16):
    return pltpu.VMEM(dims, dtype)


def vmem(x):
    return pltpu.with_memory_space_constraint(x, pltpu.VMEM)


def hbm(*arrays):
    return [pltpu.with_memory_space_constraint(x, pltpu.HBM) for x in arrays]


class Copies:
    def __init__(self, sem):
        self.sem, self.started = sem, []

    def start(self, source, target):
        copy = pltpu.make_async_copy(source, target, self.sem.at[len(self.started)])
        copy.start()
        self.started.append(copy)
        return copy

    def wait(self):
        for copy in self.started:
            copy.wait()


IN_HBM = pl.BlockSpec(memory_space=pltpu.HBM)
IN_VMEM = pl.BlockSpec(memory_space=pltpu.VMEM)


def sems(count):
    return pltpu.SemaphoreType.DMA((count,))


def dot(a, b):
    return jnp.dot(a, b, preferred_element_type=F32)


def owned(dev):
    pair, odd = dev // 2, dev % 2
    return (5 * pair + 3 * odd, 5 * pair + 3 * odd + 1), 5 * pair + 2, odd


def cols(index):
    return slice(index * HD, (index + 1) * HD)


def pack_heads_kernel(q_hbm, k_hbm, v_hbm, out_hbm, q_ref, k_ref, v_ref, out_ref, in_sem, out_sem):
    sides = ((q_hbm, q_ref), (k_hbm, k_ref), (v_hbm, v_ref))
    at = [pl.ds(5 * HD * p, 5 * HD) for p in range(4)]
    arriving = Copies(in_sem)
    waits = [[arriving.start(x.at[:, at[p]], y.at[:, at[p]]) for x, y in sides] for p in range(4)]
    leaving = Copies(out_sem)
    for p in range(4):
        for copy in waits[p]:
            copy.wait()
        for dev in (2 * p, 2 * p + 1):
            heads, shared, odd = owned(dev)
            for i, h in enumerate(heads):
                out_ref[dev, i * HD : (i + 1) * HD, :] = q_ref[:, cols(h)]
            out_ref[dev, 256:320, :] = q_ref[64 * odd : 64 * odd + 64, cols(shared)]
            for base, ref in ((QROWS, k_ref), (QROWS + KVROWS, v_ref)):
                for i, h in enumerate(heads + (shared,)):
                    out_ref[dev, base + i * HD : base + (i + 1) * HD, :] = ref[:, cols(h)]
        both = pl.ds(2 * p, 2)
        leaving.start(out_ref.at[both], out_hbm.at[both])
    leaving.wait()


def pack_heads(q, k, v):
    rows = QROWS + 2 * KVROWS
    return pl.pallas_call(
        pack_heads_kernel,
        in_specs=[IN_HBM] * 3,
        out_specs=IN_HBM,
        out_shape=shape(NB, rows, HD),
        scratch_shapes=[pltpu.VMEM((TOK, WIDTH), BF16)] * 3 + [pltpu.VMEM((NB, rows, HD), BF16), sems(12), sems(4)],
        compiler_params=params(16),
        name="pack_heads",
    )(*hbm(q, k, v))


def unpack_grads_kernel(in_ref, q_hbm, k_hbm, v_hbm, q_ref, k_ref, v_ref, sem):
    leaving = Copies(sem)
    for p in range(4):
        for dev in (2 * p, 2 * p + 1):
            heads, shared, odd = owned(dev)
            for i, h in enumerate(heads):
                q_ref[:, cols(h)] = in_ref[dev, i * HD : (i + 1) * HD, :]
            q_ref[64 * odd : 64 * odd + 64, cols(shared)] = in_ref[dev, 256:320, :]
            for base, ref in ((QROWS, k_ref), (QROWS + KVROWS, v_ref)):
                for i, h in enumerate(heads):
                    ref[:, cols(h)] = in_ref[dev, base + i * HD : base + (i + 1) * HD, :]
        for base, ref in ((QROWS, k_ref), (QROWS + KVROWS, v_ref)):
            halves = [in_ref[2 * p + odd, base + 256 : base + 384, :].astype(F32) for odd in range(2)]
            ref[:, cols(5 * p + 2)] = (halves[0] + halves[1]).astype(BF16)
        at = pl.ds(5 * HD * p, 5 * HD)
        for x, y in ((q_ref, q_hbm), (k_ref, k_hbm), (v_ref, v_hbm)):
            leaving.start(x.at[:, at], y.at[:, at])
    leaving.wait()


def unpack_grads(buf):
    return pl.pallas_call(
        unpack_grads_kernel,
        in_specs=[IN_VMEM],
        out_specs=[IN_HBM] * 3,
        out_shape=[shape(TOK, WIDTH)] * 3,
        scratch_shapes=[pltpu.VMEM((TOK, WIDTH), BF16)] * 3 + [sems(12)],
        compiler_params=params(16),
        name="unpack_grads",
    )(vmem(buf))


def query_tiles():
    tiles = [(hi, slice(2 * t, 2 * t + 2), slice(hi * HD, (hi + 1) * HD), t) for hi in range(2) for t in range(4)]
    return tiles + [(2, slice(4 * t, 4 * t + 4), slice(256, 320), t) for t in range(2)]


def key_range(hi, t):
    return (0, 768) if hi < 2 and t == 0 else (256, 1024) if hi < 2 and t == 3 else (0, 1024)


def same_segment(hi, t, split, odd, keys_seg):
    lane = lax.broadcasted_iota(jnp.int32, (1, 256), 1)
    if hi < 2:
        frame = 256 * t + lane
    else:
        frame = 512 * t + (lane >> 6) * 128 + odd * 64 + (lane & 63)
    return keys_seg == (frame >= split).astype(jnp.int32)


def attention_kernel(info_ref, buf_ref, o_hbm, lse_hbm, o_ref, lse_ref, sem):
    split, odd = info_ref[0], info_ref[1]
    keys_seg = (lax.broadcasted_iota(jnp.int32, (LEN, 1), 0) >= split).astype(jnp.int32)
    held = None
    for number, (hi, blocks, rows, t) in enumerate(query_tiles()):
        if hi != held:
            held = hi
            k = buf_ref[:, QROWS + hi * HD : QROWS + (hi + 1) * HD, :].reshape(LEN, HD)
            v = buf_ref[:, QROWS + KVROWS + hi * HD : QROWS + KVROWS + (hi + 1) * HD, :].reshape(LEN, HD)
            v_t = v.astype(F32).T.astype(BF16)
        q = buf_ref[blocks, rows, :].reshape(256, HD)
        low, high = key_range(hi, t)
        scores = lax.dot_general(k[low:high], q, NT, preferred_element_type=F32) * SCALE2
        scores = jnp.where(same_segment(hi, t, split, odd, keys_seg[low:high]), scores, -1e30)
        top = jnp.max(scores, 0, keepdims=True)
        e = jnp.exp2(scores - top)
        total = jnp.sum(e, 0, keepdims=True)
        out = dot(v_t[:, low:high], e.astype(BF16)) / total
        o_ref[blocks, rows, :] = out.T.astype(BF16).reshape(o_ref[blocks, rows, :].shape)
        lse_ref[number] = jnp.broadcast_to(top + jnp.log2(total), (8, 256))
    leaving = Copies(sem)
    leaving.start(o_ref, o_hbm)
    leaving.start(lse_ref, lse_hbm)
    leaving.wait()


def attention(info, buf):
    return pl.pallas_call(
        attention_kernel,
        in_specs=[pl.BlockSpec(memory_space=pltpu.SMEM), IN_VMEM],
        out_specs=[IN_HBM] * 2,
        out_shape=[shape(NB, QROWS, HD), shape(10, 8, 256, dtype=F32)],
        scratch_shapes=[pltpu.VMEM((NB, QROWS, HD), BF16), pltpu.VMEM((10, 8, 256), F32), sems(2)],
        compiler_params=params(40),
        name="attention",
    )(info, buf)


def attention_grad_kernel(info_ref, buf_ref, do_ref, o_ref, lse_ref, out_hbm, out_ref, sem):
    leaving = Copies(sem)
    split, odd = info_ref[0], info_ref[1]
    keys_seg = (lax.broadcasted_iota(jnp.int32, (LEN, 1), 0) >= split).astype(jnp.int32)
    held = None
    sums = None

    def flush(hi):
        k_at, v_at = QROWS + hi * HD, QROWS + KVROWS + hi * HD
        for c in range(4):
            blocks = slice(2 * c, 2 * c + 2)
            out_ref[blocks, k_at : k_at + HD, :] = (sums[c][0] * SCALE).astype(BF16).reshape(2, TOK, HD)
            out_ref[blocks, v_at : v_at + HD, :] = sums[c][1].astype(BF16).reshape(2, TOK, HD)
        for part in ((hi * HD, HD if hi < 2 else 64), (k_at, HD), (v_at, HD)):
            at = pl.ds(*part)
            leaving.start(out_ref.at[:, at, :], out_hbm.at[:, at, :])

    for number, (hi, blocks, rows, t) in enumerate(query_tiles()):
        if hi != held:
            if held is not None:
                flush(held)
            held = hi
            sums = [None] * 4
            k = buf_ref[:, QROWS + hi * HD : QROWS + (hi + 1) * HD, :].reshape(LEN, HD)
            v = buf_ref[:, QROWS + KVROWS + hi * HD : QROWS + KVROWS + (hi + 1) * HD, :].reshape(LEN, HD)
            k_t = k.astype(F32).T.astype(BF16)
        q = buf_ref[blocks, rows, :].reshape(256, HD)
        grad = do_ref[blocks, rows, :].reshape(256, HD)
        out = o_ref[blocks, rows, :].reshape(256, HD)
        delta = jnp.sum((grad.astype(F32) * out.astype(F32)).T, 0, keepdims=True)
        low, high = key_range(hi, t)
        scores = lax.dot_general(k[low:high], q, NT, preferred_element_type=F32) * SCALE2
        scores = jnp.where(same_segment(hi, t, split, odd, keys_seg[low:high]), scores, -1e30)
        probs = jnp.exp2(scores - lse_ref[number, 0:1, :])
        d_probs = lax.dot_general(v[low:high], grad, NT, preferred_element_type=F32)
        d_scores = (probs * (d_probs - delta)).astype(BF16)
        terms = (dot(d_scores, q), dot(probs.astype(BF16), grad))
        for c in range(low // 256, high // 256):
            at = slice(c * 256 - low, c * 256 - low + 256)
            parts = [term[at] for term in terms]
            sums[c] = parts if sums[c] is None else [x + y for x, y in zip(sums[c], parts)]
        d_q = (dot(k_t[:, low:high], d_scores) * SCALE).T.astype(BF16)
        out_ref[blocks, rows, :] = d_q.reshape(out_ref[blocks, rows, :].shape)
    flush(held)
    leaving.wait()


def attention_grad(info, buf, grad, out, lse):
    rows = QROWS + 2 * KVROWS
    return pl.pallas_call(
        attention_grad_kernel,
        in_specs=[pl.BlockSpec(memory_space=pltpu.SMEM)] + [IN_VMEM] * 4,
        out_specs=IN_HBM,
        out_shape=shape(NB, rows, HD),
        scratch_shapes=[pltpu.VMEM((NB, rows, HD), BF16), sems(9)],
        compiler_params=params(40),
        name="attention_grad",
    )(info, buf, grad, out, lse)


def place_kernel(ids_ref, out_ref):
    expert = lax.broadcasted_iota(jnp.int32, (EXPERTS, TOK), 0)
    chosen = ((ids_ref[0:1, :] == expert) | (ids_ref[1:2, :] == expert)).astype(F32)
    before = lax.broadcasted_iota(jnp.int32, (TOK, TOK), 0) < lax.broadcasted_iota(jnp.int32, (TOK, TOK), 1)
    slot = dot(chosen.astype(BF16), before.astype(BF16))
    slot = jnp.where(chosen > 0.5, slot, -100.0).astype(jnp.int32)
    slot = slot.reshape(EXPERTS, 1, TOK)
    row = lax.broadcasted_iota(jnp.int32, (EXPERTS, 8, TOK), 1)
    out_ref[...] = close_up((slot == row).astype(F32)).astype(BF16)


def place_rows(ids):
    return pl.pallas_call(
        place_kernel,
        out_shape=shape(EXPERTS * SLOTS, TOK),
        compiler_params=params(24),
        name="place_rows",
    )(ids)


def close_up(x):
    count = x.shape[0] // 4
    row = lax.broadcasted_iota(jnp.int32, (1, 8, HD), 1)
    x = x.reshape(count, 4, 8, HD)
    b, c, d = pltpu.roll(x[:, 1], 6, 1), pltpu.roll(x[:, 2], 4, 1), pltpu.roll(x[:, 3], 2, 1)
    parts = (jnp.where(row < 6, x[:, 0], b), jnp.where(row < 4, b, c), jnp.where(row < 2, c, d))
    return jnp.concatenate([p[:, None] for p in parts], 1).reshape(count * 24, HD)


def spread(x):
    count = x.shape[0] // 24
    row = lax.broadcasted_iota(jnp.int32, (1, 8, HD), 1)
    x = x.reshape(count, 3, 8, HD)
    b = pltpu.roll(jnp.where(row >= 6, x[:, 0], x[:, 1]), 2, 1)
    c = pltpu.roll(jnp.where(row >= 4, x[:, 1], x[:, 2]), 4, 1)
    d = pltpu.roll(x[:, 2], 6, 1)
    return jnp.concatenate([p[:, None] for p in (x[:, 0], b, c, d)], 1).reshape(count * 4, 8, HD)


GROUPS = [(slice(g * 16, g * 16 + 16), slice(g * 96, g * 96 + 96)) for g in range(4)]


def load_chunks(buf_hbm, buf_ref, arriving):
    for g in range(4):
        at = pl.ds(16 * g, 16)
        arriving.start(buf_hbm.at[at], buf_ref.at[at])
    return lambda g: arriving.started[g].wait()


def rows_from_chunks(buf_ref, out_ref, needed=lambda g: None, ready=lambda g: None):
    row = lax.broadcasted_iota(jnp.int32, (1, 8, HD), 1)
    for g, (chunks, rows) in enumerate(GROUPS):
        needed(g)

        def tile(j):
            if j == 14:
                return buf_ref[chunks, 112:120, :].astype(F32)
            pair = buf_ref[chunks, (j // 2) * 16 : (j // 2 + 1) * 16, :].astype(F32)
            return pair.reshape(16, 2, 8, HD)[:, j % 2]

        for u in range(5):
            tiles = [tile(3 * u + v) for v in range(3)]
            for v in range(3):
                out_ref[rows, cols(3 * u + v)] = close_up(tiles[v]).astype(BF16)
            r = [pltpu.roll(tiles[v], (2 + 2 * v) % 8, 1) for v in range(3)]
            extra = jnp.where(row < 2, r[0], jnp.where(row < 4, r[1], r[2]))
            out_ref[rows, cols(15 + u)] = close_up(extra).astype(BF16)
        ready(g)


def chunks_from_rows(in_ref, out_ref, out_hbm, leaving):
    row = lax.broadcasted_iota(jnp.int32, (1, 8, HD), 1)
    for g, (chunks, rows) in enumerate(GROUPS):
        before = None
        for u in range(5):
            last = spread(in_ref[rows, cols(15 + u)])
            for v in range(3):
                j = 3 * u + v
                now = jnp.where(row < 6, spread(in_ref[rows, cols(j)]), pltpu.roll(last, (6 - 2 * v) % 8, 1))
                if j % 2:
                    both = jnp.concatenate([before, now], 1).astype(BF16)
                    out_ref[chunks, (j // 2) * 16 : (j // 2 + 1) * 16, :] = both
                before = now
        out_ref[chunks, 112:120, :] = before.astype(BF16)
        at = pl.ds(16 * g, 16)
        leaving.start(out_ref.at[at], out_hbm.at[at])


def dispatch(place_ref, x_ref, rows_ref, out_ref, out_hbm, leaving):
    for c in range(5):
        at = slice(c * 512, (c + 1) * 512)
        rows_ref[:, at] = dot(place_ref[...], x_ref[:, at])
    chunks_from_rows(rows_ref, out_ref, out_hbm, leaving)
    leaving.wait()


def send_grads_kernel(place_ref, grad_ref, out_hbm, rows_ref, out_ref, sem):
    dispatch(place_ref, grad_ref, rows_ref, out_ref, out_hbm, Copies(sem))


def send_grads(place, grad):
    return pl.pallas_call(
        send_grads_kernel,
        out_specs=IN_HBM,
        out_shape=shape(EXPERTS, CHUNK, HD),
        scratch_shapes=[
            pltpu.VMEM((EXPERTS * SLOTS, WIDTH), F32),
            pltpu.VMEM((EXPERTS, CHUNK, HD), BF16),
            sems(8),
        ],
        compiler_params=params(24),
        name="send_grads",
    )(place, *hbm(grad))


def norm_kernel(place_ref, att_ref, stream_ref, gain_ref, mixed_hbm, out_hbm, mixed_ref, routed_ref, rows_ref, out_ref, sem):
    leaving = Copies(sem)
    for dev in range(NB):
        heads, shared, odd = owned(dev)
        for i, h in enumerate(heads):
            att = att_ref[dev, i * HD : (i + 1) * HD, :].astype(F32)
            mixed_ref[:, cols(h)] = (stream_ref[:, cols(h)].astype(F32) + att).astype(BF16)
        half = slice(64 * odd, 64 * odd + 64)
        att = att_ref[dev, 256:320, :].astype(F32)
        mixed_ref[half, cols(shared)] = (stream_ref[half, cols(shared)].astype(F32) + att).astype(BF16)
    leaving.start(mixed_ref, mixed_hbm)
    mixed = mixed_ref[...].astype(F32)
    rstd = lax.rsqrt(jnp.mean(mixed * mixed, -1, keepdims=True) + 1e-06)
    routed_ref[...] = (mixed * rstd * gain_ref[...]).astype(BF16)
    dispatch(place_ref, routed_ref, rows_ref, out_ref, out_hbm, leaving)


def norm_and_send(place, att, stream, gain):
    return pl.pallas_call(
        norm_kernel,
        out_specs=[IN_HBM] * 2,
        out_shape=[shape(TOK, WIDTH), shape(EXPERTS, CHUNK, HD)],
        scratch_shapes=[
            pltpu.VMEM((TOK, WIDTH), BF16),
            pltpu.VMEM((TOK, WIDTH), BF16),
            pltpu.VMEM((EXPERTS * SLOTS, WIDTH), F32),
            pltpu.VMEM((EXPERTS, CHUNK, HD), BF16),
            sems(9),
        ],
        compiler_params=params(24),
        name="norm_and_send",
    )(place, att, *hbm(stream), gain)


def unpack_into(buf_ref, rows_ref, rows_hbm, leaving, needed=lambda g: None):
    def ready(g):
        at = pl.ds(96 * g, 96)
        leaving.start(rows_ref.at[at], rows_hbm.at[at])

    rows_from_chunks(buf_ref, rows_ref, needed, ready)


def unpack_rows_kernel(buf_hbm, rows_hbm, buf_ref, rows_ref, in_sem, sem):
    leaving = Copies(sem)
    unpack_into(buf_ref, rows_ref, rows_hbm, leaving, load_chunks(buf_hbm, buf_ref, Copies(in_sem)))
    leaving.wait()


def unpack_rows(buf):
    rows = EXPERTS * SLOTS
    return pl.pallas_call(
        unpack_rows_kernel,
        in_specs=[IN_HBM],
        out_specs=IN_HBM,
        out_shape=shape(rows, WIDTH),
        scratch_shapes=[pltpu.VMEM((EXPERTS, CHUNK, HD), BF16), pltpu.VMEM((rows, WIDTH), BF16), sems(4), sems(4)],
        compiler_params=params(16),
        cost_estimate=pl.CostEstimate(flops=0, bytes_accessed=6 * MIB, transcendentals=0),
        name="unpack_rows",
    )(*hbm(buf))


def grad_rows_kernel(mine_ref, other_ref, down_ref, t_mine_hbm, t_other_hbm, t_mine_ref, t_other_ref, sem):
    leaving = Copies(sem)
    sides = ((mine_ref, t_mine_ref, t_mine_hbm), (other_ref, t_other_ref, t_other_hbm))
    for ref, t_ref, t_hbm in sides:
        for n in range(2):
            half = slice(n * 256, (n + 1) * 256)
            t_ref[:, half] = lax.dot_general(ref[...], down_ref[half, :], NT, preferred_element_type=F32)
        leaving.start(t_ref, t_hbm)
    leaving.wait()


def grad_rows(mine, other, w_down):
    rows = EXPERTS * SLOTS
    return pl.pallas_call(
        grad_rows_kernel,
        in_specs=[IN_VMEM] * 3,
        out_specs=[IN_HBM] * 2,
        out_shape=[shape(rows, HIDDEN, dtype=F32)] * 2,
        scratch_shapes=[pltpu.VMEM((rows, HIDDEN), F32)] * 2 + [sems(2)],
        compiler_params=params(32),
        cost_estimate=pl.CostEstimate(flops=4 * rows * WIDTH * HIDDEN, bytes_accessed=16 * MIB, transcendentals=0),
        name="grad_rows",
    )(*hbm(mine, other, w_down))


def expert_kernel(first, rows_ref, t_ref, w_gate_ref, w_up_ref, router_ref, gain_ref, sums_in_ref, *refs):
    *held, back_out, sums_ref = refs[:5]
    refs = refs[5:]
    if first:
        rows_hbm, refs = refs[0], refs[1:]
    d_a_ref, d_b_ref, hidden_ref, part_ref, back_ref, sem = refs[:6]
    leaving = Copies(sem)
    if first:
        up_copy = Copies(refs[8]).start(w_up_ref, refs[7])
        w_up_ref = refs[7]
        unpack_into(rows_ref, refs[6], rows_hbm, leaving)
        rows_ref = refs[6]
    logit = lax.dot_general(rows_ref[...], router_ref[...], NT, preferred_element_type=F32)[:, 0:1]
    sig = jax.nn.sigmoid(logit)
    gate = sig.astype(BF16).astype(F32)
    score = None
    for n in range(2):
        half = slice(n * 256, (n + 1) * 256)
        a_val = dot(rows_ref[...], w_gate_ref[:, half])
        if first and n == 0:
            up_copy.wait()
        b_val = dot(rows_ref[...], w_up_ref[:, half])
        t_val = t_ref[:, half]
        sg = jax.nn.sigmoid(a_val)
        silu = a_val * sg
        hidden = (silu * b_val).astype(BF16).astype(F32)
        term = jnp.sum(hidden * t_val, -1, keepdims=True)
        score = term if score is None else score + term
        d_hidden = gate * t_val
        d_a_ref[:, half] = (d_hidden * b_val * sg * (1.0 + a_val * (1.0 - sg))).astype(BF16)
        d_b_ref[:, half] = (d_hidden * silu).astype(BF16)
        hidden_ref[:, half] = (gate * hidden).astype(BF16)
    for ref, target in zip((d_a_ref, d_b_ref, hidden_ref), held):
        leaving.start(ref, target)
    d_logit = score.astype(BF16).astype(F32) * sig * (1.0 - sig)
    for c in range(5):
        at = slice(c * 512, (c + 1) * 512)
        part = (
            lax.dot_general(d_a_ref[...], w_gate_ref[at, :], NT, preferred_element_type=F32)
            + lax.dot_general(d_b_ref[...], w_up_ref[at, :], NT, preferred_element_type=F32)
            + d_logit * router_ref[0:1, at].astype(F32)
        )
        part_ref[:, at] = part
        rows = rows_ref[:, at].astype(F32)
        sums_ref[0:1, at] = sums_in_ref[0:1, at] + jnp.sum(d_logit * rows, 0, keepdims=True)
        sums_ref[1:2, at] = sums_in_ref[1:2, at] + jnp.sum(part * rows, 0, keepdims=True) / gain_ref[:, at]

    chunks_from_rows(part_ref, back_ref, back_out, leaving)
    leaving.wait()


def expert_rows(first, rows_in, t_val, w_gate, w_up, router, gain, sums):
    rows = EXPERTS * SLOTS
    scratch = [pltpu.VMEM((rows, HIDDEN), BF16)] * 3
    scratch += [pltpu.VMEM((rows, WIDTH), F32), pltpu.VMEM((EXPERTS, CHUNK, HD), BF16), sems(11)]
    out_specs = [IN_HBM] * 4 + [IN_VMEM]
    out_shape = [shape(rows, HIDDEN)] * 3 + [shape(EXPERTS, CHUNK, HD), jax.ShapeDtypeStruct((2, WIDTH), F32)]
    if first:
        scratch += [pltpu.VMEM((rows, WIDTH), BF16), pltpu.VMEM((WIDTH, HIDDEN), BF16), sems(1)]
        (w_up,) = hbm(w_up)
        out_specs.append(IN_HBM)
        out_shape.append(shape(rows, WIDTH))
    return pl.pallas_call(
        functools.partial(expert_kernel, first),
        in_specs=[IN_VMEM] * 3 + [IN_HBM if first else IN_VMEM] + [IN_VMEM] * 3,
        out_specs=out_specs,
        out_shape=out_shape,
        scratch_shapes=scratch,
        compiler_params=params(24),
        cost_estimate=pl.CostEstimate(flops=8 * rows * WIDTH * HIDDEN, bytes_accessed=16 * MIB, transcendentals=0),
        name="expert_rows",
    )(rows_in, t_val, w_gate, w_up, router, gain, sums)


def weight_grads_kernel(ra, rb, ga, gb, daa, dab, dba, dbb, ha, hb, gate_ref, up_ref, down_ref):
    def product(first, second):
        terms = [lax.dot_general(x[...], y[...], TN, preferred_element_type=F32) for x, y in (first, second)]
        return (terms[0] + terms[1]).astype(BF16)

    gate_ref[...] = product((ra, daa), (rb, dab))
    up_ref[...] = product((ra, dba), (rb, dbb))
    down_ref[...] = product((ha, ga), (hb, gb))


def weight_grads(rows_in, grads, first, second):
    rows = EXPERTS * SLOTS
    wide = pl.BlockSpec((rows, 512), lambda i: (0, i))
    whole = pl.BlockSpec((rows, HIDDEN), lambda i: (0, 0))
    down = pl.BlockSpec((512, HIDDEN), lambda i: (i, 0))
    return pl.pallas_call(
        weight_grads_kernel,
        grid=(WIDTH // 512,),
        in_specs=[wide] * 4 + [whole] * 6,
        out_specs=[down, down, pl.BlockSpec((HIDDEN, 512), lambda i: (0, i))],
        out_shape=[shape(WIDTH, HIDDEN), shape(WIDTH, HIDDEN), shape(HIDDEN, WIDTH)],
        compiler_params=params(32),
        cost_estimate=pl.CostEstimate(flops=12 * rows * WIDTH * HIDDEN, bytes_accessed=20 * MIB, transcendentals=0),
        name="weight_grads",
    )(*hbm(*rows_in, *grads, first[0], second[0], first[1], second[1], first[2], second[2]))


def add_back_kernel(mine_hbm, other_hbm, sums_ref, out_hbm, mine_ref, other_ref, out_ref, in_sem, sem):
    arriving, leaving = Copies(in_sem), Copies(sem)
    groups = [pl.ds(g * 16, 16) for g in range(EXPERTS // 16)]
    for g in groups:
        arriving.start(mine_hbm.at[g], mine_ref.at[g])
        arriving.start(other_hbm.at[g], other_ref.at[g])
    for i, g in enumerate(groups):
        out_ref[g, 128:160, :] = jnp.broadcast_to(sums_ref[8:40, :].astype(BF16)[None], (16, 32, HD))
        arriving.started[2 * i].wait()
        arriving.started[2 * i + 1].wait()
        for t in range(7):
            at = slice(t * 16, (t + 1) * 16)
            out_ref[g, at, :] = (mine_ref[g, at, :].astype(F32) + other_ref[g, at, :].astype(F32)).astype(BF16)
        total = mine_ref[g, 112:120, :].astype(F32) + other_ref[g, 112:120, :].astype(F32)
        top = jnp.broadcast_to(sums_ref[0:8, :][None], (16, 8, HD))
        out_ref[g, 112:128, :] = jnp.concatenate([total, top], 1).astype(BF16)
        leaving.start(out_ref.at[g], out_hbm.at[g])
    leaving.wait()


def add_back(mine, other, sums):
    return pl.pallas_call(
        add_back_kernel,
        in_specs=[IN_HBM, IN_HBM, IN_VMEM],
        out_specs=IN_HBM,
        out_shape=shape(EXPERTS, BACK, HD),
        scratch_shapes=[
            pltpu.VMEM((EXPERTS, CHUNK, HD), BF16),
            pltpu.VMEM((EXPERTS, CHUNK, HD), BF16),
            pltpu.VMEM((EXPERTS, BACK, HD), BF16),
            sems(8),
            sems(4),
        ],
        compiler_params=params(16),
        name="add_back",
    )(*hbm(mine, other), sums)


def combine_kernel(place_ref, back_hbm, mixed_hbm, grad_hbm, gain_ref, stream_hbm, out_ref, tail_hbm, *scratch):
    back_ref, rows_ref, d_ref, stream_ref, grad_ref, mixed_ref, tail_ref, back_sem, sem, out_sem = scratch
    arriving, leaving = Copies(sem), Copies(out_sem)
    needed = load_chunks(back_hbm, back_ref, Copies(back_sem))
    arriving.start(mixed_hbm, mixed_ref)
    arriving.start(grad_hbm, grad_ref)
    rows_from_chunks(back_ref, rows_ref, needed)
    tail_ref[:, 0:8, :] = back_ref[:, 112:128, :].astype(F32)[:, 8:16]
    tail_ref[:, 8:40, :] = back_ref[:, 128:160, :].astype(F32)
    leaving.start(tail_ref, tail_hbm)
    for c in range(5):
        at = slice(c * 512, (c + 1) * 512)
        d_ref[:, at] = lax.dot_general(place_ref[...], rows_ref[:, at], TN, preferred_element_type=F32)
    arriving.wait()
    mixed = mixed_ref[...].astype(F32)
    rstd = lax.rsqrt(jnp.mean(mixed * mixed, -1, keepdims=True) + 1e-06)
    normed = mixed * rstd
    g = d_ref[...] * gain_ref[...]
    inner = jnp.mean(g * normed, -1, keepdims=True)
    stream_ref[...] = (grad_ref[...].astype(F32) + rstd * (g - normed * inner)).astype(BF16)
    leaving.start(stream_ref, stream_hbm)
    for dev in range(NB):
        heads, shared, odd = owned(dev)
        for i, h in enumerate(heads):
            out_ref[dev, i * HD : (i + 1) * HD, :] = stream_ref[:, cols(h)]
        out_ref[dev, 256:320, :] = stream_ref[64 * odd : 64 * odd + 64, cols(shared)]
    leaving.wait()


def combine(place, back, mixed, grad, gain):
    return pl.pallas_call(
        combine_kernel,
        in_specs=[IN_VMEM] + [IN_HBM] * 3 + [IN_VMEM],
        out_specs=[IN_HBM, IN_VMEM, IN_HBM],
        out_shape=[
            shape(TOK, WIDTH),
            jax.ShapeDtypeStruct((NB, QROWS, HD), BF16),
            shape(EXPERTS, 40, HD, dtype=F32),
        ],
        scratch_shapes=[
            pltpu.VMEM((EXPERTS, BACK, HD), BF16),
            pltpu.VMEM((EXPERTS * SLOTS, WIDTH), BF16),
            pltpu.VMEM((TOK, WIDTH), F32),
            pltpu.VMEM((TOK, WIDTH), BF16),
            pltpu.VMEM((TOK, WIDTH), BF16),
            pltpu.VMEM((TOK, WIDTH), BF16),
            pltpu.VMEM((EXPERTS, 40, HD), F32),
            sems(4),
            sems(2),
            sems(2),
        ],
        compiler_params=params(24),
        name="combine",
    )(place, *hbm(back, mixed, grad), gain)


def swap_cores(x):
    return lax.ppermute(x, "core", [(0, 1), (1, 0)])


def over_outer(x):
    return lax.all_to_all(x, "outer", split_axis=0, concat_axis=0, tiled=True)


def over_chips(x):
    return lax.all_to_all(x, ("outer", "chip"), split_axis=0, concat_axis=0, tiled=True)


def body(
    stream_in,
    queries,
    key_rows,
    value_rows,
    segment_ids,
    norm_gain,
    router_w,
    expert_ids,
    gate_w,
    up_w,
    down_w,
    out_grad,
):
    at = lax.axis_index("outer")
    split = jnp.sum((segment_ids[0] == 0).astype(jnp.int32))
    info = jnp.stack([split, at % 2]).astype(jnp.int32)
    gain = norm_gain.reshape(1, WIDTH)
    grads_local = out_grad[0]

    together = lax.optimization_barrier
    qkv = over_outer(pack_heads(queries[0], key_rows[0], value_rows[0]))
    place = place_rows(expert_ids[0].T)
    qkv, grads_buf = together((qkv, send_grads(place, grads_local)))
    grads_mine = over_chips(grads_buf)
    att, lse = attention(info, qkv)
    att, grads_mine = together((att, grads_mine))
    att_back = over_outer(att)
    mixed, rows_buf = norm_and_send(place, att_back, stream_in[0], gain)
    grads_first = unpack_rows(grads_mine)
    rows_buf, grads_first = together((rows_buf, grads_first))
    rows_mine = over_chips(rows_buf)

    expert = at * 8 + lax.axis_index("chip")
    router = jnp.broadcast_to(lax.dynamic_slice_in_dim(router_w.T, expert, 1, 0), (8, WIDTH))
    grads_second = swap_cores(grads_first)
    t_first, t_second = grad_rows(grads_first, grads_second, down_w[0])
    rows_mine, t_first, t_second, router = together((rows_mine, t_first, t_second, router))
    weights = gate_w[0], up_w[0]
    rows_other = swap_cores(rows_mine)
    rows_first = unpack_rows(rows_mine)
    rows_other, rows_first = together((rows_other, rows_first))
    nothing = jnp.zeros((2, WIDTH), F32)
    *second, back_other, sums, rows_second = expert_rows(
        True, rows_other, t_second, *weights, router, gain, nothing
    )
    back_other = swap_cores(back_other)
    *first, back_mine, sums = expert_rows(False, rows_first, t_first, *weights, router, gain, sums)
    back = over_chips(add_back(back_mine, back_other, sums.reshape(40, HD)))
    gate_grad, up_grad, down_grad = weight_grads(
        (rows_first, rows_second), (grads_first, grads_second), first, second
    )
    back, gate_grad, up_grad, down_grad = together((back, gate_grad, up_grad, down_grad))

    stream_grad, grad_heads, tail = combine(place, back, mixed, grads_local, gain)
    grad_in = over_outer(grad_heads)
    grads_buf = attention_grad(info, qkv, grad_in, att, lse)
    grads_buf, tail = together((grads_buf, tail))
    router_part = tail[:, :20].reshape(EXPERTS * 20, HD)
    gain_part = jnp.sum(tail[:, 20:], 0)
    parts = jnp.concatenate([router_part, gain_part])
    parts = parts + swap_cores(parts)
    router_grad = parts[: EXPERTS * 20].reshape(EXPERTS, WIDTH).T
    gain_grad = parts[EXPERTS * 20 :].reshape(WIDTH)
    query_grad, key_grad, value_grad = unpack_grads(over_outer(grads_buf))
    return (
        stream_grad[None],
        query_grad[None],
        key_grad[None],
        value_grad[None],
        gain_grad,
        router_grad,
        gate_grad[None],
        up_grad[None],
        down_grad[None],
    )


def solution(mesh):
    chips = Mesh(mesh.devices.reshape(8, 8, 2), ("outer", "chip", "core"))
    inner = ("chip", "core")
    every = ("outer", "chip", "core")
    frames = P(inner, "outer", None)
    pieces = P(every, None, None)
    placed = (
        frames,
        frames,
        frames,
        frames,
        P(inner, None),
        P(),
        P(),
        frames,
        pieces,
        pieces,
        pieces,
        frames,
    )
    return jax.shard_map(
        body,
        mesh=chips,
        in_specs=placed,
        out_specs=(frames, frames, frames, frames, P(), P(), pieces, pieces, pieces),
        check_vma=False,
    )
```

```python
import functools

import jax
import jax.numpy as jnp
from jax import lax
from jax.experimental import pallas as pl
from jax.experimental.pallas import tpu as pltpu
from jax.sharding import Mesh, PartitionSpec as P

F32 = jnp.float32
BF16 = jnp.bfloat16
HEADS = 20
HD = 128
NB = 8
TOK = 128
LEN = 1024
WIDTH = 2560
EXPERTS = 64
HIDDEN = 512
SLOTS = 6
QROWS = 320
KVROWS = 384
CHUNK = 120
BACK = 160
SCALE = HD**-0.5
SCALE2 = SCALE * 1.4426950408889634
NT = (((1,), (1,)), ((), ()))
TN = (((0,), (0,)), ((), ()))
MIB = 1 << 20


def params(mib):
    return pltpu.CompilerParams(vmem_limit_bytes=mib * MIB)


def shape(*dims, dtype=BF16):
    return pltpu.HBM(dims, dtype)


def kept(*dims, dtype=BF16):
    return pltpu.VMEM(dims, dtype)


def vmem(x):
    return pltpu.with_memory_space_constraint(x, pltpu.VMEM)


def hbm(*arrays):
    return [pltpu.with_memory_space_constraint(x, pltpu.HBM) for x in arrays]


class Copies:
    def __init__(self, sem):
        self.sem, self.started = sem, []

    def start(self, source, target):
        copy = pltpu.make_async_copy(source, target, self.sem.at[len(self.started)])
        copy.start()
        self.started.append(copy)
        return copy

    def wait(self):
        for copy in self.started:
            copy.wait()


IN_HBM = pl.BlockSpec(memory_space=pltpu.HBM)
IN_VMEM = pl.BlockSpec(memory_space=pltpu.VMEM)


def sems(count):
    return pltpu.SemaphoreType.DMA((count,))


def dot(a, b):
    return jnp.dot(a, b, preferred_element_type=F32)


def owned(dev):
    pair, odd = dev // 2, dev % 2
    return (5 * pair + 3 * odd, 5 * pair + 3 * odd + 1), 5 * pair + 2, odd


def cols(index):
    return slice(index * HD, (index + 1) * HD)


def pack_heads_kernel(q_hbm, k_hbm, v_hbm, out_hbm, q_ref, k_ref, v_ref, out_ref, in_sem, out_sem):
    sides = ((q_hbm, q_ref), (k_hbm, k_ref), (v_hbm, v_ref))
    at = [pl.ds(5 * HD * p, 5 * HD) for p in range(4)]
    arriving = Copies(in_sem)
    waits = [[arriving.start(x.at[:, at[p]], y.at[:, at[p]]) for x, y in sides] for p in range(4)]
    leaving = Copies(out_sem)
    for p in range(4):
        for copy in waits[p]:
            copy.wait()
        for dev in (2 * p, 2 * p + 1):
            heads, shared, odd = owned(dev)
            for i, h in enumerate(heads):
                out_ref[dev, i * HD : (i + 1) * HD, :] = q_ref[:, cols(h)]
            out_ref[dev, 256:320, :] = q_ref[64 * odd : 64 * odd + 64, cols(shared)]
            for base, ref in ((QROWS, k_ref), (QROWS + KVROWS, v_ref)):
                for i, h in enumerate(heads + (shared,)):
                    out_ref[dev, base + i * HD : base + (i + 1) * HD, :] = ref[:, cols(h)]
        both = pl.ds(2 * p, 2)
        leaving.start(out_ref.at[both], out_hbm.at[both])
    leaving.wait()


def pack_heads(q, k, v):
    rows = QROWS + 2 * KVROWS
    return pl.pallas_call(
        pack_heads_kernel,
        in_specs=[IN_HBM] * 3,
        out_specs=IN_HBM,
        out_shape=shape(NB, rows, HD),
        scratch_shapes=[pltpu.VMEM((TOK, WIDTH), BF16)] * 3 + [pltpu.VMEM((NB, rows, HD), BF16), sems(12), sems(4)],
        compiler_params=params(16),
        name="pack_heads",
    )(*hbm(q, k, v))


def unpack_grads_kernel(in_ref, q_hbm, k_hbm, v_hbm, q_ref, k_ref, v_ref, sem):
    leaving = Copies(sem)
    for p in range(4):
        for dev in (2 * p, 2 * p + 1):
            heads, shared, odd = owned(dev)
            for i, h in enumerate(heads):
                q_ref[:, cols(h)] = in_ref[dev, i * HD : (i + 1) * HD, :]
            q_ref[64 * odd : 64 * odd + 64, cols(shared)] = in_ref[dev, 256:320, :]
            for base, ref in ((QROWS, k_ref), (QROWS + KVROWS, v_ref)):
                for i, h in enumerate(heads):
                    ref[:, cols(h)] = in_ref[dev, base + i * HD : base + (i + 1) * HD, :]
        for base, ref in ((QROWS, k_ref), (QROWS + KVROWS, v_ref)):
            halves = [in_ref[2 * p + odd, base + 256 : base + 384, :].astype(F32) for odd in range(2)]
            ref[:, cols(5 * p + 2)] = (halves[0] + halves[1]).astype(BF16)
        at = pl.ds(5 * HD * p, 5 * HD)
        for x, y in ((q_ref, q_hbm), (k_ref, k_hbm), (v_ref, v_hbm)):
            leaving.start(x.at[:, at], y.at[:, at])
    leaving.wait()


def unpack_grads(buf):
    return pl.pallas_call(
        unpack_grads_kernel,
        in_specs=[IN_VMEM],
        out_specs=[IN_HBM] * 3,
        out_shape=[shape(TOK, WIDTH)] * 3,
        scratch_shapes=[pltpu.VMEM((TOK, WIDTH), BF16)] * 3 + [sems(12)],
        compiler_params=params(16),
        name="unpack_grads",
    )(vmem(buf))


def query_tiles():
    tiles = [(hi, slice(2 * t, 2 * t + 2), slice(hi * HD, (hi + 1) * HD), t) for hi in range(2) for t in range(4)]
    return tiles + [(2, slice(4 * t, 4 * t + 4), slice(256, 320), t) for t in range(2)]


def key_range(hi, t):
    return (0, 768) if hi < 2 and t == 0 else (256, 1024) if hi < 2 and t == 3 else (0, 1024)


def same_segment(hi, t, split, odd, keys_seg):
    lane = lax.broadcasted_iota(jnp.int32, (1, 256), 1)
    if hi < 2:
        frame = 256 * t + lane
    else:
        frame = 512 * t + (lane >> 6) * 128 + odd * 64 + (lane & 63)
    return keys_seg == (frame >= split).astype(jnp.int32)


def attention_kernel(info_ref, buf_ref, o_hbm, lse_hbm, o_ref, lse_ref, sem):
    split, odd = info_ref[0], info_ref[1]
    keys_seg = (lax.broadcasted_iota(jnp.int32, (LEN, 1), 0) >= split).astype(jnp.int32)
    held = None
    for number, (hi, blocks, rows, t) in enumerate(query_tiles()):
        if hi != held:
            held = hi
            k = buf_ref[:, QROWS + hi * HD : QROWS + (hi + 1) * HD, :].reshape(LEN, HD)
            v = buf_ref[:, QROWS + KVROWS + hi * HD : QROWS + KVROWS + (hi + 1) * HD, :].reshape(LEN, HD)
            v_t = v.astype(F32).T.astype(BF16)
        q = buf_ref[blocks, rows, :].reshape(256, HD)
        low, high = key_range(hi, t)
        scores = lax.dot_general(k[low:high], q, NT, preferred_element_type=F32) * SCALE2
        scores = jnp.where(same_segment(hi, t, split, odd, keys_seg[low:high]), scores, -1e30)
        top = jnp.max(scores, 0, keepdims=True)
        e = jnp.exp2(scores - top)
        total = jnp.sum(e, 0, keepdims=True)
        out = dot(v_t[:, low:high], e.astype(BF16)) / total
        o_ref[blocks, rows, :] = out.T.astype(BF16).reshape(o_ref[blocks, rows, :].shape)
        lse_ref[number] = jnp.broadcast_to(top + jnp.log2(total), (8, 256))
    leaving = Copies(sem)
    leaving.start(o_ref, o_hbm)
    leaving.start(lse_ref, lse_hbm)
    leaving.wait()


def attention(info, buf):
    return pl.pallas_call(
        attention_kernel,
        in_specs=[pl.BlockSpec(memory_space=pltpu.SMEM), IN_VMEM],
        out_specs=[IN_HBM] * 2,
        out_shape=[shape(NB, QROWS, HD), shape(10, 8, 256, dtype=F32)],
        scratch_shapes=[pltpu.VMEM((NB, QROWS, HD), BF16), pltpu.VMEM((10, 8, 256), F32), sems(2)],
        compiler_params=params(40),
        name="attention",
    )(info, buf)


def attention_grad_kernel(info_ref, buf_ref, do_ref, o_ref, lse_ref, out_hbm, out_ref, sem):
    leaving = Copies(sem)
    split, odd = info_ref[0], info_ref[1]
    keys_seg = (lax.broadcasted_iota(jnp.int32, (LEN, 1), 0) >= split).astype(jnp.int32)
    held = None
    sums = None

    def flush(hi):
        k_at, v_at = QROWS + hi * HD, QROWS + KVROWS + hi * HD
        for c in range(4):
            blocks = slice(2 * c, 2 * c + 2)
            out_ref[blocks, k_at : k_at + HD, :] = (sums[c][0] * SCALE).astype(BF16).reshape(2, TOK, HD)
            out_ref[blocks, v_at : v_at + HD, :] = sums[c][1].astype(BF16).reshape(2, TOK, HD)
        for part in ((hi * HD, HD if hi < 2 else 64), (k_at, HD), (v_at, HD)):
            at = pl.ds(*part)
            leaving.start(out_ref.at[:, at, :], out_hbm.at[:, at, :])

    for number, (hi, blocks, rows, t) in enumerate(query_tiles()):
        if hi != held:
            if held is not None:
                flush(held)
            held = hi
            sums = [None] * 4
            k = buf_ref[:, QROWS + hi * HD : QROWS + (hi + 1) * HD, :].reshape(LEN, HD)
            v = buf_ref[:, QROWS + KVROWS + hi * HD : QROWS + KVROWS + (hi + 1) * HD, :].reshape(LEN, HD)
            k_t = k.astype(F32).T.astype(BF16)
        q = buf_ref[blocks, rows, :].reshape(256, HD)
        grad = do_ref[blocks, rows, :].reshape(256, HD)
        out = o_ref[blocks, rows, :].reshape(256, HD)
        delta = jnp.sum((grad.astype(F32) * out.astype(F32)).T, 0, keepdims=True)
        low, high = key_range(hi, t)
        scores = lax.dot_general(k[low:high], q, NT, preferred_element_type=F32) * SCALE2
        scores = jnp.where(same_segment(hi, t, split, odd, keys_seg[low:high]), scores, -1e30)
        probs = jnp.exp2(scores - lse_ref[number, 0:1, :])
        d_probs = lax.dot_general(v[low:high], grad, NT, preferred_element_type=F32)
        d_scores = (probs * (d_probs - delta)).astype(BF16)
        terms = (dot(d_scores, q), dot(probs.astype(BF16), grad))
        for c in range(low // 256, high // 256):
            at = slice(c * 256 - low, c * 256 - low + 256)
            parts = [term[at] for term in terms]
            sums[c] = parts if sums[c] is None else [x + y for x, y in zip(sums[c], parts)]
        d_q = (dot(k_t[:, low:high], d_scores) * SCALE).T.astype(BF16)
        out_ref[blocks, rows, :] = d_q.reshape(out_ref[blocks, rows, :].shape)
    flush(held)
    leaving.wait()


def attention_grad(info, buf, grad, out, lse):
    rows = QROWS + 2 * KVROWS
    return pl.pallas_call(
        attention_grad_kernel,
        in_specs=[pl.BlockSpec(memory_space=pltpu.SMEM)] + [IN_VMEM] * 4,
        out_specs=IN_HBM,
        out_shape=shape(NB, rows, HD),
        scratch_shapes=[pltpu.VMEM((NB, rows, HD), BF16), sems(9)],
        compiler_params=params(40),
        name="attention_grad",
    )(info, buf, grad, out, lse)


def place_kernel(ids_ref, out_ref):
    expert = lax.broadcasted_iota(jnp.int32, (EXPERTS, TOK), 0)
    chosen = ((ids_ref[0:1, :] == expert) | (ids_ref[1:2, :] == expert)).astype(F32)
    before = lax.broadcasted_iota(jnp.int32, (TOK, TOK), 0) < lax.broadcasted_iota(jnp.int32, (TOK, TOK), 1)
    slot = dot(chosen.astype(BF16), before.astype(BF16))
    slot = jnp.where(chosen > 0.5, slot, -100.0).astype(jnp.int32)
    slot = slot.reshape(EXPERTS, 1, TOK)
    row = lax.broadcasted_iota(jnp.int32, (EXPERTS, 8, TOK), 1)
    out_ref[...] = close_up((slot == row).astype(F32)).astype(BF16)


def place_rows(ids):
    return pl.pallas_call(
        place_kernel,
        out_shape=shape(EXPERTS * SLOTS, TOK),
        compiler_params=params(24),
        name="place_rows",
    )(ids)


def close_up(x):
    count = x.shape[0] // 4
    row = lax.broadcasted_iota(jnp.int32, (1, 8, HD), 1)
    x = x.reshape(count, 4, 8, HD)
    b, c, d = pltpu.roll(x[:, 1], 6, 1), pltpu.roll(x[:, 2], 4, 1), pltpu.roll(x[:, 3], 2, 1)
    parts = (jnp.where(row < 6, x[:, 0], b), jnp.where(row < 4, b, c), jnp.where(row < 2, c, d))
    return jnp.concatenate([p[:, None] for p in parts], 1).reshape(count * 24, HD)


def spread(x):
    count = x.shape[0] // 24
    row = lax.broadcasted_iota(jnp.int32, (1, 8, HD), 1)
    x = x.reshape(count, 3, 8, HD)
    b = pltpu.roll(jnp.where(row >= 6, x[:, 0], x[:, 1]), 2, 1)
    c = pltpu.roll(jnp.where(row >= 4, x[:, 1], x[:, 2]), 4, 1)
    d = pltpu.roll(x[:, 2], 6, 1)
    return jnp.concatenate([p[:, None] for p in (x[:, 0], b, c, d)], 1).reshape(count * 4, 8, HD)


GROUPS = [(slice(g * 16, g * 16 + 16), slice(g * 96, g * 96 + 96)) for g in range(4)]


def load_chunks(buf_hbm, buf_ref, arriving):
    for g in range(4):
        at = pl.ds(16 * g, 16)
        arriving.start(buf_hbm.at[at], buf_ref.at[at])
    return lambda g: arriving.started[g].wait()


def rows_from_chunks(buf_ref, out_ref, needed=lambda g: None, ready=lambda g: None):
    row = lax.broadcasted_iota(jnp.int32, (1, 8, HD), 1)
    for g, (chunks, rows) in enumerate(GROUPS):
        needed(g)

        def tile(j):
            if j == 14:
                return buf_ref[chunks, 112:120, :].astype(F32)
            pair = buf_ref[chunks, (j // 2) * 16 : (j // 2 + 1) * 16, :].astype(F32)
            return pair.reshape(16, 2, 8, HD)[:, j % 2]

        for u in range(5):
            tiles = [tile(3 * u + v) for v in range(3)]
            for v in range(3):
                out_ref[rows, cols(3 * u + v)] = close_up(tiles[v]).astype(BF16)
            r = [pltpu.roll(tiles[v], (2 + 2 * v) % 8, 1) for v in range(3)]
            extra = jnp.where(row < 2, r[0], jnp.where(row < 4, r[1], r[2]))
            out_ref[rows, cols(15 + u)] = close_up(extra).astype(BF16)
        ready(g)


def chunks_from_rows(in_ref, out_ref, out_hbm, leaving):
    row = lax.broadcasted_iota(jnp.int32, (1, 8, HD), 1)
    for g, (chunks, rows) in enumerate(GROUPS):
        before = None
        for u in range(5):
            last = spread(in_ref[rows, cols(15 + u)])
            for v in range(3):
                j = 3 * u + v
                now = jnp.where(row < 6, spread(in_ref[rows, cols(j)]), pltpu.roll(last, (6 - 2 * v) % 8, 1))
                if j % 2:
                    both = jnp.concatenate([before, now], 1).astype(BF16)
                    out_ref[chunks, (j // 2) * 16 : (j // 2 + 1) * 16, :] = both
                before = now
        out_ref[chunks, 112:120, :] = before.astype(BF16)
        at = pl.ds(16 * g, 16)
        leaving.start(out_ref.at[at], out_hbm.at[at])


def dispatch(place_ref, x_ref, rows_ref, out_ref, out_hbm, leaving):
    for c in range(5):
        at = slice(c * 512, (c + 1) * 512)
        rows_ref[:, at] = dot(place_ref[...], x_ref[:, at])
    chunks_from_rows(rows_ref, out_ref, out_hbm, leaving)
    leaving.wait()


def send_grads_kernel(place_ref, grad_ref, out_hbm, rows_ref, out_ref, sem):
    dispatch(place_ref, grad_ref, rows_ref, out_ref, out_hbm, Copies(sem))


def send_grads(place, grad):
    return pl.pallas_call(
        send_grads_kernel,
        out_specs=IN_HBM,
        out_shape=shape(EXPERTS, CHUNK, HD),
        scratch_shapes=[
            pltpu.VMEM((EXPERTS * SLOTS, WIDTH), F32),
            pltpu.VMEM((EXPERTS, CHUNK, HD), BF16),
            sems(8),
        ],
        compiler_params=params(24),
        name="send_grads",
    )(place, *hbm(grad))


def norm_kernel(place_ref, att_ref, stream_ref, gain_ref, mixed_hbm, out_hbm, mixed_ref, routed_ref, rows_ref, out_ref, sem):
    leaving = Copies(sem)
    for dev in range(NB):
        heads, shared, odd = owned(dev)
        for i, h in enumerate(heads):
            att = att_ref[dev, i * HD : (i + 1) * HD, :].astype(F32)
            mixed_ref[:, cols(h)] = (stream_ref[:, cols(h)].astype(F32) + att).astype(BF16)
        half = slice(64 * odd, 64 * odd + 64)
        att = att_ref[dev, 256:320, :].astype(F32)
        mixed_ref[half, cols(shared)] = (stream_ref[half, cols(shared)].astype(F32) + att).astype(BF16)
    leaving.start(mixed_ref, mixed_hbm)
    mixed = mixed_ref[...].astype(F32)
    rstd = lax.rsqrt(jnp.mean(mixed * mixed, -1, keepdims=True) + 1e-06)
    routed_ref[...] = (mixed * rstd * gain_ref[...]).astype(BF16)
    dispatch(place_ref, routed_ref, rows_ref, out_ref, out_hbm, leaving)


def norm_and_send(place, att, stream, gain):
    return pl.pallas_call(
        norm_kernel,
        out_specs=[IN_HBM] * 2,
        out_shape=[shape(TOK, WIDTH), shape(EXPERTS, CHUNK, HD)],
        scratch_shapes=[
            pltpu.VMEM((TOK, WIDTH), BF16),
            pltpu.VMEM((TOK, WIDTH), BF16),
            pltpu.VMEM((EXPERTS * SLOTS, WIDTH), F32),
            pltpu.VMEM((EXPERTS, CHUNK, HD), BF16),
            sems(9),
        ],
        compiler_params=params(24),
        name="norm_and_send",
    )(place, att, *hbm(stream), gain)


def unpack_into(buf_ref, rows_ref, rows_hbm, leaving, needed=lambda g: None):
    def ready(g):
        at = pl.ds(96 * g, 96)
        leaving.start(rows_ref.at[at], rows_hbm.at[at])

    rows_from_chunks(buf_ref, rows_ref, needed, ready)


def unpack_rows_kernel(buf_hbm, rows_hbm, buf_ref, rows_ref, in_sem, sem):
    leaving = Copies(sem)
    unpack_into(buf_ref, rows_ref, rows_hbm, leaving, load_chunks(buf_hbm, buf_ref, Copies(in_sem)))
    leaving.wait()


def unpack_rows(buf):
    rows = EXPERTS * SLOTS
    return pl.pallas_call(
        unpack_rows_kernel,
        in_specs=[IN_HBM],
        out_specs=IN_HBM,
        out_shape=shape(rows, WIDTH),
        scratch_shapes=[pltpu.VMEM((EXPERTS, CHUNK, HD), BF16), pltpu.VMEM((rows, WIDTH), BF16), sems(4), sems(4)],
        compiler_params=params(16),
        cost_estimate=pl.CostEstimate(flops=0, bytes_accessed=6 * MIB, transcendentals=0),
        name="unpack_rows",
    )(*hbm(buf))


def grad_rows_kernel(mine_ref, other_ref, down_ref, t_mine_hbm, t_other_hbm, t_mine_ref, t_other_ref, sem):
    leaving = Copies(sem)
    sides = ((mine_ref, t_mine_ref, t_mine_hbm), (other_ref, t_other_ref, t_other_hbm))
    for ref, t_ref, t_hbm in sides:
        for n in range(2):
            half = slice(n * 256, (n + 1) * 256)
            t_ref[:, half] = lax.dot_general(ref[...], down_ref[half, :], NT, preferred_element_type=F32)
        leaving.start(t_ref, t_hbm)
    leaving.wait()


def grad_rows(mine, other, w_down):
    rows = EXPERTS * SLOTS
    return pl.pallas_call(
        grad_rows_kernel,
        in_specs=[IN_VMEM] * 3,
        out_specs=[IN_HBM] * 2,
        out_shape=[shape(rows, HIDDEN, dtype=F32)] * 2,
        scratch_shapes=[pltpu.VMEM((rows, HIDDEN), F32)] * 2 + [sems(2)],
        compiler_params=params(32),
        cost_estimate=pl.CostEstimate(flops=4 * rows * WIDTH * HIDDEN, bytes_accessed=16 * MIB, transcendentals=0),
        name="grad_rows",
    )(*hbm(mine, other, w_down))


def expert_kernel(first, rows_ref, t_ref, w_gate_ref, w_up_ref, router_ref, gain_ref, sums_in_ref, *refs):
    *held, back_out, sums_ref = refs[:5]
    refs = refs[5:]
    if first:
        rows_hbm, refs = refs[0], refs[1:]
    d_a_ref, d_b_ref, hidden_ref, part_ref, back_ref, sem = refs[:6]
    leaving = Copies(sem)
    if first:
        up_copy = Copies(refs[8]).start(w_up_ref, refs[7])
        w_up_ref = refs[7]
        unpack_into(rows_ref, refs[6], rows_hbm, leaving)
        rows_ref = refs[6]
    logit = lax.dot_general(rows_ref[...], router_ref[...], NT, preferred_element_type=F32)[:, 0:1]
    sig = jax.nn.sigmoid(logit)
    gate = sig.astype(BF16).astype(F32)
    score = None
    for n in range(2):
        half = slice(n * 256, (n + 1) * 256)
        a_val = dot(rows_ref[...], w_gate_ref[:, half])
        if first and n == 0:
            up_copy.wait()
        b_val = dot(rows_ref[...], w_up_ref[:, half])
        t_val = t_ref[:, half]
        sg = jax.nn.sigmoid(a_val)
        silu = a_val * sg
        hidden = (silu * b_val).astype(BF16).astype(F32)
        term = jnp.sum(hidden * t_val, -1, keepdims=True)
        score = term if score is None else score + term
        d_hidden = gate * t_val
        d_a_ref[:, half] = (d_hidden * b_val * sg * (1.0 + a_val * (1.0 - sg))).astype(BF16)
        d_b_ref[:, half] = (d_hidden * silu).astype(BF16)
        hidden_ref[:, half] = (gate * hidden).astype(BF16)
    for ref, target in zip((d_a_ref, d_b_ref, hidden_ref), held):
        leaving.start(ref, target)
    d_logit = score.astype(BF16).astype(F32) * sig * (1.0 - sig)
    for c in range(5):
        at = slice(c * 512, (c + 1) * 512)
        part = (
            lax.dot_general(d_a_ref[...], w_gate_ref[at, :], NT, preferred_element_type=F32)
            + lax.dot_general(d_b_ref[...], w_up_ref[at, :], NT, preferred_element_type=F32)
            + d_logit * router_ref[0:1, at].astype(F32)
        )
        part_ref[:, at] = part
        rows = rows_ref[:, at].astype(F32)
        sums_ref[0:1, at] = sums_in_ref[0:1, at] + jnp.sum(d_logit * rows, 0, keepdims=True)
        sums_ref[1:2, at] = sums_in_ref[1:2, at] + jnp.sum(part * rows, 0, keepdims=True) / gain_ref[:, at]

    chunks_from_rows(part_ref, back_ref, back_out, leaving)
    leaving.wait()


def expert_rows(first, rows_in, t_val, w_gate, w_up, router, gain, sums):
    rows = EXPERTS * SLOTS
    scratch = [pltpu.VMEM((rows, HIDDEN), BF16)] * 3
    scratch += [pltpu.VMEM((rows, WIDTH), F32), pltpu.VMEM((EXPERTS, CHUNK, HD), BF16), sems(11)]
    out_specs = [IN_HBM] * 4 + [IN_VMEM]
    out_shape = [shape(rows, HIDDEN)] * 3 + [shape(EXPERTS, CHUNK, HD), jax.ShapeDtypeStruct((2, WIDTH), F32)]
    if first:
        scratch += [pltpu.VMEM((rows, WIDTH), BF16), pltpu.VMEM((WIDTH, HIDDEN), BF16), sems(1)]
        (w_up,) = hbm(w_up)
        out_specs.append(IN_HBM)
        out_shape.append(shape(rows, WIDTH))
    return pl.pallas_call(
        functools.partial(expert_kernel, first),
        in_specs=[IN_VMEM] * 3 + [IN_HBM if first else IN_VMEM] + [IN_VMEM] * 3,
        out_specs=out_specs,
        out_shape=out_shape,
        scratch_shapes=scratch,
        compiler_params=params(24),
        cost_estimate=pl.CostEstimate(flops=8 * rows * WIDTH * HIDDEN, bytes_accessed=16 * MIB, transcendentals=0),
        name="expert_rows",
    )(rows_in, t_val, w_gate, w_up, router, gain, sums)


def weight_grads_kernel(ra, rb, ga, gb, daa, dab, dba, dbb, ha, hb, gate_ref, up_ref, down_ref):
    def product(first, second):
        terms = [lax.dot_general(x[...], y[...], TN, preferred_element_type=F32) for x, y in (first, second)]
        return (terms[0] + terms[1]).astype(BF16)

    gate_ref[...] = product((ra, daa), (rb, dab))
    up_ref[...] = product((ra, dba), (rb, dbb))
    down_ref[...] = product((ha, ga), (hb, gb))


def weight_grads(rows_in, grads, first, second):
    rows = EXPERTS * SLOTS
    wide = pl.BlockSpec((rows, 512), lambda i: (0, i))
    whole = pl.BlockSpec((rows, HIDDEN), lambda i: (0, 0))
    down = pl.BlockSpec((512, HIDDEN), lambda i: (i, 0))
    return pl.pallas_call(
        weight_grads_kernel,
        grid=(WIDTH // 512,),
        in_specs=[wide] * 4 + [whole] * 6,
        out_specs=[down, down, pl.BlockSpec((HIDDEN, 512), lambda i: (0, i))],
        out_shape=[shape(WIDTH, HIDDEN), shape(WIDTH, HIDDEN), shape(HIDDEN, WIDTH)],
        compiler_params=params(32),
        cost_estimate=pl.CostEstimate(flops=12 * rows * WIDTH * HIDDEN, bytes_accessed=20 * MIB, transcendentals=0),
        name="weight_grads",
    )(*hbm(*rows_in, *grads, first[0], second[0], first[1], second[1], first[2], second[2]))


def add_back_kernel(mine_hbm, other_hbm, sums_ref, out_hbm, mine_ref, other_ref, out_ref, in_sem, sem):
    arriving, leaving = Copies(in_sem), Copies(sem)
    groups = [pl.ds(g * 16, 16) for g in range(EXPERTS // 16)]
    for g in groups:
        arriving.start(mine_hbm.at[g], mine_ref.at[g])
        arriving.start(other_hbm.at[g], other_ref.at[g])
    sums = jnp.concatenate([sums_ref[i : i + 1, cols(c)] for i in range(2) for c in range(20)], 0)
    for i, g in enumerate(groups):
        out_ref[g, 128:160, :] = jnp.broadcast_to(sums[8:40].astype(BF16)[None], (16, 32, HD))
        arriving.started[2 * i].wait()
        arriving.started[2 * i + 1].wait()
        for t in range(7):
            at = slice(t * 16, (t + 1) * 16)
            out_ref[g, at, :] = (mine_ref[g, at, :].astype(F32) + other_ref[g, at, :].astype(F32)).astype(BF16)
        total = mine_ref[g, 112:120, :].astype(F32) + other_ref[g, 112:120, :].astype(F32)
        top = jnp.broadcast_to(sums[0:8][None], (16, 8, HD))
        out_ref[g, 112:128, :] = jnp.concatenate([total, top], 1).astype(BF16)
        leaving.start(out_ref.at[g], out_hbm.at[g])
    leaving.wait()


def add_back(mine, other, sums):
    return pl.pallas_call(
        add_back_kernel,
        in_specs=[IN_HBM, IN_HBM, IN_VMEM],
        out_specs=IN_HBM,
        out_shape=shape(EXPERTS, BACK, HD),
        scratch_shapes=[
            pltpu.VMEM((EXPERTS, CHUNK, HD), BF16),
            pltpu.VMEM((EXPERTS, CHUNK, HD), BF16),
            pltpu.VMEM((EXPERTS, BACK, HD), BF16),
            sems(8),
            sems(4),
        ],
        compiler_params=params(16),
        name="add_back",
    )(*hbm(mine, other), sums)


def combine_kernel(place_ref, back_hbm, mixed_hbm, grad_hbm, gain_ref, stream_hbm, out_ref, *scratch):
    back_ref, rows_ref, d_ref, stream_ref, grad_ref, mixed_ref, back_sem, sem, out_sem = scratch
    arriving, leaving = Copies(sem), Copies(out_sem)
    needed = load_chunks(back_hbm, back_ref, Copies(back_sem))
    arriving.start(mixed_hbm, mixed_ref)
    arriving.start(grad_hbm, grad_ref)
    rows_from_chunks(back_ref, rows_ref, needed)
    for c in range(5):
        at = slice(c * 512, (c + 1) * 512)
        d_ref[:, at] = lax.dot_general(place_ref[...], rows_ref[:, at], TN, preferred_element_type=F32)
    arriving.wait()
    mixed = mixed_ref[...].astype(F32)
    rstd = lax.rsqrt(jnp.mean(mixed * mixed, -1, keepdims=True) + 1e-06)
    normed = mixed * rstd
    g = d_ref[...] * gain_ref[...]
    inner = jnp.mean(g * normed, -1, keepdims=True)
    stream_ref[...] = (grad_ref[...].astype(F32) + rstd * (g - normed * inner)).astype(BF16)
    leaving.start(stream_ref, stream_hbm)
    for dev in range(NB):
        heads, shared, odd = owned(dev)
        for i, h in enumerate(heads):
            out_ref[dev, i * HD : (i + 1) * HD, :] = stream_ref[:, cols(h)]
        out_ref[dev, 256:320, :] = stream_ref[64 * odd : 64 * odd + 64, cols(shared)]
    leaving.wait()


def combine(place, back, mixed, grad, gain):
    return pl.pallas_call(
        combine_kernel,
        in_specs=[IN_VMEM] + [IN_HBM] * 3 + [IN_VMEM],
        out_specs=[IN_HBM, IN_VMEM],
        out_shape=[
            shape(TOK, WIDTH),
            jax.ShapeDtypeStruct((NB, QROWS, HD), BF16),
        ],
        scratch_shapes=[
            pltpu.VMEM((EXPERTS, BACK, HD), BF16),
            pltpu.VMEM((EXPERTS * SLOTS, WIDTH), BF16),
            pltpu.VMEM((TOK, WIDTH), F32),
            pltpu.VMEM((TOK, WIDTH), BF16),
            pltpu.VMEM((TOK, WIDTH), BF16),
            pltpu.VMEM((TOK, WIDTH), BF16),
            sems(4),
            sems(2),
            sems(2),
        ],
        compiler_params=params(24),
        name="combine",
    )(place, *hbm(back, mixed, grad), gain)


def swap_cores(x):
    return lax.ppermute(x, "core", [(0, 1), (1, 0)])


def over_outer(x):
    return lax.all_to_all(x, "outer", split_axis=0, concat_axis=0, tiled=True)


def over_chips(x):
    return lax.all_to_all(x, ("outer", "chip"), split_axis=0, concat_axis=0, tiled=True)


def body(
    stream_in,
    queries,
    key_rows,
    value_rows,
    segment_ids,
    norm_gain,
    router_w,
    expert_ids,
    gate_w,
    up_w,
    down_w,
    out_grad,
):
    at = lax.axis_index("outer")
    split = jnp.sum((segment_ids[0] == 0).astype(jnp.int32))
    info = jnp.stack([split, at % 2]).astype(jnp.int32)
    gain = norm_gain.reshape(1, WIDTH)
    grads_local = out_grad[0]

    together = lax.optimization_barrier
    qkv = over_outer(pack_heads(queries[0], key_rows[0], value_rows[0]))
    place = place_rows(expert_ids[0].T)
    qkv, grads_buf = together((qkv, send_grads(place, grads_local)))
    grads_mine = over_chips(grads_buf)
    att, lse = attention(info, qkv)
    att, grads_mine = together((att, grads_mine))
    att_back = over_outer(att)
    mixed, rows_buf = norm_and_send(place, att_back, stream_in[0], gain)
    grads_first = unpack_rows(grads_mine)
    rows_buf, grads_first = together((rows_buf, grads_first))
    rows_mine = over_chips(rows_buf)

    expert = at * 8 + lax.axis_index("chip")
    router = jnp.broadcast_to(lax.dynamic_slice_in_dim(router_w.T, expert, 1, 0), (8, WIDTH))
    grads_second = swap_cores(grads_first)
    t_first, t_second = grad_rows(grads_first, grads_second, down_w[0])
    rows_mine, t_first, t_second, router = together((rows_mine, t_first, t_second, router))
    weights = gate_w[0], up_w[0]
    rows_other = swap_cores(rows_mine)
    rows_first = unpack_rows(rows_mine)
    rows_other, rows_first = together((rows_other, rows_first))
    nothing = jnp.zeros((2, WIDTH), F32)
    *second, back_other, sums, rows_second = expert_rows(
        True, rows_other, t_second, *weights, router, gain, nothing
    )
    back_other = swap_cores(back_other)
    *first, back_mine, sums = expert_rows(False, rows_first, t_first, *weights, router, gain, sums)
    back = over_chips(add_back(back_mine, back_other, sums))
    gate_grad, up_grad, down_grad = weight_grads(
        (rows_first, rows_second), (grads_first, grads_second), first, second
    )
    back, gate_grad, up_grad, down_grad = together((back, gate_grad, up_grad, down_grad))

    stream_grad, grad_heads = combine(place, back, mixed, grads_local, gain)
    grad_in = over_outer(grad_heads)
    grads_buf = attention_grad(info, qkv, grad_in, att, lse)
    grads_buf, back = together((grads_buf, back))
    tail = back[:, CHUNK:].astype(F32)
    router_part = tail[:, :20].reshape(EXPERTS * 20, HD)
    gain_part = jnp.sum(tail[:, 20:], 0)
    parts = jnp.concatenate([router_part, gain_part])
    parts = parts + swap_cores(parts)
    router_grad = parts[: EXPERTS * 20].reshape(EXPERTS, WIDTH).T
    gain_grad = parts[EXPERTS * 20 :].reshape(WIDTH)
    query_grad, key_grad, value_grad = unpack_grads(over_outer(grads_buf))
    return (
        stream_grad[None],
        query_grad[None],
        key_grad[None],
        value_grad[None],
        gain_grad,
        router_grad,
        gate_grad[None],
        up_grad[None],
        down_grad[None],
    )


def solution(mesh):
    chips = Mesh(mesh.devices.reshape(8, 8, 2), ("outer", "chip", "core"))
    inner = ("chip", "core")
    every = ("outer", "chip", "core")
    frames = P(inner, "outer", None)
    pieces = P(every, None, None)
    placed = (
        frames,
        frames,
        frames,
        frames,
        P(inner, None),
        P(),
        P(),
        frames,
        pieces,
        pieces,
        pieces,
        frames,
    )
    return jax.shard_map(
        body,
        mesh=chips,
        in_specs=placed,
        out_specs=(frames, frames, frames, frames, P(), P(), pieces, pieces, pieces),
        check_vma=False,
    )
```
